32 devices in a mesh: rows: 16 (over z, y, x), heads: 2 (over core).
Axes of the slice: x: 2, y: 2, z: 4, core: 2. Of those that a mesh axis runs over, the one named last changes fastest.
Arguments:
- feats: float32 [16384, 100], P(('rows', 'heads')), as said below
- feature_mask: int32 [16, 100], P('rows'), may hold values from 0 to 1, as said below
- splits: int32 [16], P('rows'), may hold values from 640 to 896
- prompt_index: int32 [16, 128], P('rows'), may hold values from 0 to 511
- prompt_bank: bfloat16 [512, 512], replicated, may hold values from -6 to 6
- enc_weight: bfloat16 [100, 512], replicated, may hold values from -0.625 to 0.625
- enc_bias: float32 [512], replicated, may hold values from -4 to 4
- qkv_weight: bfloat16 [3, 512, 512], P(None, None, 'heads'), may hold values from -0.25 to 0.25
- out_weight: bfloat16 [512, 512], P('heads'), may hold values from -2 to 2
- out_bias: float32 [512], replicated, may hold values from -4 to 4
- attn_gain: float32 [512], replicated, may hold values from 0.25 to 1.75
- attn_shift: float32 [512], replicated, may hold values from -4 to 4
- up_weight: bfloat16 [512, 1024], P(None, 'heads'), may hold values from -0.25 to 0.25
- up_bias: float32 [1024], P('heads'), may hold values from -6 to 6
- down_weight: bfloat16 [1024, 512], P('heads'), may hold values from -0.1875 to 0.1875
- down_bias: float32 [512], replicated, may hold values from -4 to 4
- ffn_gain: float32 [512], replicated, may hold values from 0.25 to 1.75
- ffn_shift: float32 [512], replicated, may hold values from -4 to 4
- cotangent: float32 [16384, 512], P(('rows', 'heads'))
Outputs:
- output: float32 [16384, 512], P(('rows', 'heads'))
- grad_feats: float32 [16384, 100], P(('rows', 'heads'))
- grad_prompt_bank: float32 [512, 512], replicated
- grad_enc_weight: float32 [100, 512], replicated
- grad_enc_bias: float32 [512], replicated
- grad_qkv_weight: float32 [3, 512, 512], P(None, None, 'heads')
- grad_out_weight: float32 [512, 512], P('heads')
- grad_out_bias: float32 [512], replicated
- grad_attn_gain: float32 [512], replicated
- grad_attn_shift: float32 [512], replicated
- grad_up_weight: float32 [512, 1024], P(None, 'heads')
- grad_up_bias: float32 [1024], P('heads')
- grad_down_weight: float32 [1024, 512], P('heads')
- grad_down_bias: float32 [512], replicated
- grad_ffn_gain: float32 [512], replicated
- grad_ffn_shift: float32 [512], replicated
The draws below stay inside these ranges and needn't reach their ends.
Inputs may be any that keep to these rules, and one draw needn't show every extreme that they name: `feature_mask`: each row holds ones first and zeros after them, between 25 and 100 ones. `feats`: zero wherever the episode's feature_mask is zero.
All inputs are finite; a program needn't handle non-finite values.
Results may differ from the reference program's by a relative error of at most 0.015.
Values may be sent and summed in bfloat16 or wider, within the bound.
A program may use at most 64 MiB of HBM per device.

```python
import math
import jax
import jax.numpy as jnp
from jax import lax

D = 512
H = 4
DH = 128
FF = 1024
F = 100
BANK = 512
P_SIZE = 128
DATA = 1024
EPIS = 16


def used_counts(key):
    return jax.random.randint(jax.random.fold_in(key, 101), (EPIS,), F // 4, F + 1)


def draw_feature_mask(key, part):
    used = used_counts(key)
    columns = jnp.arange(F)
    return (columns[None, :] < used[:, None]).astype(jnp.int32)


def draw_feats(key, part):
    used = used_counts(key)
    key = jax.random.fold_in(key, 2)
    parts_keys = jax.random.split(key, 4)
    column_scale = jnp.exp(jax.random.uniform(parts_keys[0], (F,), minval=0.0, maxval=math.log(10.0)))
    offset = jax.random.normal(parts_keys[1], (F,)) * column_scale * 0.8
    row_scale = jnp.exp(jax.random.uniform(parts_keys[2], (EPIS * DATA, 1), minval=0.0, maxval=math.log(2.0)))
    episode = jnp.arange(EPIS * DATA) // DATA
    position = episode.astype(jnp.float32) / max(EPIS - 1, 1)
    noise = jax.random.normal(parts_keys[3], (EPIS * DATA, F))
    rising = 3.0 ** position
    live = jnp.arange(F)[None, :] < used[episode][:, None]
    values = (offset + column_scale * noise) * row_scale * rising[:, None]
    return jnp.where(live, values, 0.0).astype(jnp.float32)


def draw_cotangent(key, part):
    key = jax.random.fold_in(key, 3)
    first_key, second_key = jax.random.split(key, 2)
    common = jax.random.normal(first_key, (1, D))
    noise = jax.random.normal(second_key, (EPIS * DATA, D))
    values = noise + 0.5 * common
    return values.astype(jnp.float32)


def place_ends(drawn, key, smallest, largest):
    longest = drawn.shape.index(max(drawn.shape))
    spots = []
    for shift in (0, 1):
        where = [jax.random.randint(jax.random.fold_in(key, axis), (), 0, length) for axis, length in enumerate(drawn.shape)]
        where[longest] = (where[longest] + shift) % drawn.shape[longest]
        spots.append(tuple(where))
    return drawn.at[spots[0]].set(smallest).at[spots[1]].set(largest)


def steps_of(key, dims, cuts, smallest, high):
    def one(dim, parts):
        draws = jax.random.uniform(jax.random.fold_in(jax.random.fold_in(key, 6), dim), (parts,), jnp.float32, smallest / len(cuts), high / len(cuts))
        return jnp.repeat(jnp.exp(draws), dims[dim] // parts).reshape((-1,) + (1,) * (len(dims) - dim - 1))

    factor_of = one(*cuts[0])
    for cut in cuts[1:]:
        factor_of = factor_of * one(*cut)
    return factor_of


def normal_values(own_key, dims, width, reach, cuts=(), dtype=jnp.bfloat16):
    values = width * jax.random.normal(own_key, dims, jnp.float32)
    if cuts:
        values = values * steps_of(own_key, dims, cuts, -0.22, 0.18)
    return jnp.clip(values, -reach, reach).astype(dtype)


def setup_inputs(seed: int = 0) -> dict:
    key_of = jax.random.split(jax.random.key(seed), 20)
    feats = draw_feats(jax.random.fold_in(key_of[19], 71), 0)
    feature_mask = draw_feature_mask(jax.random.fold_in(key_of[19], 71), 0)
    splits = place_ends(jax.random.randint(key_of[2], (EPIS,), 5 * DATA // 8, 7 * DATA // 8 + 1), jax.random.fold_in(key_of[2], 1), 5 * DATA // 8, (7 * DATA // 8 + 1) - 1).astype(jnp.int32)
    prompt_index = place_ends(jax.random.randint(key_of[3], (EPIS, P_SIZE), 0, BANK), jax.random.fold_in(key_of[3], 1), 0, BANK - 1).astype(jnp.int32)
    prompt_bank = normal_values(key_of[4], (BANK, D), 1.0, 6.0)
    enc_weight = normal_values(key_of[5], (F, D), F ** -0.5, 0.625)
    enc_bias = normal_values(key_of[6], (D,), 0.3, 4.0, (), jnp.float32)
    qkv_weight = normal_values(key_of[7], (3, D, H * DH), D ** -0.5, 0.25, ((2, 2),))
    out_weight = normal_values(key_of[8], (H * DH, D), (H * DH // 64) ** -0.5, 2.0, ((0, 2),))
    out_bias = normal_values(key_of[9], (D,), 0.3, 4.0, (), jnp.float32)
    attn_gain = jnp.clip(1.0 + 0.15 * jax.random.normal(key_of[10], (D,), jnp.float32), 0.25, 1.75)
    attn_shift = normal_values(key_of[11], (D,), 0.3, 4.0, (), jnp.float32)
    up_weight = normal_values(key_of[12], (D, FF), D ** -0.5, 0.25, ((1, 2),))
    up_bias = normal_values(key_of[13], (FF,), 0.5, 6.0, ((0, 2),), jnp.float32)
    down_weight = normal_values(key_of[14], (FF, D), FF ** -0.5, 0.1875, ((0, 2),))
    down_bias = normal_values(key_of[15], (D,), 0.3, 4.0, (), jnp.float32)
    ffn_gain = jnp.clip(1.0 + 0.15 * jax.random.normal(key_of[16], (D,), jnp.float32), 0.25, 1.75)
    ffn_shift = normal_values(key_of[17], (D,), 0.3, 4.0, (), jnp.float32)
    cotangent = draw_cotangent(jax.random.fold_in(key_of[19], 71), 0)
    return {"feats": feats, "feature_mask": feature_mask, "splits": splits, "prompt_index": prompt_index, "prompt_bank": prompt_bank, "enc_weight": enc_weight, "enc_bias": enc_bias, "qkv_weight": qkv_weight, "out_weight": out_weight, "out_bias": out_bias, "attn_gain": attn_gain, "attn_shift": attn_shift, "up_weight": up_weight, "up_bias": up_bias, "down_weight": down_weight, "down_bias": down_bias, "ffn_gain": ffn_gain, "ffn_shift": ffn_shift, "cotangent": cotangent}


@jax.custom_vjp
def low(v):
    return lax.optimization_barrier(v.astype(jnp.bfloat16)).astype(jnp.float32)

@jax.custom_vjp
def low_back(v):
    return v

def low_keep(v):
    return (low(v), None)

def low_pass(kept, grad):
    return (grad,)

def back_keep(v):
    return (v, None)

def back_low(kept, grad):
    return (low(grad),)
low.defvjp(low_keep, low_pass)
low_back.defvjp(back_keep, back_low)
highest = lax.Precision.HIGHEST
epsilon = 1e-05

def product(left, right):
    return jnp.dot(left, right, precision=highest, preferred_element_type=jnp.float32)

def normalize(values, gain, shift):
    center = values - lax.optimization_barrier(jnp.mean(values, axis=-1, keepdims=True))
    spread = lax.optimization_barrier(jnp.mean(center * center, axis=-1, keepdims=True))
    return center * lax.rsqrt(spread + epsilon) * gain + shift

def episode_layer(weights, inputs):
    enc_weight, enc_bias, qkv_weight, out_weight, out_bias, attn_gain, attn_shift, up_weight, up_bias, down_weight, down_bias, ffn_gain, ffn_shift = weights
    normed, prompt_rows, split = inputs
    hidden_in = low_back(product(low(normed), enc_weight) + enc_bias)
    hidden_low = low(hidden_in)
    prompt_low = low(prompt_rows)
    queries = low(low_back(product(hidden_low, qkv_weight[0])))
    key_rows = low(low_back(jnp.concatenate([product(prompt_low, qkv_weight[1]), product(hidden_low, qkv_weight[1])], axis=0)))
    value_rows = low(low_back(jnp.concatenate([product(prompt_low, qkv_weight[2]), product(hidden_low, qkv_weight[2])], axis=0)))
    heads_q = queries.reshape(DATA, H, DH)
    heads_k = key_rows.reshape(P_SIZE + DATA, H, DH)
    heads_v = value_rows.reshape(P_SIZE + DATA, H, DH)
    scores = low_back(jnp.einsum('qhd,khd->hqk', heads_q, heads_k, precision=highest))
    visible = jnp.arange(P_SIZE + DATA) < P_SIZE + split
    scaled = jnp.where(visible[None, None, :], scores * DH ** (-0.5), -1e+30)
    shares = jax.nn.softmax(scaled, axis=-1)
    attended = jnp.einsum('hqk,khd->qhd', low(shares), heads_v, precision=highest)
    attended = low(low_back(attended.reshape(DATA, H * DH)))
    branch = low_back(product(attended, out_weight) + out_bias)
    after_attn = normalize(hidden_in + branch, attn_gain, attn_shift)
    upper = low_back(product(low(after_attn), up_weight) + up_bias)
    mixed = low_back(product(low(jax.nn.gelu(upper, approximate=False)), down_weight) + down_bias)
    return normalize(after_attn + mixed, ffn_gain, ffn_shift)

def reference(feats, feature_mask, splits, prompt_index, prompt_bank, enc_weight, enc_bias, qkv_weight, out_weight, out_bias, attn_gain, attn_shift, up_weight, up_bias, down_weight, down_bias, ffn_gain, ffn_shift, cotangent):
    weights = (enc_weight.astype(jnp.float32), enc_bias, qkv_weight.astype(jnp.float32), out_weight.astype(jnp.float32), out_bias, attn_gain, attn_shift, up_weight.astype(jnp.float32), up_bias, down_weight.astype(jnp.float32), down_bias, ffn_gain, ffn_shift)
    bank = prompt_bank.astype(jnp.float32)
    live = feature_mask.astype(jnp.float32)
    boost = jnp.sqrt(F / lax.optimization_barrier(jnp.sum(live, axis=1)))

    def forward(table, bank_rows, layer_weights):
        row_total = EPIS * DATA
        feat_mean = lax.optimization_barrier(jnp.sum(table, axis=0)) / row_total
        feat_var = lax.optimization_barrier(jnp.sum(table * table, axis=0)) / row_total - feat_mean * feat_mean
        inverse = lax.rsqrt(feat_var + epsilon)
        normed = ((table - feat_mean) * inverse).reshape(EPIS, DATA, F) * (live * boost[:, None])[:, None, :]
        prompt_rows = bank_rows[prompt_index]

        def step(carry, inputs):
            return (carry, episode_layer(layer_weights, inputs))
        _, outputs = lax.scan(jax.checkpoint(step), jnp.zeros((), jnp.float32), (normed, prompt_rows, splits))
        return outputs.reshape(EPIS * DATA, D)
    output, pull = jax.vjp(forward, feats, bank, weights)
    grad_feats, grad_bank, grads = pull(cotangent)
    return (output, grad_feats, grad_bank, grads[0], grads[1], grads[2], grads[3], grads[4], grads[5], grads[6], grads[7], grads[8], grads[9], grads[10], grads[11], grads[12])
```

```python
import functools
import math

import jax
import jax.numpy as jnp
from jax import lax
from jax.experimental import pallas as pl
from jax.experimental.pallas import tpu as pltpu
from jax.sharding import PartitionSpec as P

BF = jnp.bfloat16
F32 = jnp.float32
MESH = pl.DeviceIdType.MESH
DH = 128
P_SIZE = 128
CONTEXT_MAX = 896
KEYS = CONTEXT_MAX + P_SIZE
EPS = 1e-05
HALF_ROOT = math.sqrt(0.5)
PDF_SCALE = 1.0 / math.sqrt(2.0 * math.pi)
LOG2E = math.log2(math.e)
SEMS = 400
VMEM_LIMIT = 60 * 2**20


def _dot(a, b, ca, cb):
    return lax.dot_general(a, b, (((ca,), (cb,)), ((), ())), preferred_element_type=F32)


def nn(a, b):
    return _dot(a, b, 1, 0)


def nt(a, b):
    return _dot(a, b, 1, 1)


def tn(a, b):
    return _dot(a, b, 0, 0)


def row_sum(v):
    return jnp.sum(v, axis=0, keepdims=True)


def lane_mean(v):
    return jnp.mean(v, axis=-1, keepdims=True)


class Links:
    def __init__(self, send, recv):
        self.send, self.recv, self.used, self.open = send, recv, 0, []

    def copy(self, src, dst, device):
        i = self.used
        self.used += 1
        assert i < SEMS
        c = pltpu.make_async_remote_copy(
            src_ref=src,
            dst_ref=dst,
            send_sem=self.send.at[i],
            recv_sem=self.recv.at[i],
            device_id=device,
            device_id_type=MESH,
        )
        c.start()
        self.open.append(c)
        return c

    def drain(self):
        for c in self.open:
            c.wait_send()
        self.open = []


class Loads:
    def __init__(self, sems):
        self.sems, self.used = sems, 0

    def copy(self, src, dst):
        c = pltpu.make_async_copy(src, dst, self.sems.at[self.used])
        self.used += 1
        c.start()
        return c


class Chunk:
    def __init__(self, ctx, refs, stages):
        self.ctx = ctx
        self.give, self.got, self.acc, self.recv, self.full = refs
        self.stages = stages
        self.n = self.acc.shape[0]
        self.at = 0
        self.core_copy = None

    def send_core(self):
        self.core_copy = self.ctx.links.copy(self.give, self.got, self.ctx.twin)

    def merge_core(self):
        self.core_copy.wait_recv()
        self.acc[...] = (self.acc[...].astype(F32) + self.got[...].astype(F32)).astype(BF)
        self.begin()

    def begin(self):
        self.base, self.len, self.off, self.k = 0, self.n, 0, 0
        self._start_scatter()

    def _digits(self, bits, mask):
        digit, row = 0, self.ctx.row
        for i, b in enumerate(bits):
            bit = (self.ctx.row // b) % 2
            if mask >> i & 1:
                row = row + b * (1 - 2 * bit)
                bit = 1 - bit
            digit = digit * 2 + bit
        return digit, row

    def _start_scatter(self):
        bits = self.stages[self.k]
        ways = 2 ** len(bits)
        q = self.len // ways
        self.copies = []
        for mask in range(1, ways):
            digit, row = self._digits(bits, mask)
            src = self.acc.at[pl.ds(pl.multiple_of(self.base + digit * q, 16), q)]
            dst = self.recv.at[pl.ds(self.off + (mask - 1) * q, q)]
            self.copies.append(self.ctx.links.copy(src, dst, (row, self.ctx.head)))

    def _end_scatter(self):
        bits = self.stages[self.k]
        ways = 2 ** len(bits)
        q = self.len // ways
        digit, _ = self._digits(bits, 0)
        self.base = self.base + digit * q
        mine = pl.ds(pl.multiple_of(self.base, 16), q)
        total = self.acc[mine, :].astype(F32)
        for i, c in enumerate(self.copies):
            c.wait_recv()
            total = total + self.recv[pl.ds(self.off + i * q, q), :].astype(F32)
        self.off += (ways - 1) * q
        self.len = q
        self.k += 1
        if self.k < len(self.stages):
            self.acc[mine, :] = total.astype(BF)
            self._start_scatter()
        else:
            self.full[mine, :] = total.astype(BF)
            self._start_gather()

    def _start_gather(self):
        bits = self.stages[self.k - 1]
        mine = pl.ds(pl.multiple_of(self.base, 16), self.len)
        self.copies = []
        for mask in range(1, 2 ** len(bits)):
            _, row = self._digits(bits, mask)
            self.copies.append(
                self.ctx.links.copy(self.full.at[mine], self.full.at[mine], (row, self.ctx.head))
            )

    def _end_gather(self):
        bits = self.stages[self.k - 1]
        for c in self.copies:
            c.wait_recv()
        digit, _ = self._digits(bits, 0)
        self.base = self.base - digit * self.len
        self.len = self.len * 2 ** len(bits)
        self.k -= 1
        if self.k > 0:
            self._start_gather()

    def steps(self):
        return 2 * len(self.stages)

    def advance(self):
        if self.at < len(self.stages):
            self._end_scatter()
        elif self.at < self.steps():
            self._end_gather()
        self.at += 1

    def finish(self):
        while self.at < self.steps():
            self.advance()


class Ctx:
    pass


def share_rows(ctx, slots, count):
    mine = slots.at[ctx.row]
    return [
        ctx.links.copy(mine, mine, (lax.rem(ctx.row + k, count), ctx.head)) for k in range(1, count)
    ]


IN_NAMES = [
    "feats", "mask", "splits", "pidx", "bank", "encw", "encb", "qkvw", "outw", "outb", "ag", "ash", "upw",
    "upb", "downw", "downb", "fg", "fsh", "cot",
]
OUT_NAMES = [
    "output", "uf", "rffn", "rqkv", "rbank", "vec", "late", "stat",
]


def layer_kernel(count, total_rows, stages, chunk_rows, names, *refs):
    g = Ctx()
    for name, ref in zip(names, refs, strict=True):
        setattr(g, name, ref)
    n, features = g.feats.shape
    ctx = Ctx()
    ctx.row, ctx.head = lax.axis_index("rows"), lax.axis_index("heads")
    h = ctx.head
    o = 1 - h
    ctx.twin = (ctx.row, o)
    ctx.links = links = Links(g.ssem, g.rsem)
    loads = Loads(g.lsem)

    l_feats = loads.copy(g.feats, g.F.at[h])
    own = {
        "qkv": (g.qkvw, g.WQKV.at[h]),
        "out": (g.outw, g.WO.at[h]),
        "upb": (g.upb, g.UB.at[h]),
        "up": (g.upw, g.WU.at[h]),
        "down": (g.downw, g.WD.at[h]),
    }
    barrier = pltpu.get_barrier_semaphore()
    pl.semaphore_signal(barrier, inc=1, device_id=ctx.twin, device_id_type=MESH)
    for k in range(1, count):
        pl.semaphore_signal(
            barrier, inc=1, device_id=(lax.rem(ctx.row + k, count), h), device_id_type=MESH
        )
    l_bank = loads.copy(g.bank, g.BANKV)
    l_own = {k: loads.copy(*v) for k, v in own.items()}
    l_cot = loads.copy(g.cot, g.COT)

    g.TILE[0] = jnp.zeros_like(g.TILE[0])
    g.LATE[0] = jnp.zeros_like(g.LATE[0])
    g.VEC[...] = jnp.zeros_like(g.VEC)
    l_feats.wait()
    f = g.F[h]
    g.TILE[0, 0:1, :features] = row_sum(f)
    g.TILE[0, 1:2, :features] = row_sum(f * f)
    pl.semaphore_wait(barrier, count)
    c_tile = links.copy(g.TILE.at[0], g.TILE.at[1], ctx.twin)
    c_feats = links.copy(g.feats, g.F.at[h], ctx.twin)
    c_tile.wait_recv()
    g.MOM[ctx.row] = g.TILE[0] + g.TILE[1]
    c_mom = share_rows(ctx, g.MOM, count)
    c_own = {k: links.copy(*v, ctx.twin) for k, v in own.items()}

    selector = lax.broadcasted_iota(jnp.int32, (g.bank.shape[0], P_SIZE), 0) == g.pidx[...]
    g.SEL[...] = jnp.where(selector, 1.0, 0.0).astype(BF)
    l_bank.wait()
    g.SRC[CONTEXT_MAX:KEYS, :] = tn(g.SEL[...], g.BANKV[...]).astype(BF)
    visible = lax.broadcasted_iota(jnp.int32, (KEYS, 1), 0)
    visible = (visible < g.splits[0]) | (visible >= CONTEXT_MAX)
    g.BIAS[...] = jnp.where(visible, 0.0, -1e30)
    for c in l_own.values():
        c.wait()
    c_own["qkv"].wait_recv()
    for j in range(4):
        s, w = j // 2, pl.ds(128 * (j % 2), 128)
        g.WKV[j, :, 0:128] = g.WQKV[s, 1, :, w]
        g.WKV[j, :, 128:256] = g.WQKV[s, 2, :, w]

    c_feats.wait_recv()
    for c in c_mom:
        c.wait_recv()
    moments = g.MOM[0]
    for k in range(1, count):
        moments = moments + g.MOM[k]
    mean = moments[0:1, :features] / total_rows
    var = moments[1:2, :features] / total_rows - mean * mean
    inverse = lax.rsqrt(var + EPS)
    live = g.mask[...].astype(F32)
    scale = live * jnp.sqrt(features / jnp.sum(live, axis=-1, keepdims=True))
    g.STAT[0:1, :features] = mean
    g.STAT[1:2, :features] = inverse
    g.STAT[2:3, :features] = scale

    for s in range(2):
        g.NL[s] = (((g.F[s] - mean) * inverse) * scale).astype(BF)
        hidden = nn(g.NL[s], g.encw[...]) + g.encb[...]
        g.HA[s] = hidden
        g.HB[s] = hidden.astype(BF)
    g.SRC[0:n, :] = g.HB[0]
    g.SRC[n:CONTEXT_MAX, :] = g.HB[1, 0 : CONTEXT_MAX - n, :]

    for s in range(2):
        q = nn(g.HB[h], g.WQKV[s, 0]).astype(BF)
        for j in range(2):
            g.Q[2 * s + j] = q[:, 128 * j : 128 * j + 128]

    def project(j, _):
        kv = nn(g.SRC[...], g.WKV[j]).astype(BF)
        g.K[j] = kv[:, 0:128]
        g.V[j] = kv[:, 128:256]
        return 0

    lax.fori_loop(0, 4, project, 0)

    def attend(j, _):
        for t in range(n // 256):
            cols = slice(256 * t, 256 * t + 256)
            scores = nt(g.K[j], g.Q[j, cols, :]) * (DH**-0.5 * LOG2E) + g.BIAS[...]
            e = jnp.exp2(scores - jnp.max(scores, axis=0, keepdims=True))
            inv = 1.0 / row_sum(e)
            g.INV[j, 0:1, cols] = inv
            e = e.astype(BF)
            g.E[j, :, cols] = e
            g.AT[j, :, cols] = (tn(g.V[j], e) * inv).astype(BF)
        return 0

    lax.fori_loop(0, 4, attend, 0)

    c_own["out"].wait_recv()
    c_own["up"].wait_recv()
    c_own["upb"].wait_recv()
    c_own["down"].wait_recv()
    for j in range(4):
        g.A[:, 128 * j : 128 * j + 128] = g.AT[j].T
    l_cot.wait()

    tile = 256

    def forward(t, _):
        rows = pl.ds(pl.multiple_of(t * tile, tile), tile)
        branch = nn(g.A[rows, 0:256], g.WO[0]) + nn(g.A[rows, 256:512], g.WO[1]) + g.outb[...]
        joined = g.HA[h, rows, :] + branch
        center = joined - lane_mean(joined)
        rstd = lax.rsqrt(lane_mean(center * center) + EPS)
        xhat = center * rstd
        after = xhat * g.ag[...] + g.ash[...]
        g.XH[rows, :] = xhat
        g.RS[rows, :] = rstd
        low = after.astype(BF)
        g.AB[rows, :] = low
        mixed = g.downb[...]
        for s in range(2):
            u = nn(low, g.WU[s]) + g.UB[s]
            phi = 0.5 * (1.0 + lax.erf(u * HALF_ROOT))
            g.DG[s, rows, :] = phi + u * (jnp.exp2(u * u * (-0.5 * LOG2E)) * PDF_SCALE)
            act = (u * phi).astype(BF)
            g.ACT[s, rows, :] = act
            mixed = mixed + nn(act, g.WD[s])
        joined = after + mixed
        center = joined - lane_mean(joined)
        rstd = lax.rsqrt(lane_mean(center * center) + EPS)
        xhat = center * rstd
        g.OUTB[rows, :] = xhat * g.fg[...] + g.fsh[...]
        ct = g.COT[rows, :]
        d = ct * g.fg[...]
        d = rstd * (d - lane_mean(d) - xhat * lane_mean(d * xhat))
        g.DJ[rows, :] = d
        gm = d.astype(BF)
        g.GM[rows, :] = gm
        g.VEC[4:5, :] += row_sum(gm.astype(F32))
        g.VEC[5:6, :] += row_sum(ct * xhat)
        g.VEC[6:7, :] += row_sum(ct)
        return 0

    lax.fori_loop(0, n // tile, forward, 0)
    l_output = loads.copy(g.OUTB, g.output)

    def put(ref, first, value):
        r = value.shape[0]
        for b in range(value.shape[1] // 128):
            ref[first + r * b : first + r * b + r, :] = value[:, 128 * b : 128 * b + 128]

    chunks = [
        Chunk(ctx, [getattr(g, f"{p}{i}") for p in ("CG", "CR", "CA", "CV", "CF")], stages[i])
        for i in range(len(chunk_rows))
    ]
    down, up, out, qkv0, qkv1, last = chunks

    put(down.give, 0, tn(g.ACT[o], g.GM[...]).astype(BF))
    down.send_core()
    put(down.acc, 0, tn(g.ACT[h], g.GM[...]).astype(BF))

    def backward(t, _):
        rows = pl.ds(pl.multiple_of(t * tile, tile), tile)
        gm = g.GM[rows, :]
        d = g.DJ[rows, :]
        for s in range(2):
            du = (g.DG[s, rows, :] * nt(gm, g.WD[s])).astype(BF)
            g.DU[s, rows, :] = du
            g.VEC[7 + s : 8 + s, :] += row_sum(du.astype(F32))
            d = d + nt(du, g.WU[s])
        xhat = g.XH[rows, :]
        g.VEC[2:3, :] += row_sum(d * xhat)
        g.VEC[3:4, :] += row_sum(d)
        d = d * g.ag[...]
        d = g.RS[rows, :] * (d - lane_mean(d) - xhat * lane_mean(d * xhat))
        g.DJ[rows, :] = d
        gb = d.astype(BF)
        g.GB[rows, :] = gb
        g.VEC[1:2, :] += row_sum(gb.astype(F32))
        return 0

    down.merge_core()
    lax.fori_loop(0, n // tile, backward, 0)
    put(up.give, 0, tn(g.AB[...], g.DU[o]).astype(BF))
    up.send_core()
    for j in range(2):
        put(out.give, 128 * j * 4, nn(g.AT[2 * o + j], g.GB[...]).astype(BF))
    out.send_core()
    c_vec = links.copy(g.VEC, g.VECR, ctx.twin)
    put(up.acc, 0, tn(g.AB[...], g.DU[h]).astype(BF))
    for j in range(2):
        put(out.acc, 128 * j * 4, nn(g.AT[2 * h + j], g.GB[...]).astype(BF))
    up.merge_core()
    out.merge_core()
    down.advance()

    for j in range(4):
        d = nt(g.WO[j // 2, 128 * (j % 2) : 128 * (j % 2) + 128, :], g.GB[...]).astype(BF)
        g.DOT[j] = d
        df = d.astype(F32)
        g.INNER[j, 0:1, :] = row_sum(df * g.AT[j].astype(F32))
        g.DOT2[j] = (df * g.INV[j, 0:1, :]).astype(BF)
        g.INV[j, 1:2, :] = g.INV[j, 0:1, :] * (DH**-0.5)

    c_vec.wait_recv()
    vec_sum = Ctx()
    vec_sum.k = 0

    def vec_start(value):
        bits = vec_stages[vec_sum.k]
        digit, _ = digits_of(bits, 0)
        slots = g.VECS.at[vec_sum.k]
        slots[digit] = value
        vec_sum.copies = []
        for mask in range(1, 2 ** len(bits)):
            _, row = digits_of(bits, mask)
            vec_sum.copies.append(links.copy(slots.at[digit], slots.at[digit], (row, h)))

    def vec_end():
        bits = vec_stages[vec_sum.k]
        for c in vec_sum.copies:
            c.wait_recv()
        value = g.VECS[vec_sum.k, 0]
        for i in range(1, 2 ** len(bits)):
            value = value + g.VECS[vec_sum.k, i]
        vec_sum.k += 1
        if vec_sum.k < len(vec_stages):
            vec_start(value)
        else:
            g.vec[...] = value

    digits_of = down._digits
    vec_stages = vec_groups(count)
    vec_start(g.VEC[...] + g.VECR[...])

    kv_copies = {}

    def attend_back(j):
        q, dot, dot2 = g.Q[j], g.DOT[j], g.DOT2[j]
        inner, factor = g.INNER[j, 0:1, :], g.INV[j, 1:2, :]

        def block(t, dq):
            rows = pl.ds(pl.multiple_of(t * 256, 256), 256)
            e = g.E[j, rows, :]
            upstream = nn(g.V[j, rows, :], dot)
            ds = (e.astype(F32) * ((upstream - inner) * factor)).astype(BF)
            g.DKV[j, rows, 0:128] = nn(ds, q).astype(BF)
            g.DKV[j, rows, 128:256] = nt(e, dot2).astype(BF)
            return dq + tn(g.K[j, rows, :], ds)

        dq = lax.fori_loop(0, KEYS // 256, block, jnp.zeros((128, n), F32))
        g.DQT[j] = dq.astype(BF)
        other = pl.ds(pl.multiple_of(o * n, n), n)
        kv_copies[j] = links.copy(g.DKV.at[j, other], g.DKVR.at[j], ctx.twin)

    def head_grads(j, chunk, ref):
        put(ref, 0, nt(g.HQT[...], g.DQT[j]).astype(BF))
        put(ref, n, nn(g.SRCT[...], g.DKVO[j]).astype(BF))

    def merge_kv(j):
        kv_copies[j].wait_recv()
        mine = pl.ds(pl.multiple_of(h * n, n), n)
        g.DKVO[j] = (g.DKV[j, mine, :].astype(F32) + g.DKVR[j].astype(F32)).astype(BF)

    g.HQT[...] = g.HB[h].T
    g.SRCT[...] = g.SRC[pl.ds(pl.multiple_of(h * n, n), n), :].T

    attend_back(0)
    down.advance()
    attend_back(2)
    up.advance()
    out.advance()
    merge_kv(0)
    merge_kv(2)

    def pair_grads(p, chunk):
        head_grads(2 * o + p, chunk, chunk.give)
        chunk.send_core()
        head_grads(2 * h + p, chunk, chunk.acc)

    pair_grads(0, qkv0)
    down.advance()
    up.advance()
    attend_back(1)
    qkv0.merge_core()
    out.advance()
    down.advance()
    up.advance()
    vec_end()
    attend_back(3)
    out.advance()
    down.advance()
    qkv0.advance()
    merge_kv(1)
    merge_kv(3)
    pair_grads(1, qkv1)

    kvh = nt(g.DKVO[0], g.WKV[0])
    for j in range(1, 4):
        kvh = kvh + nt(g.DKVO[j], g.WKV[j])
    edge = CONTEXT_MAX - n
    g.DP[0] = kvh[edge:n, :].astype(BF)
    c_prompt = links.copy(g.DP.at[0], g.DP.at[1], ctx.twin)
    for j in range(4):
        g.DQ[:, 128 * j : 128 * j + 128] = g.DQT[j].T
    dh = g.DJ[...]
    for j in range(4):
        w = g.WQKV[j // 2, 0, :, 128 * (j % 2) : 128 * (j % 2) + 128]
        dh = dh + nt(g.DQ[:, 128 * j : 128 * j + 128], w)
    gh = dh[0:edge] + kvh[0:edge]
    g.GH[0:edge, :] = gh.astype(BF)
    first = jnp.where(h == 0, 1.0, 0.0)
    g.GH[edge:n, :] = (dh[edge:n] + kvh[edge:n] * first).astype(BF)
    gh = g.GH[...]
    qkv1.merge_core()

    uf = nt(gh, g.encw[...]) * scale
    g.UF[...] = uf
    g.LATE[0, 0:1, :features] = row_sum(uf)
    g.LATE[0, 1:2, :features] = row_sum(uf * (g.F[h] - mean))
    eb = row_sum(gh.astype(F32))
    for b in range(4):
        g.LATE[0, 2 + b : 3 + b, :] = eb[:, 128 * b : 128 * b + 128]
    c_late = links.copy(g.LATE.at[0], g.LATE.at[1], ctx.twin)
    l_uf = loads.copy(g.UF, g.uf)
    c_late.wait_recv()
    g.LSUM[ctx.row] = g.LATE[0] + g.LATE[1]
    c_late_rows = share_rows(ctx, g.LSUM, count)

    enc = tn(g.NL[h], gh)
    g.ENC[0:features, :] = enc
    g.ENC[features:, :] = jnp.zeros_like(g.ENC[features:, :])
    bank_rows = g.bank.shape[0] // 2
    enc_at = bank_rows * 4
    for b in range(4):
        cols = slice(128 * b, 128 * b + 128)
        last.give[64 * b : 64 * b + 64, :] = g.ENC[pl.ds(pl.multiple_of(o * 64, 64), 64), cols].astype(BF)
        last.acc[enc_at + 64 * b : enc_at + 64 * b + 64, :] = g.ENC[
            pl.ds(pl.multiple_of(h * 64, 64), 64), cols
        ].astype(BF)
    last.send_core()
    c_prompt.wait_recv()
    put(
        last.acc,
        0,
        nn(g.SEL[pl.ds(pl.multiple_of(h * bank_rows, bank_rows), bank_rows), :], g.DP[o]).astype(BF),
    )
    last.core_copy.wait_recv()
    rows = slice(enc_at, enc_at + 256)
    last.acc[rows, :] = (last.acc[rows, :].astype(F32) + last.got[...].astype(F32)).astype(BF)
    if last.n > enc_at + 256:
        last.acc[enc_at + 256 :, :] = jnp.zeros_like(last.acc[enc_at + 256 :, :])
    last.begin()
    up.advance()
    out.advance()

    rest = [down, up, out, qkv0, qkv1, last]
    while any(c.at < c.steps() for c in rest):
        for c in rest:
            c.advance()
    if vec_sum.k < len(vec_stages):
        vec_end()
    c_last = links.copy(last.full, g.TWIN, ctx.twin)
    stores = [l_output, l_uf]
    at = 0
    for c in (down, up, out):
        stores.append(loads.copy(c.full, g.rffn.at[pl.ds(at, c.n)]))
        at += c.n
    at = 0
    for c in (qkv0, qkv1):
        stores.append(loads.copy(c.full.at[0:1536], g.rqkv.at[pl.ds(at, 1536)]))
        at += 1536
    for c in c_late_rows:
        c.wait_recv()
    late = g.LSUM[0]
    for k in range(1, count):
        late = late + g.LSUM[k]
    g.late[...] = late
    g.stat[...] = g.STAT[...]
    stores.append(loads.copy(last.full.at[0 : enc_at + 256], g.rbank.at[h]))
    c_last.wait_recv()
    stores.append(loads.copy(g.TWIN.at[0 : enc_at + 256], g.rbank.at[o]))
    for c in stores:
        c.wait()
    links.drain()


def vec_groups(count):
    bits = [2**i for i in range(count.bit_length() - 1)]
    return [tuple(bits[i : i + 2]) for i in range(0, len(bits), 2)]


def finish_kernel(total_rows, names, *refs):
    g = Ctx()
    for name, ref in zip(names, refs, strict=True):
        setattr(g, name, ref)
    h = lax.axis_index("heads")
    features = g.feats.shape[1]

    def block(ref, first, rows):
        return ref[first : first + rows, :].astype(F32)

    for b in range(4):
        cols = slice(128 * b, 128 * b + 128)
        g.o_down[:, cols] = block(g.rffn, 512 * b, 512)
        g.o_up[:, cols] = block(g.rffn, 2048 + 512 * b, 512)
        for j in range(2):
            g.o_out[128 * j : 128 * j + 128, cols] = block(g.rffn, 4096 + 512 * j + 128 * b, 128)
        for s in range(2):
            g.o_bank[256 * s : 256 * s + 256, cols] = g.rbank[s, 256 * b : 256 * b + 256, :].astype(F32)
        g.o_encw[0:64, cols] = g.rbank[0, 1024 + 64 * b : 1024 + 64 * b + 64, :].astype(F32)
        g.o_encw[64:features, cols] = g.rbank[1, 1024 + 64 * b : 1024 + 64 * b + features - 64, :].astype(F32)
        g.o_encb[:, cols] = g.late[2 + b : 3 + b, :]
    for c in range(3):
        for p in range(2):
            g.o_qkv[c, :, 128 * p : 128 * p + 128] = block(g.rqkv, 1536 * p + 512 * c, 512)
    g.o_outb[...] = g.vec[1:2, :]
    g.o_ag[...] = g.vec[2:3, :]
    g.o_ash[...] = g.vec[3:4, :]
    g.o_downb[...] = g.vec[4:5, :]
    g.o_fg[...] = g.vec[5:6, :]
    g.o_fsh[...] = g.vec[6:7, :]
    g.o_upb[...] = g.vec[pl.ds(7 + h, 1), :]
    mean, inverse = g.stat[0:1, :features], g.stat[1:2, :features]
    b1, b2 = g.late[0:1, :features], g.late[1:2, :features]
    var_grad = -0.5 * inverse * inverse * inverse * b2
    first = (-inverse * b1 - 2.0 * mean * var_grad) / total_rows
    g.o_feats[...] = g.uf[...] * inverse + first + g.feats[...] * (2.0 * var_grad / total_rows)
    g.o_output[...] = g.output[...]


def per_device(
    feats,
    feature_mask,
    splits,
    prompt_index,
    prompt_bank,
    enc_weight,
    enc_bias,
    qkv_weight,
    out_weight,
    out_bias,
    attn_gain,
    attn_shift,
    up_weight,
    up_bias,
    down_weight,
    down_bias,
    ffn_gain,
    ffn_shift,
    cotangent,
):
    n, features = feats.shape
    count = lax.axis_size("rows")
    total_rows = n * count * lax.axis_size("heads")
    d = prompt_bank.shape[1]
    args = [
        feats, feature_mask, splits, prompt_index, prompt_bank, enc_weight, enc_bias[None], qkv_weight, out_weight,
        out_bias[None], attn_gain[None], attn_shift[None], up_weight, up_bias[None], down_weight, down_bias[None],
        ffn_gain[None], ffn_shift[None], cotangent,
    ]
    vmem = pl.BlockSpec(memory_space=pltpu.VMEM)
    hbm = pl.BlockSpec(memory_space=pl.ANY)
    large = {"feats", "bank", "qkvw", "outw", "upw", "upb", "downw", "cot"}
    in_specs = [
        hbm if k in large else pl.BlockSpec(memory_space=pltpu.SMEM) if k == "splits" else vmem for k in IN_NAMES
    ]
    bits = [2**i for i in range(count.bit_length() - 1)]
    grain = 16 * count
    chunk_rows = [-(-r // grain) * grain for r in (2048, 2048, 1024, 1536, 1536, 1280)]
    if count == 16:
        x, y, z, w = bits
        stages = [
            [(x,), (y,), (z,), (w,)],
            [(y,), (z,), (x,), (w,)],
            [(z,), (x,), (y,), (w,)],
            [(x,), (y,), (z,), (w,)],
            [(z,), (x,), (y,), (w,)],
            [(y,), (x,), (z,), (w,)],
        ]
    else:
        stages = [vec_groups(count)] * 6
    S = jax.ShapeDtypeStruct
    outs = {
        "output": S((n, d), F32),
        "uf": S((n, features), F32),
        "rffn": S((sum(chunk_rows[:3]), 128), BF),
        "rqkv": S((3072, 128), BF),
        "rbank": S((2, 1280, 128), BF),
        "vec": S((16, d), F32),
        "late": S((8, 128), F32),
        "stat": S((8, 128), F32),
    }
    out_specs = [vmem if k in ("vec", "late", "stat") else hbm for k in OUT_NAMES]
    V = pltpu.VMEM
    scratch = {
        "F": V((2, n, features), F32),
        "WQKV": V((2, 3, d, 256), BF),
        "WO": V((2, 256, d), BF),
        "UB": V((2, 1, 512), F32),
        "WU": V((2, d, 512), BF),
        "WD": V((2, 512, d), BF),
        "BANKV": V(prompt_bank.shape, BF),
        "COT": V((n, d), F32),
        "TILE": V((2, 8, 128), F32),
        "LATE": V((2, 8, 128), F32),
        "MOM": V((count, 8, 128), F32),
        "LSUM": V((count, 8, 128), F32),
        "STAT": V((8, 128), F32),
        "VEC": V((16, d), F32),
        "VECR": V((16, d), F32),
        "VECS": V((len(vec_groups(count)), 4, 16, d), F32),
        "SEL": V((prompt_bank.shape[0], P_SIZE), BF),
        "SRC": V((KEYS, d), BF),
        "BIAS": V((KEYS, 1), F32),
        "WKV": V((4, d, 256), BF),
        "NL": V((2, n, features), BF),
        "HA": V((2, n, d), F32),
        "HB": V((2, n, d), BF),
        "Q": V((4, n, 128), BF),
        "K": V((4, KEYS, 128), BF),
        "V": V((4, KEYS, 128), BF),
        "E": V((4, KEYS, n), BF),
        "INV": V((4, 8, n), F32),
        "INNER": V((4, 8, n), F32),
        "AT": V((4, 128, n), BF),
        "A": V((n, d), BF),
        "XH": V((n, d), F32),
        "RS": V((n, 1), F32),
        "AB": V((n, d), BF),
        "DG": V((2, n, 512), F32),
        "ACT": V((2, n, 512), BF),
        "DU": V((2, n, 512), BF),
        "OUTB": V((n, d), F32),
        "DJ": V((n, d), F32),
        "GM": V((n, d), BF),
        "GB": V((n, d), BF),
        "DOT": V((4, 128, n), BF),
        "DOT2": V((4, 128, n), BF),
        "DKV": V((4, KEYS, 256), BF),
        "DKVR": V((4, n, 256), BF),
        "DKVO": V((4, n, 256), BF),
        "DQT": V((4, 128, n), BF),
        "DQ": V((n, d), BF),
        "HQT": V((d, n), BF),
        "SRCT": V((d, n), BF),
        "DP": V((2, P_SIZE, d), BF),
        "GH": V((n, d), BF),
        "UF": V((n, features), F32),
        "ENC": V((128, d), F32),
        "TWIN": V((chunk_rows[5], 128), BF),
    }
    for i, r in enumerate(chunk_rows):
        small = 256 if i == 5 else r
        scratch[f"CG{i}"] = V((small, 128), BF)
        scratch[f"CR{i}"] = V((small, 128), BF)
        scratch[f"CA{i}"] = V((r, 128), BF)
        scratch[f"CV{i}"] = V((r, 128), BF)
        scratch[f"CF{i}"] = V((r, 128), BF)
    scratch["ssem"] = pltpu.SemaphoreType.DMA((SEMS,))
    scratch["rsem"] = pltpu.SemaphoreType.DMA((SEMS,))
    scratch["lsem"] = pltpu.SemaphoreType.DMA((40,))
    names = IN_NAMES + OUT_NAMES + list(scratch)
    results = pl.pallas_call(
        functools.partial(layer_kernel, count, total_rows, stages, chunk_rows, names),
        out_shape=[outs[k] for k in OUT_NAMES],
        in_specs=in_specs,
        out_specs=out_specs,
        scratch_shapes=list(scratch.values()),
        compiler_params=pltpu.CompilerParams(
            collective_id=0, has_side_effects=True, vmem_limit_bytes=VMEM_LIMIT
        ),
        name="layer",
    )(*args)
    finals = {
        "o_output": S((n, d), F32),
        "o_feats": S((n, features), F32),
        "o_bank": S(prompt_bank.shape, F32),
        "o_encw": S(enc_weight.shape, F32),
        "o_encb": S((1, d), F32),
        "o_qkv": S(qkv_weight.shape, F32),
        "o_out": S(out_weight.shape, F32),
        "o_outb": S((1, d), F32),
        "o_ag": S((1, d), F32),
        "o_ash": S((1, d), F32),
        "o_up": S(up_weight.shape, F32),
        "o_upb": S((1, up_bias.shape[0]), F32),
        "o_down": S(down_weight.shape, F32),
        "o_downb": S((1, d), F32),
        "o_fg": S((1, d), F32),
        "o_fsh": S((1, d), F32),
    }
    final = pl.pallas_call(
        functools.partial(finish_kernel, total_rows, ["feats"] + OUT_NAMES + list(finals)),
        out_shape=list(finals.values()),
        in_specs=[vmem] * (1 + len(OUT_NAMES)),
        out_specs=[vmem] * len(finals),
        compiler_params=pltpu.CompilerParams(vmem_limit_bytes=VMEM_LIMIT),
        name="finish",
    )(feats, *results)
    return tuple(
        v[0] if k in ("o_encb", "o_outb", "o_ag", "o_ash", "o_upb", "o_downb", "o_fg", "o_fsh") else v
        for k, v in zip(finals, final, strict=True)
    )


def solution(mesh):
    whole = P(("rows", "heads"), None)
    placed = (
        whole, P("rows", None), P("rows"), P("rows", None), P(), P(), P(), P(None, None, "heads"), P("heads", None),
        P(), P(), P(), P(None, "heads"), P("heads"), P("heads", None), P(), P(), P(), whole,
    )
    return jax.shard_map(
        per_device,
        mesh=mesh,
        in_specs=placed,
        out_specs=(
            whole, whole, P(), P(), P(), P(None, None, "heads"), P("heads", None), P(), P(), P(), P(None, "heads"),
            P("heads"), P("heads", None), P(), P(), P(),
        ),
        check_vma=False,
    )
```

```python
import functools
import math

import jax
import jax.numpy as jnp
from jax import lax
from jax.experimental import pallas as pl
from jax.experimental.pallas import tpu as pltpu
from jax.sharding import PartitionSpec as P

BF = jnp.bfloat16
F32 = jnp.float32
MESH = pl.DeviceIdType.MESH
DH = 128
P_SIZE = 128
CONTEXT_MAX = 896
KEYS = CONTEXT_MAX + P_SIZE
EPS = 1e-05
HALF_ROOT = math.sqrt(0.5)
PDF_SCALE = 1.0 / math.sqrt(2.0 * math.pi)
LOG2E = math.log2(math.e)
VMEM_LIMIT = 60 * 2**20


def _dot(a, b, ca, cb):
    return lax.dot_general(a, b, (((ca,), (cb,)), ((), ())), preferred_element_type=F32)


def nn(a, b):
    return _dot(a, b, 1, 0)


def nt(a, b):
    return _dot(a, b, 1, 1)


def tn(a, b):
    return _dot(a, b, 0, 0)


def row_sum(v):
    return jnp.sum(v, axis=0, keepdims=True)


def lane_mean(v):
    return jnp.mean(v, axis=-1, keepdims=True)


class Links:
    def __init__(self, send, recv):
        self.send, self.recv, self.sent, self.received, self.open = send, recv, 0, 0, []

    def send_sem(self):
        self.sent += 1
        return self.send.at[self.sent - 1]

    def recv_sem(self):
        self.received += 1
        return self.recv.at[self.received - 1]

    def start(self, src, dst, device, send, recv):
        c = pltpu.make_async_remote_copy(
            src_ref=src, dst_ref=dst, send_sem=send, recv_sem=recv, device_id=device, device_id_type=MESH
        )
        c.start()
        return c

    def copy(self, src, dst, device):
        c = self.start(src, dst, device, self.send_sem(), self.recv_sem())
        self.open.append(c.wait_send)
        return c

    def drain(self):
        for wait in self.open:
            wait()
        self.open = []


def wait_bytes(ref, sem):
    pltpu.make_async_copy(ref, ref, sem).wait()


class Loads:
    def __init__(self, sems):
        self.sems, self.used = sems, 0

    def copy(self, src, dst):
        c = pltpu.make_async_copy(src, dst, self.sems.at[self.used])
        self.used += 1
        c.start()
        return c


class Part:
    def __init__(self, ctx, block, first, rows, stages):
        self.ctx, self.first, self.rows, self.stages = ctx, first, rows, stages
        self.acc, self.recv, self.full = block.acc, block.recv, block.full
        self.at = 0
        self.send_sem = None

    def begin(self):
        self.base, self.len, self.off, self.k = self.first, self.rows, self.first, 0
        self.send_sem = self.ctx.links.send_sem()
        self._start_scatter()

    def _digits(self, bits, mask):
        digit, row = 0, self.ctx.row
        for i, b in enumerate(bits):
            bit = (self.ctx.row // b) % 2
            if mask >> i & 1:
                row = row + b * (1 - 2 * bit)
                bit = 1 - bit
            digit = digit * 2 + bit
        return digit, row

    def _wait(self, rows):
        view = self.full.at[pl.ds(0, rows)]
        wait_bytes(view, self.recv_sem)
        wait_bytes(view, self.send_sem)

    def _start_scatter(self):
        bits = self.stages[self.k]
        ways = 2 ** len(bits)
        q = self.len // ways
        self.recv_sem = self.ctx.links.recv_sem()
        for mask in range(1, ways):
            digit, row = self._digits(bits, mask)
            src = self.acc.at[pl.ds(pl.multiple_of(self.base + digit * q, 16), q)]
            dst = self.recv.at[pl.ds(self.off + (mask - 1) * q, q)]
            self.ctx.links.start(src, dst, (row, self.ctx.head), self.send_sem, self.recv_sem)

    def _end_scatter(self):
        bits = self.stages[self.k]
        ways = 2 ** len(bits)
        q = self.len // ways
        digit, _ = self._digits(bits, 0)
        self.base = self.base + digit * q
        mine = pl.ds(pl.multiple_of(self.base, 16), q)
        self._wait((ways - 1) * q)
        total = self.acc[mine, :].astype(F32)
        for i in range(ways - 1):
            total = total + self.recv[pl.ds(self.off + i * q, q), :].astype(F32)
        self.off += (ways - 1) * q
        self.len = q
        self.k += 1
        if self.k < len(self.stages):
            self.acc[mine, :] = total.astype(BF)
            self._start_scatter()
        else:
            self.full[mine, :] = total.astype(BF)
            self._start_gather()

    def _start_gather(self):
        bits = self.stages[self.k - 1]
        mine = self.full.at[pl.ds(pl.multiple_of(self.base, 16), self.len)]
        self.recv_sem = self.ctx.links.recv_sem()
        for mask in range(1, 2 ** len(bits)):
            _, row = self._digits(bits, mask)
            self.ctx.links.start(mine, mine, (row, self.ctx.head), self.send_sem, self.recv_sem)

    def _end_gather(self):
        bits = self.stages[self.k - 1]
        ways = 2 ** len(bits)
        self._wait((ways - 1) * self.len)
        digit, _ = self._digits(bits, 0)
        self.base = self.base - digit * self.len
        self.len = self.len * ways
        self.k -= 1
        if self.k > 0:
            self._start_gather()

    def done(self):
        return self.at == 2 * len(self.stages)

    def advance(self):
        if self.at < len(self.stages):
            self._end_scatter()
        elif not self.done():
            self._end_gather()
        self.at += 1


class Block:
    def __init__(self, ctx, refs, cuts):
        self.ctx = ctx
        self.give, self.got, self.acc, self.recv, self.full = refs
        self.n = self.acc.shape[0]
        self.parts, first = [], 0
        for rows, stages in cuts:
            self.parts.append(Part(ctx, self, first, rows, stages))
            first += rows

    def send_core(self):
        self.core_copy = self.ctx.links.copy(self.give, self.got, self.ctx.twin)

    def merge_core(self):
        self.core_copy.wait_recv()
        for part in self.parts:
            rows = slice(part.first, part.first + part.rows)
            self.acc[rows, :] = (self.acc[rows, :].astype(F32) + self.got[rows, :].astype(F32)).astype(BF)
            part.begin()


class Ctx:
    pass


def share_rows(ctx, slots, count):
    mine = slots.at[ctx.row]
    send, recv = ctx.links.send_sem(), ctx.links.recv_sem()
    for k in range(1, count):
        ctx.links.start(mine, mine, (lax.rem(ctx.row + k, count), ctx.head), send, recv)
    others = slots.at[pl.ds(0, count - 1)]
    ctx.links.open.append(functools.partial(wait_bytes, others, send))
    return functools.partial(wait_bytes, others, recv)


SMALL = [
    "mask", "pidx", "encw", "encb", "outb", "ag", "ash", "downb", "fg", "fsh",
]
IN_NAMES = [
    "feats", "mask", "splits", "pidx", "bank", "encw", "encb", "qkvw", "outw", "outb", "ag", "ash", "upw",
    "upb", "downw", "downb", "fg", "fsh", "cot",
]
OUT_NAMES = [
    "output", "uf", "rffn", "rqkv", "rbank", "vec", "late", "stat",
]
CUTS = {
    "d": [(1024, [(1, 2), (4, 8)]), (1024, [(1, 2), (4, 8)])],
    "u": [(1024, [(2,), (1,), (4, 8)]), (1024, [(1,), (2,), (4, 8)])],
    "o": [(1024, [(1,), (2,), (4, 8)])],
    "q": [(768, [(1, 2), (4,), (8,)]), (768, [(4,), (1, 2), (8,)])],
    "r": [(512, [(2,), (1, 4), (8,)]), (512, [(2, 4), (1,), (8,)]), (512, [(1,), (2, 4), (8,)])],
    "l": [(512, [(1,), (2,), (4, 8)]), (512, [(4, 8), (1, 2)]), (256, [(1, 2), (4,), (8,)])],
}
PLAN = [
    [],
    [],
    [],
    ["d0"],
    [],
    [],
    ["d1", "d0"],
    ["u0", "u1"],
    ["d1", "o0", "d0"],
    ["u1", "u0"],
    [],
    ["d1", "o0"],
    ["q1", "u1", "d0", "u0"],
    ["o0", "q0"],
    ["u1", "d1", "q1", "r2", "u0", "r0"],
    ["o0", "q0", "r1", "l0"],
    ["l2", "l1", "u1", "q1", "u0", "r2", "r0", "r1", "q0", "o0", "l2", "l0", "l1", "q1", "r2", "r0", "r1", "q0", "l2", "u1", "l0", "u0", "r2", "r0", "r1", "q0", "l2", "o0", "l1", "l0", "r2", "q1", "l2", "r0", "r1", "l0", "q0", "l1", "r2", "r0", "l2", "q1", "l0", "r1"],
]


def layer_kernel(count, total_rows, cuts, plan, sem_counts, names, *refs):
    g = Ctx()
    for name, ref in zip(names, refs, strict=True):
        setattr(g, name, ref)
    features, n = g.feats.shape
    ctx = Ctx()
    ctx.row, ctx.head = lax.axis_index("rows"), lax.axis_index("heads")
    h = ctx.head
    o = 1 - h
    ctx.twin = (ctx.row, o)
    ctx.links = links = Links(g.ssem, g.rsem)
    loads = Loads(g.lsem)

    l_feats = loads.copy(g.feats, g.F.at[h])
    own = {
        "qkv": (g.qkvw, g.WQKV.at[h]),
        "out": (g.outw, g.WO.at[h]),
        "upb": (g.upb, g.UB.at[h]),
        "up": (g.upw, g.WU.at[h]),
        "down": (g.downw, g.WD.at[h]),
    }
    g.TILE[...] = jnp.zeros_like(g.TILE)
    barrier = pltpu.get_barrier_semaphore()
    pl.semaphore_signal(barrier, inc=1, device_id=ctx.twin, device_id_type=MESH)
    for k in range(1, count):
        pl.semaphore_signal(
            barrier, inc=1, device_id=(lax.rem(ctx.row + k, count), h), device_id_type=MESH
        )
    l_small = [loads.copy(getattr(g, k), getattr(g, k + "_")) for k in SMALL]
    l_bank = loads.copy(g.bank, g.BANKV)
    l_own = {k: loads.copy(*v) for k, v in own.items()}
    l_cot = loads.copy(g.cot, g.COT)

    def to_rows(columns):
        for i, c in enumerate(columns):
            g.SQUARE[0:features, i : i + 1] = c
        return g.SQUARE[...].T[0:8, :]

    def lane_sum(v):
        return jnp.sum(v, axis=-1, keepdims=True)

    g.SQUARE[...] = jnp.zeros_like(g.SQUARE)
    l_feats.wait()
    f = g.F[h]
    g.TILE[0] = to_rows([lane_sum(f), lane_sum(f * f)])
    pl.semaphore_wait(barrier, count)
    c_tile = links.copy(g.TILE.at[0], g.TILE.at[1], ctx.twin)
    c_feats = links.copy(g.feats, g.F.at[h], ctx.twin)
    c_tile.wait_recv()
    g.MOM[ctx.row] = g.TILE[0] + g.TILE[1]
    wait_moments = share_rows(ctx, g.MOM, count)
    c_own = {k: links.copy(*v, ctx.twin) for k, v in own.items()}

    for c in l_small:
        c.wait()
    selector = lax.broadcasted_iota(jnp.int32, (g.bank.shape[0], P_SIZE), 0) == g.pidx_[...]
    g.SEL[...] = jnp.where(selector, 1.0, 0.0).astype(BF)
    l_bank.wait()
    g.SRC[CONTEXT_MAX:KEYS, :] = tn(g.SEL[...], g.BANKV[...]).astype(BF)
    visible = lax.broadcasted_iota(jnp.int32, (KEYS, 1), 0)
    visible = (visible < g.splits[0]) | (visible >= CONTEXT_MAX)
    g.BIAS[...] = jnp.where(visible, 0.0, -1e30)
    g.VEC[...] = jnp.zeros_like(g.VEC)
    g.LATE[0] = jnp.zeros_like(g.LATE[0])
    live = g.mask_[...].astype(F32)
    scale = live * jnp.sqrt(features / jnp.sum(live, axis=-1, keepdims=True))
    g.STAT[...] = jnp.zeros_like(g.STAT)
    g.STAT[2:3, 0:features] = scale
    for c in l_own.values():
        c.wait()
    c_own["qkv"].wait_recv()
    for j in range(4):
        s, w = j // 2, pl.ds(128 * (j % 2), 128)
        g.WKV[j, :, 0:128] = g.WQKV[s, 1, :, w]
        g.WKV[j, :, 128:256] = g.WQKV[s, 2, :, w]

    c_feats.wait_recv()
    wait_moments()
    moments = g.MOM[0]
    for k in range(1, count):
        moments = moments + g.MOM[k]
    mean = moments[0:1, :] / total_rows
    var = moments[1:2, :] / total_rows - mean * mean
    g.STAT[0:1, :] = mean
    g.STAT[1:2, :] = lax.rsqrt(var + EPS)
    g.SQUARE[0:8, :] = g.STAT[...]
    columns = g.SQUARE[...].T
    mean, inverse, scale = [columns[0:features, i : i + 1] for i in range(3)]
    g.COLS[...] = columns[0:features, :]

    for s in range(2):
        g.NL[s] = (((g.F[s] - mean) * inverse) * scale).astype(BF)
        hidden = tn(g.NL[s], g.encw_[...]) + g.encb_[...]
        g.HA[s] = hidden
        g.HB[s] = hidden.astype(BF)
    g.SRC[0:n, :] = g.HB[0]
    g.SRC[n:CONTEXT_MAX, :] = g.HB[1, 0 : CONTEXT_MAX - n, :]

    for s in range(2):
        q = nn(g.HB[h], g.WQKV[s, 0]).astype(BF)
        for j in range(2):
            g.Q[2 * s + j] = q[:, 128 * j : 128 * j + 128]

    def project(j, _):
        kv = nn(g.SRC[...], g.WKV[j]).astype(BF)
        g.K[j] = kv[:, 0:128]
        g.V[j] = kv[:, 128:256]
        return 0

    lax.fori_loop(0, 4, project, 0)

    def attend(j, _):
        for t in range(n // 256):
            cols = slice(256 * t, 256 * t + 256)
            scores = nt(g.K[j], g.Q[j, cols, :]) * (DH**-0.5 * LOG2E) + g.BIAS[...]
            e = jnp.exp2(scores - jnp.max(scores, axis=0, keepdims=True))
            inv = 1.0 / row_sum(e)
            g.INV[j, 0:1, cols] = inv
            e = e.astype(BF)
            g.E[j, :, cols] = e
            g.AT[j, :, cols] = (tn(g.V[j], e) * inv).astype(BF)
        return 0

    lax.fori_loop(0, 4, attend, 0)

    c_own["out"].wait_recv()
    c_own["up"].wait_recv()
    c_own["upb"].wait_recv()
    c_own["down"].wait_recv()
    for j in range(4):
        g.A[:, 128 * j : 128 * j + 128] = g.AT[j].T
    l_cot.wait()

    tile = 256

    def forward(t, _):
        rows = pl.ds(pl.multiple_of(t * tile, tile), tile)
        branch = nn(g.A[rows, 0:256], g.WO[0]) + nn(g.A[rows, 256:512], g.WO[1]) + g.outb_[...]
        joined = g.HA[h, rows, :] + branch
        center = joined - lane_mean(joined)
        rstd = lax.rsqrt(lane_mean(center * center) + EPS)
        xhat = center * rstd
        after = xhat * g.ag_[...] + g.ash_[...]
        g.XH[rows, :] = xhat
        g.RS[rows, :] = rstd
        low = after.astype(BF)
        g.AB[rows, :] = low
        mixed = g.downb_[...]
        for s in range(2):
            u = nn(low, g.WU[s]) + g.UB[s]
            phi = 0.5 * (1.0 + lax.erf(u * HALF_ROOT))
            g.DG[s, rows, :] = phi + u * (jnp.exp2(u * u * (-0.5 * LOG2E)) * PDF_SCALE)
            act = (u * phi).astype(BF)
            g.ACT[s, rows, :] = act
            mixed = mixed + nn(act, g.WD[s])
        joined = after + mixed
        center = joined - lane_mean(joined)
        rstd = lax.rsqrt(lane_mean(center * center) + EPS)
        xhat = center * rstd
        g.OUTB[rows, :] = xhat * g.fg_[...] + g.fsh_[...]
        ct = g.COT[rows, :]
        d = ct * g.fg_[...]
        d = rstd * (d - lane_mean(d) - xhat * lane_mean(d * xhat))
        g.DJ[rows, :] = d
        gm = d.astype(BF)
        g.GM[rows, :] = gm
        g.VEC[4:5, :] += row_sum(gm.astype(F32))
        g.VEC[5:6, :] += row_sum(ct * xhat)
        g.VEC[6:7, :] += row_sum(ct)
        return 0

    lax.fori_loop(0, n // tile, forward, 0)
    l_output = loads.copy(g.OUTB, g.output)

    def put(ref, first, value):
        r = value.shape[0]
        for b in range(value.shape[1] // 128):
            ref[first + r * b : first + r * b + r, :] = value[:, 128 * b : 128 * b + 128]

    blocks = {
        k: Block(ctx, [getattr(g, p + k) for p in ("CG", "CR", "CA", "CV", "CF")], v) for k, v in cuts.items()
    }
    down, up, out, qkv0, qkv1, last = blocks.values()

    def tick(i):
        for k in plan[i] if i < len(plan) else []:
            blocks[k[0]].parts[int(k[1])].advance()

    put(down.give, 0, tn(g.ACT[o], g.GM[...]).astype(BF))
    down.send_core()
    put(down.acc, 0, tn(g.ACT[h], g.GM[...]).astype(BF))
    down.merge_core()

    def backward(t):
        rows = slice(t * tile, t * tile + tile)
        gm = g.GM[rows, :]
        d = g.DJ[rows, :]
        for s in range(2):
            du = (g.DG[s, rows, :] * nt(gm, g.WD[s])).astype(BF)
            g.DU[s, rows, :] = du
            g.VEC[7 + s : 8 + s, :] += row_sum(du.astype(F32))
            d = d + nt(du, g.WU[s])
        xhat = g.XH[rows, :]
        g.VEC[2:3, :] += row_sum(d * xhat)
        g.VEC[3:4, :] += row_sum(d)
        d = d * g.ag_[...]
        d = g.RS[rows, :] * (d - lane_mean(d) - xhat * lane_mean(d * xhat))
        g.DJ[rows, :] = d
        gb = d.astype(BF)
        g.GB[rows, :] = gb
        g.VEC[1:2, :] += row_sum(gb.astype(F32))

    for t in range(n // tile):
        backward(t)
    tick(2)
    put(up.give, 0, tn(g.AB[...], g.DU[o]).astype(BF))
    up.send_core()
    for j in range(2):
        put(out.give, 128 * j * 4, nn(g.AT[2 * o + j], g.GB[...]).astype(BF))
    out.send_core()
    c_vec = links.copy(g.VEC, g.VECR, ctx.twin)
    put(up.acc, 0, tn(g.AB[...], g.DU[h]).astype(BF))
    for j in range(2):
        put(out.acc, 128 * j * 4, nn(g.AT[2 * h + j], g.GB[...]).astype(BF))
    tick(3)
    up.merge_core()
    out.merge_core()
    tick(4)

    for j in range(4):
        d = nt(g.WO[j // 2, 128 * (j % 2) : 128 * (j % 2) + 128, :], g.GB[...]).astype(BF)
        g.DOT[j] = d
        df = d.astype(F32)
        g.INNER[j, 0:1, :] = row_sum(df * g.AT[j].astype(F32))
        g.DOT2[j] = (df * g.INV[j, 0:1, :]).astype(BF)
        g.INV[j, 1:2, :] = g.INV[j, 0:1, :] * (DH**-0.5)

    vec_stages = vec_groups(count)
    vec = Ctx()
    vec.k = 0

    def vec_start(value):
        bits = vec_stages[vec.k]
        digit, _ = down.parts[0]._digits(bits, 0)
        slots = g.VECS.at[vec.k]
        slots[digit] = value
        send, vec.sem = links.send_sem(), links.recv_sem()
        others = slots.at[pl.ds(0, 2 ** len(bits) - 1)]
        for mask in range(1, 2 ** len(bits)):
            _, row = down.parts[0]._digits(bits, mask)
            links.start(slots.at[digit], slots.at[digit], (row, h), send, vec.sem)
        links.open.append(functools.partial(wait_bytes, others, send))

    def vec_end():
        ways = 2 ** len(vec_stages[vec.k])
        wait_bytes(g.VECS.at[vec.k, pl.ds(0, ways - 1)], vec.sem)
        value = g.VECS[vec.k, 0]
        for i in range(1, ways):
            value = value + g.VECS[vec.k, i]
        vec.k += 1
        if vec.k < len(vec_stages):
            vec_start(value)
        else:
            g.vec[...] = value

    kv_copies = {}

    def attend_back(j):
        q, dot, dot2 = g.Q[j], g.DOT[j], g.DOT2[j]
        inner, factor = g.INNER[j, 0:1, :], g.INV[j, 1:2, :]

        def block(t, dq):
            rows = pl.ds(pl.multiple_of(t * 256, 256), 256)
            e = g.E[j, rows, :]
            upstream = nn(g.V[j, rows, :], dot)
            ds = (e.astype(F32) * ((upstream - inner) * factor)).astype(BF)
            g.DKV[j, rows, 0:128] = nn(ds, q).astype(BF)
            g.DKV[j, rows, 128:256] = nt(e, dot2).astype(BF)
            return dq + tn(g.K[j, rows, :], ds)

        dq = lax.fori_loop(0, KEYS // 256, block, jnp.zeros((128, n), F32))
        g.DQT[j] = dq.astype(BF)
        other = pl.ds(pl.multiple_of(o * n, n), n)
        kv_copies[j] = links.copy(g.DKV.at[j, other], g.DKVR.at[j], ctx.twin)

    def merge_kv(j):
        kv_copies[j].wait_recv()
        mine = pl.ds(pl.multiple_of(h * n, n), n)
        g.DKVO[j] = (g.DKV[j, mine, :].astype(F32) + g.DKVR[j].astype(F32)).astype(BF)

    def head_grads(j, ref):
        put(ref, 0, nt(g.HQT[...], g.DQT[j]).astype(BF))
        put(ref, n, nn(g.SRCT[...], g.DKVO[j]).astype(BF))

    def pair_grads(p, block):
        head_grads(2 * o + p, block.give)
        block.send_core()
        head_grads(2 * h + p, block.acc)

    g.HQT[...] = g.HB[h].T
    g.SRCT[...] = g.SRC[pl.ds(pl.multiple_of(h * n, n), n), :].T
    tick(5)
    attend_back(0)
    tick(6)
    attend_back(2)
    tick(7)
    merge_kv(0)
    merge_kv(2)
    pair_grads(0, qkv0)
    tick(8)
    qkv0.merge_core()
    c_vec.wait_recv()
    vec_start(g.VEC[...] + g.VECR[...])
    tick(9)
    attend_back(1)
    tick(10)
    attend_back(3)
    tick(11)
    vec_end()
    merge_kv(1)
    merge_kv(3)
    pair_grads(1, qkv1)
    tick(12)
    qkv1.merge_core()
    tick(13)

    kvh = nt(g.DKVO[0], g.WKV[0])
    for j in range(1, 4):
        kvh = kvh + nt(g.DKVO[j], g.WKV[j])
    edge = CONTEXT_MAX - n
    g.DP[0] = kvh[edge:n, :].astype(BF)
    c_prompt = links.copy(g.DP.at[0], g.DP.at[1], ctx.twin)
    for j in range(4):
        g.DQ[:, 128 * j : 128 * j + 128] = g.DQT[j].T
    dh = g.DJ[...]
    for j in range(4):
        w = g.WQKV[j // 2, 0, :, 128 * (j % 2) : 128 * (j % 2) + 128]
        dh = dh + nt(g.DQ[:, 128 * j : 128 * j + 128], w)
    g.GH[0:edge, :] = (dh[0:edge] + kvh[0:edge]).astype(BF)
    first = jnp.where(h == 0, 1.0, 0.0)
    g.GH[edge:n, :] = (dh[edge:n] + kvh[edge:n] * first).astype(BF)
    gh = g.GH[...]
    g.ENC[0:features, :] = nn(g.NL[h], gh)
    g.ENC[features:, :] = jnp.zeros_like(g.ENC[features:, :])
    bank_rows = g.bank.shape[0] // 2
    enc_at = bank_rows * 4
    for b in range(4):
        cols = slice(128 * b, 128 * b + 128)
        last.give[64 * b : 64 * b + 64, :] = g.ENC[pl.ds(pl.multiple_of(o * 64, 64), 64), cols].astype(BF)
        last.acc[enc_at + 64 * b : enc_at + 64 * b + 64, :] = g.ENC[
            pl.ds(pl.multiple_of(h * 64, 64), 64), cols
        ].astype(BF)
    last.send_core()
    c_prompt.wait_recv()
    put(
        last.acc,
        0,
        nn(g.SEL[pl.ds(pl.multiple_of(h * bank_rows, bank_rows), bank_rows), :], g.DP[o]).astype(BF),
    )
    last.core_copy.wait_recv()
    rows = slice(enc_at, enc_at + 256)
    last.acc[rows, :] = (last.acc[rows, :].astype(F32) + last.got[...].astype(F32)).astype(BF)
    if last.n > enc_at + 256:
        last.acc[enc_at + 256 :, :] = jnp.zeros_like(last.acc[enc_at + 256 :, :])
    for part in last.parts:
        part.begin()
    tick(14)

    scale = g.COLS[:, 2:3]
    uf = nt(g.encw_[...], gh) * scale
    g.UF[...] = uf
    g.SQUARE[...] = jnp.zeros_like(g.SQUARE)
    g.LATE[0] = to_rows([lane_sum(uf), lane_sum(uf * (g.F[h] - g.COLS[:, 0:1]))])
    eb = row_sum(gh.astype(F32))
    for b in range(4):
        g.LATE[0, 2 + b : 3 + b, :] = eb[:, 128 * b : 128 * b + 128]
    c_late = links.copy(g.LATE.at[0], g.LATE.at[1], ctx.twin)
    l_uf = loads.copy(g.UF, g.uf)
    tick(15)
    c_late.wait_recv()
    g.LSUM[ctx.row] = g.LATE[0] + g.LATE[1]
    wait_late = share_rows(ctx, g.LSUM, count)
    tick(16)
    rest = [p for b in blocks.values() for p in b.parts]
    while not all(p.done() for p in rest):
        for p in rest:
            if not p.done():
                p.advance()
    while vec.k < len(vec_stages):
        vec_end()
    c_last = links.copy(last.full, g.TWIN, ctx.twin)
    stores = [l_output, l_uf]
    at = 0
    for b in (down, up, out):
        stores.append(loads.copy(b.full, g.rffn.at[pl.ds(at, b.n)]))
        at += b.n
    at = 0
    for b in (qkv0, qkv1):
        stores.append(loads.copy(b.full.at[0:1536], g.rqkv.at[pl.ds(at, 1536)]))
        at += 1536
    wait_late()
    late = g.LSUM[0]
    for k in range(1, count):
        late = late + g.LSUM[k]
    g.late[...] = late
    g.stat[...] = g.STAT[...]
    stores.append(loads.copy(last.full.at[0 : enc_at + 256], g.rbank.at[h]))
    c_last.wait_recv()
    stores.append(loads.copy(g.TWIN.at[0 : enc_at + 256], g.rbank.at[o]))
    for c in stores:
        c.wait()
    links.drain()
    assert (links.sent, links.received, loads.used) == sem_counts, (links.sent, links.received, loads.used)


def vec_groups(count):
    bits = [2**i for i in range(count.bit_length() - 1)]
    return [tuple(bits[i : i + 2]) for i in range(0, len(bits), 2)]


def finish_kernel(total_rows, names, *refs):
    g = Ctx()
    for name, ref in zip(names, refs, strict=True):
        setattr(g, name, ref)
    h = lax.axis_index("heads")
    features = g.feats.shape[0]
    copies = []

    def copy(src, dst):
        c = pltpu.make_async_copy(src, dst, g.sems.at[len(copies)])
        c.start()
        copies.append(c)
        return c

    c_output = copy(g.output, g.OUTPUT)
    c_ffn = copy(g.rffn, g.RFFN)
    c_qkv = copy(g.rqkv, g.RQKV)
    c_bank = copy(g.rbank, g.RBANK)
    c_feats = copy(g.feats, g.FEATS)
    c_uf = copy(g.uf, g.UF)

    def block(ref, first, rows):
        return ref[first : first + rows, :].astype(F32)

    c_output.wait()
    outs = [copy(g.OUTPUT, g.o_output)]
    c_ffn.wait()
    for b in range(4):
        cols = slice(128 * b, 128 * b + 128)
        g.DOWN[:, cols] = block(g.RFFN, 512 * b, 512)
    outs.append(copy(g.DOWN, g.o_down))
    for b in range(4):
        cols = slice(128 * b, 128 * b + 128)
        g.UP[:, cols] = block(g.RFFN, 2048 + 512 * b, 512)
    outs.append(copy(g.UP, g.o_up))
    for b in range(4):
        cols = slice(128 * b, 128 * b + 128)
        for j in range(2):
            g.OUT[128 * j : 128 * j + 128, cols] = block(g.RFFN, 4096 + 512 * j + 128 * b, 128)
    outs.append(copy(g.OUT, g.o_out))
    c_qkv.wait()
    for c in range(3):
        for p in range(2):
            g.QKV[c, :, 128 * p : 128 * p + 128] = block(g.RQKV, 1536 * p + 512 * c, 512)
    outs.append(copy(g.QKV, g.o_qkv))
    c_bank.wait()
    for b in range(4):
        cols = slice(128 * b, 128 * b + 128)
        for s in range(2):
            g.BANKV[256 * s : 256 * s + 256, cols] = g.RBANK[s, 256 * b : 256 * b + 256, :].astype(F32)
        g.o_encw[0:64, cols] = g.RBANK[0, 1024 + 64 * b : 1024 + 64 * b + 64, :].astype(F32)
        g.o_encw[64:features, cols] = g.RBANK[1, 1024 + 64 * b : 1024 + 64 * b + features - 64, :].astype(F32)
        g.o_encb[:, cols] = g.late[2 + b : 3 + b, :]
    outs.append(copy(g.BANKV, g.o_bank))
    g.o_outb[...] = g.vec[1:2, :]
    g.o_ag[...] = g.vec[2:3, :]
    g.o_ash[...] = g.vec[3:4, :]
    g.o_downb[...] = g.vec[4:5, :]
    g.o_fg[...] = g.vec[5:6, :]
    g.o_fsh[...] = g.vec[6:7, :]
    g.o_upb[...] = g.vec[pl.ds(7 + h, 1), :]
    mean, inverse = g.stat[0:1, :], g.stat[1:2, :]
    b1, b2 = g.late[0:1, :], g.late[1:2, :]
    var_grad = -0.5 * inverse * inverse * inverse * b2
    g.SQUARE[...] = jnp.zeros_like(g.SQUARE)
    g.SQUARE[0:1, :] = inverse
    g.SQUARE[1:2, :] = (-inverse * b1 - 2.0 * mean * var_grad) / total_rows
    g.SQUARE[2:3, :] = 2.0 * var_grad / total_rows
    columns = g.SQUARE[...].T
    inverse, first, slope = [columns[0:features, i : i + 1] for i in range(3)]
    c_feats.wait()
    c_uf.wait()
    g.o_feats[...] = g.UF[...] * inverse + first + g.FEATS[...] * slope
    for c in outs:
        c.wait()


def per_device(
    feats,
    feature_mask,
    splits,
    prompt_index,
    prompt_bank,
    enc_weight,
    enc_bias,
    qkv_weight,
    out_weight,
    out_bias,
    attn_gain,
    attn_shift,
    up_weight,
    up_bias,
    down_weight,
    down_bias,
    ffn_gain,
    ffn_shift,
    cotangent,
):
    n, features = feats.shape
    count = lax.axis_size("rows")
    total_rows = n * count * lax.axis_size("heads")
    d = prompt_bank.shape[1]
    columns = feats.T
    args = [
        columns, feature_mask, splits, prompt_index, prompt_bank, enc_weight, enc_bias[None], qkv_weight, out_weight,
        out_bias[None], attn_gain[None], attn_shift[None], up_weight, up_bias[None], down_weight, down_bias[None],
        ffn_gain[None], ffn_shift[None], cotangent,
    ]
    vmem = pl.BlockSpec(memory_space=pltpu.VMEM)
    hbm = pl.BlockSpec(memory_space=pl.ANY)
    in_specs = [pl.BlockSpec(memory_space=pltpu.SMEM) if k == "splits" else hbm for k in IN_NAMES]
    bits = [2**i for i in range(count.bit_length() - 1)]
    grain = 16 * count
    block_rows = {"d": 2048, "u": 2048, "o": 1024, "q": 1536, "r": 1536, "l": 1280}
    if count == 16:
        cuts, plan = CUTS, PLAN
    else:
        cuts, plan = {k: [(-(-r // grain) * grain, vec_groups(count))] for k, r in block_rows.items()}, []
    block_rows = {k: sum(r for r, _ in v) for k, v in cuts.items()}
    S = jax.ShapeDtypeStruct
    outs = {
        "output": S((n, d), F32),
        "uf": S((features, n), F32),
        "rffn": S((block_rows["d"] + block_rows["u"] + block_rows["o"], 128), BF),
        "rqkv": S((3072, 128), BF),
        "rbank": S((2, 1280, 128), BF),
        "vec": S((16, d), F32),
        "late": S((8, 128), F32),
        "stat": S((8, 128), F32),
    }
    out_specs = [vmem if k in ("vec", "late", "stat") else hbm for k in OUT_NAMES]
    V = pltpu.VMEM
    scratch = {k + "_": V(args[IN_NAMES.index(k)].shape, args[IN_NAMES.index(k)].dtype) for k in SMALL}
    scratch |= {
        "F": V((2, features, n), F32),
        "WQKV": V((2, 3, d, 256), BF),
        "WO": V((2, 256, d), BF),
        "UB": V((2, 1, 512), F32),
        "WU": V((2, d, 512), BF),
        "WD": V((2, 512, d), BF),
        "BANKV": V(prompt_bank.shape, BF),
        "COT": V((n, d), F32),
        "SQUARE": V((128, 128), F32),
        "COLS": V((features, 128), F32),
        "TILE": V((2, 8, 128), F32),
        "LATE": V((2, 8, 128), F32),
        "MOM": V((count, 8, 128), F32),
        "LSUM": V((count, 8, 128), F32),
        "STAT": V((8, 128), F32),
        "VEC": V((16, d), F32),
        "VECR": V((16, d), F32),
        "VECS": V((len(vec_groups(count)), 4, 16, d), F32),
        "SEL": V((prompt_bank.shape[0], P_SIZE), BF),
        "SRC": V((KEYS, d), BF),
        "BIAS": V((KEYS, 1), F32),
        "WKV": V((4, d, 256), BF),
        "NL": V((2, features, n), BF),
        "HA": V((2, n, d), F32),
        "HB": V((2, n, d), BF),
        "Q": V((4, n, 128), BF),
        "K": V((4, KEYS, 128), BF),
        "V": V((4, KEYS, 128), BF),
        "E": V((4, KEYS, n), BF),
        "INV": V((4, 8, n), F32),
        "INNER": V((4, 8, n), F32),
        "AT": V((4, 128, n), BF),
        "A": V((n, d), BF),
        "XH": V((n, d), F32),
        "RS": V((n, 1), F32),
        "AB": V((n, d), BF),
        "DG": V((2, n, 512), F32),
        "ACT": V((2, n, 512), BF),
        "DU": V((2, n, 512), BF),
        "OUTB": V((n, d), F32),
        "DJ": V((n, d), F32),
        "GM": V((n, d), BF),
        "GB": V((n, d), BF),
        "DOT": V((4, 128, n), BF),
        "DOT2": V((4, 128, n), BF),
        "DKV": V((4, KEYS, 256), BF),
        "DKVR": V((4, n, 256), BF),
        "DKVO": V((4, n, 256), BF),
        "DQT": V((4, 128, n), BF),
        "DQ": V((n, d), BF),
        "HQT": V((d, n), BF),
        "SRCT": V((d, n), BF),
        "DP": V((2, P_SIZE, d), BF),
        "GH": V((n, d), BF),
        "UF": V((features, n), F32),
        "ENC": V((128, d), F32),
        "TWIN": V((block_rows["l"], 128), BF),
    }
    for k, r in block_rows.items():
        small = 256 if k == "l" else r
        scratch["CG" + k] = V((small, 128), BF)
        scratch["CR" + k] = V((small, 128), BF)
        scratch["CA" + k] = V((r, 128), BF)
        scratch["CV" + k] = V((r, 128), BF)
        scratch["CF" + k] = V((r, 128), BF)
    parts = [stages for v in cuts.values() for _, stages in v]
    once = 23 + len(vec_groups(count))
    sem_counts = (once + len(parts), once + sum(2 * len(s) for s in parts), 17 + len(SMALL))
    for k, v in zip(("ssem", "rsem", "lsem"), sem_counts, strict=True):
        scratch[k] = pltpu.SemaphoreType.DMA((v,))
    names = IN_NAMES + OUT_NAMES + list(scratch)
    results = pl.pallas_call(
        functools.partial(layer_kernel, count, total_rows, cuts, plan, sem_counts, names),
        out_shape=[outs[k] for k in OUT_NAMES],
        in_specs=in_specs,
        out_specs=out_specs,
        scratch_shapes=list(scratch.values()),
        compiler_params=pltpu.CompilerParams(
            collective_id=0, has_side_effects=True, vmem_limit_bytes=VMEM_LIMIT
        ),
        name="layer",
    )(*args)
    finals = {
        "o_output": S((n, d), F32),
        "o_feats": S((features, n), F32),
        "o_bank": S(prompt_bank.shape, F32),
        "o_encw": S(enc_weight.shape, F32),
        "o_encb": S((1, d), F32),
        "o_qkv": S(qkv_weight.shape, F32),
        "o_out": S(out_weight.shape, F32),
        "o_outb": S((1, d), F32),
        "o_ag": S((1, d), F32),
        "o_ash": S((1, d), F32),
        "o_up": S(up_weight.shape, F32),
        "o_upb": S((1, up_bias.shape[0]), F32),
        "o_down": S(down_weight.shape, F32),
        "o_downb": S((1, d), F32),
        "o_fg": S((1, d), F32),
        "o_fsh": S((1, d), F32),
    }
    moved = {"o_output", "o_bank", "o_qkv", "o_out", "o_up", "o_down"}
    work = {
        "OUTPUT": V((n, d), F32),
        "RFFN": V(outs["rffn"].shape, BF),
        "RQKV": V((3072, 128), BF),
        "RBANK": V((2, 1280, 128), BF),
        "FEATS": V((features, n), F32),
        "UF": V((features, n), F32),
        "DOWN": V(down_weight.shape, F32),
        "UP": V(up_weight.shape, F32),
        "OUT": V(out_weight.shape, F32),
        "QKV": V(qkv_weight.shape, F32),
        "BANKV": V(prompt_bank.shape, F32),
        "SQUARE": V((128, 128), F32),
        "sems": pltpu.SemaphoreType.DMA((12,)),
    }
    final = pl.pallas_call(
        functools.partial(finish_kernel, total_rows, ["feats"] + OUT_NAMES + list(finals) + list(work)),
        out_shape=list(finals.values()),
        in_specs=[vmem if k in ("vec", "late", "stat") else hbm for k in ["feats"] + OUT_NAMES],
        out_specs=[hbm if k in moved else vmem for k in finals],
        scratch_shapes=list(work.values()),
        compiler_params=pltpu.CompilerParams(vmem_limit_bytes=VMEM_LIMIT),
        name="finish",
    )(columns, *results)
    vectors = ("o_encb", "o_outb", "o_ag", "o_ash", "o_upb", "o_downb", "o_fg", "o_fsh")
    return tuple(
        v[0] if k in vectors else v.T if k == "o_feats" else v for k, v in zip(finals, final, strict=True)
    )


def solution(mesh):
    whole = P(("rows", "heads"), None)
    placed = (
        whole, P("rows", None), P("rows"), P("rows", None), P(), P(), P(), P(None, None, "heads"), P("heads", None),
        P(), P(), P(), P(None, "heads"), P("heads"), P("heads", None), P(), P(), P(), whole,
    )
    return jax.shard_map(
        per_device,
        mesh=mesh,
        in_specs=placed,
        out_specs=(
            whole, whole, P(), P(), P(), P(None, None, "heads"), P("heads", None), P(), P(), P(), P(None, "heads"),
            P("heads"), P("heads", None), P(), P(), P(),
        ),
        check_vma=False,
    )
```

```python
import functools
import math

import jax
import jax.numpy as jnp
from jax import lax
from jax.experimental import pallas as pl
from jax.experimental.pallas import tpu as pltpu
from jax.sharding import PartitionSpec as P

BF = jnp.bfloat16
F32 = jnp.float32
MESH = pl.DeviceIdType.MESH
DH = 128
P_SIZE = 128
CONTEXT_MAX = 896
CONTEXT_MIN = 640
KEYS = CONTEXT_MAX + P_SIZE
EPS = 1e-05
HALF_ROOT = math.sqrt(0.5)
PDF_SCALE = 1.0 / math.sqrt(2.0 * math.pi)
LOG2E = math.log2(math.e)
Q_SCALE = DH**-0.5 * LOG2E
VMEM_LIMIT = 52 * 2**20


def _dot(a, b, ca, cb):
    return lax.dot_general(a, b, (((ca,), (cb,)), ((), ())), preferred_element_type=F32)


def nn(a, b):
    return _dot(a, b, 1, 0)


def nt(a, b):
    return _dot(a, b, 1, 1)


def tn(a, b):
    return _dot(a, b, 0, 0)


def row_sum(v):
    return jnp.sum(v, axis=0, keepdims=True)


def lane_mean(v):
    return jnp.mean(v, axis=-1, keepdims=True)


class Links:
    def __init__(self, send, recv):
        self.send, self.recv, self.sent, self.received, self.open = send, recv, 0, 0, []

    def send_sem(self):
        self.sent += 1
        return self.send.at[self.sent - 1]

    def recv_sem(self):
        self.received += 1
        return self.recv.at[self.received - 1]

    def start(self, src, dst, device, send, recv):
        c = pltpu.make_async_remote_copy(
            src_ref=src, dst_ref=dst, send_sem=send, recv_sem=recv, device_id=device, device_id_type=MESH
        )
        c.start()
        return c

    def copy(self, src, dst, device):
        c = self.start(src, dst, device, self.send_sem(), self.recv_sem())
        self.open.append(c.wait_send)
        return c

    def drain(self):
        for wait in self.open:
            wait()
        self.open = []


def wait_bytes(ref, sem):
    pltpu.make_async_copy(ref, ref, sem).wait()


class Loads:
    def __init__(self, sems):
        self.sems, self.used = sems, 0

    def copy(self, src, dst):
        c = pltpu.make_async_copy(src, dst, self.sems.at[self.used])
        self.used += 1
        c.start()
        return c


class Part:
    def __init__(self, ctx, block, first, rows, stages):
        self.ctx, self.first, self.rows, self.stages = ctx, first, rows, stages
        self.acc, self.recv, self.full = block.acc, block.recv, block.full
        self.at = 0
        self.send_sem = None

    def begin(self):
        self.base, self.len, self.off, self.k = self.first, self.rows, self.first, 0
        self.send_sem = self.ctx.links.send_sem()
        self._start_scatter()

    def _digits(self, bits, mask):
        digit, row = 0, self.ctx.row
        for i, b in enumerate(bits):
            bit = (self.ctx.row // b) % 2
            if mask >> i & 1:
                row = row + b * (1 - 2 * bit)
                bit = 1 - bit
            digit = digit * 2 + bit
        return digit, row

    def _wait(self, rows):
        view = self.full.at[pl.ds(0, rows)]
        wait_bytes(view, self.recv_sem)
        wait_bytes(view, self.send_sem)

    def _start_scatter(self):
        bits = self.stages[self.k]
        ways = 2 ** len(bits)
        q = self.len // ways
        self.recv_sem = self.ctx.links.recv_sem()
        for mask in range(1, ways):
            digit, row = self._digits(bits, mask)
            src = self.acc.at[pl.ds(pl.multiple_of(self.base + digit * q, 16), q)]
            dst = self.recv.at[pl.ds(self.off + (mask - 1) * q, q)]
            self.ctx.links.start(src, dst, (row, self.ctx.head), self.send_sem, self.recv_sem)

    def _end_scatter(self):
        bits = self.stages[self.k]
        ways = 2 ** len(bits)
        q = self.len // ways
        digit, _ = self._digits(bits, 0)
        self.base = self.base + digit * q
        mine = pl.ds(pl.multiple_of(self.base, 16), q)
        self._wait((ways - 1) * q)
        total = self.acc[mine, :].astype(F32)
        for i in range(ways - 1):
            total = total + self.recv[pl.ds(self.off + i * q, q), :].astype(F32)
        self.off += (ways - 1) * q
        self.len = q
        self.k += 1
        if self.k < len(self.stages):
            self.acc[mine, :] = total.astype(BF)
            self._start_scatter()
        else:
            self.full[mine, :] = total.astype(BF)
            self._start_gather()

    def _start_gather(self):
        bits = self.stages[self.k - 1]
        mine = self.full.at[pl.ds(pl.multiple_of(self.base, 16), self.len)]
        self.recv_sem = self.ctx.links.recv_sem()
        for mask in range(1, 2 ** len(bits)):
            _, row = self._digits(bits, mask)
            self.ctx.links.start(mine, mine, (row, self.ctx.head), self.send_sem, self.recv_sem)

    def _end_gather(self):
        bits = self.stages[self.k - 1]
        ways = 2 ** len(bits)
        self._wait((ways - 1) * self.len)
        digit, _ = self._digits(bits, 0)
        self.base = self.base - digit * self.len
        self.len = self.len * ways
        self.k -= 1
        if self.k > 0:
            self._start_gather()

    def done(self):
        return self.at == 2 * len(self.stages)

    def advance(self):
        if self.at < len(self.stages):
            self._end_scatter()
        elif not self.done():
            self._end_gather()
        self.at += 1


class Block:
    def __init__(self, ctx, refs, cuts):
        self.ctx = ctx
        self.give, self.got, self.acc, self.recv, self.full = refs
        self.n = self.acc.shape[0]
        self.parts, first = [], 0
        for rows, stages in cuts:
            self.parts.append(Part(ctx, self, first, rows, stages))
            first += rows

    def send_core(self):
        self.core_copy = self.ctx.links.copy(self.give, self.got, self.ctx.twin)

    def merge_core(self):
        self.core_copy.wait_recv()
        for part in self.parts:
            rows = slice(part.first, part.first + part.rows)
            self.acc[rows, :] = (self.acc[rows, :].astype(F32) + self.got[rows, :].astype(F32)).astype(BF)
            part.begin()


class Ctx:
    pass


def share_rows(ctx, slots, count):
    mine = slots.at[ctx.row]
    send, recv = ctx.links.send_sem(), ctx.links.recv_sem()
    for k in range(1, count):
        ctx.links.start(mine, mine, (lax.rem(ctx.row + k, count), ctx.head), send, recv)
    others = slots.at[pl.ds(0, count - 1)]
    ctx.links.open.append(functools.partial(wait_bytes, others, send))
    return functools.partial(wait_bytes, others, recv)


SMALL = [
    "mask", "pidx", "encw", "encb", "outb", "ag", "ash", "downb", "fg", "fsh",
]
IN_NAMES = [
    "feats", "mask", "splits", "pidx", "bank", "encw", "encb", "qkvw", "outw", "outb", "ag", "ash", "upw",
    "upb", "downw", "downb", "fg", "fsh", "cot",
]
OUT_NAMES = [
    "output", "uf", "rffn", "rqkv", "rbank", "vec", "late", "stat",
]
CUTS = {
    "d": [(1536, [(1, 2), (4, 8)]), (512, [(2,), (1,), (4,), (8,)])],
    "u": [(1024, [(4,), (1, 2), (8,)]), (1024, [(1, 2), (4, 8)])],
    "o": [(1024, [(2,), (8,), (1, 4)])],
    "q": [(768, [(1,), (2,), (4,), (8,)]), (768, [(4,), (1,), (2,), (8,)])],
    "r": [(512, [(1,), (2, 4), (8,)]), (768, [(1,), (2,), (4, 8)]), (256, [(1,), (2, 4), (8,)])],
    "l": [(512, [(2, 4), (1,), (8,)]), (512, [(4,), (1, 2), (8,)]), (256, [(1, 2), (4, 8)])],
}
PLAN = [
    [],
    [],
    [],
    [],
    [],
    [],
    [],
    [],
    [],
    [],
    [],
    ["d0"],
    [],
    ["d1"],
    ["u0"],
    [],
    ["u1", "d0"],
    ["q0", "q1", "d1"],
    ["o0"],
    [],
    ["u1", "u0", "q0", "q1", "d1", "d0", "r0", "l0", "l1", "q1", "r1", "r2", "o0", "l2", "u1", "u0", "q0", "d1", "q1", "r0", "l2", "d0", "u0", "l0", "q0", "d1", "r1", "l1", "q1", "r2", "r0", "o0", "l2", "l0", "d1", "q0", "u1", "r1", "l1", "r2", "r0", "l0", "u0", "q1", "q0", "o0", "l2", "r1", "d1", "l1", "l0", "r2", "r0", "q1", "q0", "r1", "u0", "d1", "r0", "o0", "l1", "l0", "q0", "r2", "q1", "r1", "o0", "r2", "l1"],
]


def layer_kernel(count, total_rows, cuts, plan, sem_counts, names, *refs):
    g = Ctx()
    for name, ref in zip(names, refs, strict=True):
        setattr(g, name, ref)
    features, n = g.feats.shape
    ctx = Ctx()
    ctx.row, ctx.head = lax.axis_index("rows"), lax.axis_index("heads")
    h = ctx.head
    o = 1 - h
    ctx.twin = (ctx.row, o)
    ctx.links = links = Links(g.ssem, g.rsem)
    loads = Loads(g.lsem)

    l_feats = loads.copy(g.feats, g.F.at[h])
    own = {
        "qkv": (g.qkvw, g.WQKV.at[h]),
        "out": (g.outw, g.WO.at[h]),
        "upb": (g.upb, g.UB.at[h]),
        "up": (g.upw, g.WU.at[h]),
        "down": (g.downw, g.WD.at[h]),
    }
    g.TILE[...] = jnp.zeros_like(g.TILE)
    barrier = pltpu.get_barrier_semaphore()
    pl.semaphore_signal(barrier, inc=1, device_id=ctx.twin, device_id_type=MESH)
    for k in range(1, count):
        pl.semaphore_signal(
            barrier, inc=1, device_id=(lax.rem(ctx.row + k, count), h), device_id_type=MESH
        )
    l_small = [loads.copy(getattr(g, k), getattr(g, k + "_")) for k in SMALL]
    l_bank = loads.copy(g.bank, g.BANKV)
    l_own = {k: loads.copy(*v) for k, v in own.items()}
    l_cot = loads.copy(g.cot, g.COT)

    def to_rows(columns):
        for i, c in enumerate(columns):
            g.SQUARE[0:features, i : i + 1] = c
        return g.SQUARE[...].T[0:8, :]

    def lane_sum(v):
        return jnp.sum(v, axis=-1, keepdims=True)

    g.SQUARE[...] = jnp.zeros_like(g.SQUARE)
    l_feats.wait()
    f = g.F[h]
    g.TILE[0] = to_rows([lane_sum(f), lane_sum(f * f)])
    pl.semaphore_wait(barrier, count)
    c_tile = links.copy(g.TILE.at[0], g.TILE.at[1], ctx.twin)
    c_feats = links.copy(g.feats, g.F.at[h], ctx.twin)
    c_tile.wait_recv()
    g.MOM[ctx.row] = g.TILE[0] + g.TILE[1]
    wait_moments = share_rows(ctx, g.MOM, count)
    c_own = {k: links.copy(*v, ctx.twin) for k, v in own.items()}

    for c in l_small:
        c.wait()
    selector = lax.broadcasted_iota(jnp.int32, (g.bank.shape[0], P_SIZE), 0) == g.pidx_[...]
    g.SEL[...] = jnp.where(selector, 1.0, 0.0).astype(BF)
    l_bank.wait()
    g.SRC[CONTEXT_MAX:KEYS, :] = tn(g.SEL[...], g.BANKV[...]).astype(BF)
    maybe = lax.broadcasted_iota(jnp.int32, (CONTEXT_MAX - CONTEXT_MIN, 1), 0) + CONTEXT_MIN
    g.BIAS[...] = jnp.where(maybe < g.splits[0], 0.0, -1e30)
    g.VEC[...] = jnp.zeros_like(g.VEC)
    g.LATE[0] = jnp.zeros_like(g.LATE[0])
    live = g.mask_[...].astype(F32)
    scale = live * jnp.sqrt(features / jnp.sum(live, axis=-1, keepdims=True))
    g.STAT[...] = jnp.zeros_like(g.STAT)
    g.STAT[2:3, 0:features] = scale
    for c in l_own.values():
        c.wait()
    c_own["qkv"].wait_recv()
    for j in range(4):
        s, w = j // 2, pl.ds(128 * (j % 2), 128)
        g.WKV[j, :, 0:128] = g.WQKV[s, 1, :, w]
        g.WKV[j, :, 128:256] = g.WQKV[s, 2, :, w]

    c_feats.wait_recv()
    wait_moments()
    moments = g.MOM[0]
    for k in range(1, count):
        moments = moments + g.MOM[k]
    mean = moments[0:1, :] / total_rows
    var = moments[1:2, :] / total_rows - mean * mean
    g.STAT[0:1, :] = mean
    g.STAT[1:2, :] = lax.rsqrt(var + EPS)
    g.SQUARE[0:8, :] = g.STAT[...]
    columns = g.SQUARE[...].T
    mean, inverse, scale = [columns[0:features, i : i + 1] for i in range(3)]
    g.COLS[...] = columns[0:features, :]

    for s in range(2):
        g.NL[s] = (((g.F[s] - mean) * inverse) * scale).astype(BF)
        hidden = tn(g.NL[s], g.encw_[...]) + g.encb_[...]
        g.HA[s] = hidden
        g.HB[s] = hidden.astype(BF)
    g.SRC[0:n, :] = g.HB[0]
    g.SRC[n:CONTEXT_MAX, :] = g.HB[1, 0 : CONTEXT_MAX - n, :]

    for s in range(2):
        q = (nn(g.HB[h], g.WQKV[s, 0]) * Q_SCALE).astype(BF)
        for j in range(2):
            g.Q[2 * s + j] = q[:, 128 * j : 128 * j + 128]

    for j in range(4):
        kv = nn(g.SRC[...], g.WKV[j]).astype(BF)
        g.K[j] = kv[:, 0:128]
        g.V[j] = kv[:, 128:256]

    for j in range(5):
        if j < 4:
            scores = nt(g.K[j], g.Q[j])
            g.S[j % 2, 0:CONTEXT_MIN, :] = scores[0:CONTEXT_MIN]
            g.S[j % 2, CONTEXT_MIN:CONTEXT_MAX, :] = scores[CONTEXT_MIN:CONTEXT_MAX] + g.BIAS[...]
            g.S[j % 2, CONTEXT_MAX:KEYS, :] = scores[CONTEXT_MAX:KEYS]
        if j > 0:
            p = j - 1
            scores = g.S[p % 2]
            e = jnp.exp2(scores - jnp.max(scores, axis=0, keepdims=True))
            inv = 1.0 / row_sum(e)
            g.INV[p, 0:1, :] = inv
            e = e.astype(BF)
            g.E[p] = e
            g.AT[p] = (tn(g.V[p], e) * inv).astype(BF)

    c_own["out"].wait_recv()
    c_own["up"].wait_recv()
    c_own["upb"].wait_recv()
    c_own["down"].wait_recv()
    for j in range(4):
        g.A[:, 128 * j : 128 * j + 128] = g.AT[j].T
    l_cot.wait()

    branch = nn(g.A[:, 0:256], g.WO[0]) + nn(g.A[:, 256:512], g.WO[1]) + g.outb_[...]
    joined = g.HA[h] + branch
    center = joined - lane_mean(joined)
    rstd = lax.rsqrt(lane_mean(center * center) + EPS)
    xhat = center * rstd
    after = xhat * g.ag_[...] + g.ash_[...]
    g.XH[...] = xhat
    g.RS[...] = rstd
    low = after.astype(BF)
    g.AB[...] = low
    mixed = g.downb_[...]
    for s in range(2):
        u = nn(low, g.WU[s]) + g.UB[s]
        phi = 0.5 * (1.0 + lax.erf(u * HALF_ROOT))
        g.DG[s] = phi + u * (jnp.exp2(u * u * (-0.5 * LOG2E)) * PDF_SCALE)
        act = (u * phi).astype(BF)
        g.ACT[s] = act
        mixed = mixed + nn(act, g.WD[s])
    joined = after + mixed
    center = joined - lane_mean(joined)
    rstd = lax.rsqrt(lane_mean(center * center) + EPS)
    xhat = center * rstd
    g.output[...] = xhat * g.fg_[...] + g.fsh_[...]
    ct = g.COT[...]
    d = ct * g.fg_[...]
    d = rstd * (d - lane_mean(d) - xhat * lane_mean(d * xhat))
    g.DJ[...] = d
    gm = d.astype(BF)
    g.GM[...] = gm
    g.VEC[4:5, :] = row_sum(gm.astype(F32))
    g.VEC[5:6, :] = row_sum(ct * xhat)
    g.VEC[6:7, :] = row_sum(ct)

    def put(ref, first, value):
        r = value.shape[0]
        for b in range(value.shape[1] // 128):
            ref[first + r * b : first + r * b + r, :] = value[:, 128 * b : 128 * b + 128]

    rows_of = {k: sum(r for r, _ in v) for k, v in cuts.items()}
    fulls, at = {"l": g.rbank.at[h]}, 0
    for k in ("d", "u", "o"):
        fulls[k] = g.rffn.at[pl.ds(at, rows_of[k])]
        at += rows_of[k]
    for i, k in enumerate(("q", "r")):
        fulls[k] = g.rqkv.at[i]
    blocks = {
        k: Block(ctx, [getattr(g, p + k) for p in ("CG", "CR", "CA", "CV")] + [fulls[k]], v)
        for k, v in cuts.items()
    }
    down, up, out, qkv0, qkv1, last = blocks.values()

    def tick(i):
        for k in plan[i] if i < len(plan) else []:
            blocks[k[0]].parts[int(k[1])].advance()

    put(down.give, 0, tn(g.ACT[o], g.GM[...]).astype(BF))
    down.send_core()
    put(down.acc, 0, tn(g.ACT[h], g.GM[...]).astype(BF))

    tile = n // 2

    def backward(t):
        rows = slice(t * tile, t * tile + tile)
        gm = g.GM[rows, :]
        d = g.DJ[rows, :]
        for s in range(2):
            du = (g.DG[s, rows, :] * nt(gm, g.WD[s])).astype(BF)
            g.DU[s, rows, :] = du
            g.VEC[7 + s : 8 + s, :] += row_sum(du.astype(F32))
            d = d + nt(du, g.WU[s])
        xhat = g.XH[rows, :]
        g.VEC[2:3, :] += row_sum(d * xhat)
        g.VEC[3:4, :] += row_sum(d)
        d = d * g.ag_[...]
        d = g.RS[rows, :] * (d - lane_mean(d) - xhat * lane_mean(d * xhat))
        g.DJ[rows, :] = d
        gb = d.astype(BF)
        g.GB[rows, :] = gb
        g.VEC[1:2, :] += row_sum(gb.astype(F32))

    backward(0)
    down.merge_core()
    backward(1)
    tick(4)
    put(up.give, 0, tn(g.AB[...], g.DU[o]).astype(BF))
    up.send_core()
    for j in range(2):
        put(out.give, 128 * j * 4, nn(g.AT[2 * o + j], g.GB[...]).astype(BF))
    out.send_core()
    c_vec = links.copy(g.VEC, g.VECR, ctx.twin)
    put(up.acc, 0, tn(g.AB[...], g.DU[h]).astype(BF))
    for j in range(2):
        put(out.acc, 128 * j * 4, nn(g.AT[2 * h + j], g.GB[...]).astype(BF))
    tick(5)

    for j in range(4):
        d = nt(g.WO[j // 2, 128 * (j % 2) : 128 * (j % 2) + 128, :], g.GB[...]).astype(BF)
        g.DOT[j] = d
        df = d.astype(F32)
        g.INNER[j, 0:1, :] = row_sum(df * g.AT[j].astype(F32))
        g.DOT2[j] = (df * g.INV[j, 0:1, :]).astype(BF)
    tick(6)
    up.merge_core()
    out.merge_core()
    tick(7)

    vec_stages = vec_groups(count)
    vec = Ctx()
    vec.k = 0

    def vec_start(value):
        bits = vec_stages[vec.k]
        digit, _ = down.parts[0]._digits(bits, 0)
        slots = g.VECS.at[vec.k]
        slots[digit] = value
        send, vec.sem = links.send_sem(), links.recv_sem()
        others = slots.at[pl.ds(0, 2 ** len(bits) - 1)]
        for mask in range(1, 2 ** len(bits)):
            _, row = down.parts[0]._digits(bits, mask)
            links.start(slots.at[digit], slots.at[digit], (row, h), send, vec.sem)
        links.open.append(functools.partial(wait_bytes, others, send))

    def vec_end():
        ways = 2 ** len(vec_stages[vec.k])
        wait_bytes(g.VECS.at[vec.k, pl.ds(0, ways - 1)], vec.sem)
        value = g.VECS[vec.k, 0]
        for i in range(1, ways):
            value = value + g.VECS[vec.k, i]
        vec.k += 1
        if vec.k < len(vec_stages):
            vec_start(value)
        else:
            g.vec[...] = value

    kv_copies = {}

    def attend_back(j):
        q, dot, dot2 = g.Q[j], g.DOT[j], g.DOT2[j]
        inner, factor = g.INNER[j, 0:1, :], g.INV[j, 0:1, :]
        dq = None
        for t in range(KEYS // 256):
            rows = slice(256 * t, 256 * t + 256)
            e = g.E[j, rows, :]
            upstream = nn(g.V[j, rows, :], dot)
            ds = (e.astype(F32) * ((upstream - inner) * factor)).astype(BF)
            g.DKV[j, rows, 0:128] = (nn(ds, q) * (DH**-0.5 / Q_SCALE)).astype(BF)
            g.DKV[j, rows, 128:256] = nt(e, dot2).astype(BF)
            part = tn(g.K[j, rows, :], ds)
            dq = part if dq is None else dq + part
        g.DQT[j] = (dq * DH**-0.5).astype(BF)
        other = pl.ds(pl.multiple_of(o * n, n), n)
        kv_copies[j] = links.copy(g.DKV.at[j, other], g.DKVR.at[j], ctx.twin)

    def merge_kv(j):
        kv_copies[j].wait_recv()
        mine = pl.ds(pl.multiple_of(h * n, n), n)
        g.DKVO[j] = (g.DKV[j, mine, :].astype(F32) + g.DKVR[j].astype(F32)).astype(BF)

    def q_grads(p, block):
        for j, ref in ((2 * o + p, block.give), (2 * h + p, block.acc)):
            put(ref, 0, nt(g.HQT[...], g.DQT[j]).astype(BF))

    def kv_grads(p, block):
        put(block.give, n, nn(g.SRCT[...], g.DKVO[2 * o + p]).astype(BF))
        block.send_core()
        put(block.acc, n, nn(g.SRCT[...], g.DKVO[2 * h + p]).astype(BF))

    g.HQT[...] = g.HB[h].T
    g.SRCT[...] = g.SRC[pl.ds(pl.multiple_of(h * n, n), n), :].T
    attend_back(0)
    tick(8)
    attend_back(2)
    tick(9)
    q_grads(0, qkv0)
    attend_back(1)
    tick(10)
    merge_kv(0)
    merge_kv(2)
    kv_grads(0, qkv0)
    tick(11)
    attend_back(3)
    tick(12)
    qkv0.merge_core()
    c_vec.wait_recv()
    vec_start(g.VEC[...] + g.VECR[...])
    tick(13)
    q_grads(1, qkv1)
    for j in range(4):
        g.DQ[:, 128 * j : 128 * j + 128] = g.DQT[j].T
    dh = g.DJ[...] + nt(g.DQ[:, 0:256], g.WQKV[0, 0]) + nt(g.DQ[:, 256:512], g.WQKV[1, 0])
    tick(14)

    merge_kv(1)
    merge_kv(3)
    kvh = nt(g.DKVO[0], g.WKV[0])
    for j in range(1, 4):
        kvh = kvh + nt(g.DKVO[j], g.WKV[j])
    edge = CONTEXT_MAX - n
    g.DP[0] = kvh[edge:n, :].astype(BF)
    c_prompt = links.copy(g.DP.at[0], g.DP.at[1], ctx.twin)
    g.GH[0:edge, :] = (dh[0:edge] + kvh[0:edge]).astype(BF)
    first = jnp.where(h == 0, 1.0, 0.0)
    g.GH[edge:n, :] = (dh[edge:n] + kvh[edge:n] * first).astype(BF)
    tick(15)
    kv_grads(1, qkv1)
    tick(16)
    gh = g.GH[...]
    g.ENC[0:features, :] = nn(g.NL[h], gh)
    g.ENC[features:, :] = jnp.zeros_like(g.ENC[features:, :])
    bank_rows = g.bank.shape[0] // 2
    enc_at = bank_rows * 4
    for b in range(4):
        cols = slice(128 * b, 128 * b + 128)
        last.give[64 * b : 64 * b + 64, :] = g.ENC[pl.ds(pl.multiple_of(o * 64, 64), 64), cols].astype(BF)
        last.acc[enc_at + 64 * b : enc_at + 64 * b + 64, :] = g.ENC[
            pl.ds(pl.multiple_of(h * 64, 64), 64), cols
        ].astype(BF)
    last.send_core()
    c_prompt.wait_recv()
    put(
        last.acc,
        0,
        nn(g.SEL[pl.ds(pl.multiple_of(h * bank_rows, bank_rows), bank_rows), :], g.DP[o]).astype(BF),
    )
    tick(17)
    qkv1.merge_core()
    last.core_copy.wait_recv()
    rows = slice(enc_at, enc_at + 256)
    last.acc[rows, :] = (last.acc[rows, :].astype(F32) + last.got[...].astype(F32)).astype(BF)
    if last.n > enc_at + 256:
        last.acc[enc_at + 256 :, :] = jnp.zeros_like(last.acc[enc_at + 256 :, :])
    for part in last.parts:
        part.begin()
    tick(18)
    vec_end()

    scale = g.COLS[:, 2:3]
    uf = nt(g.encw_[...], gh) * scale
    g.uf[...] = uf
    g.SQUARE[...] = jnp.zeros_like(g.SQUARE)
    g.LATE[0] = to_rows([lane_sum(uf), lane_sum(uf * (g.F[h] - g.COLS[:, 0:1]))])
    eb = row_sum(gh.astype(F32))
    for b in range(4):
        g.LATE[0, 2 + b : 3 + b, :] = eb[:, 128 * b : 128 * b + 128]
    c_late = links.copy(g.LATE.at[0], g.LATE.at[1], ctx.twin)
    tick(19)
    c_late.wait_recv()
    g.LSUM[ctx.row] = g.LATE[0] + g.LATE[1]
    wait_late = share_rows(ctx, g.LSUM, count)
    tick(20)
    rest = [p for b in blocks.values() for p in b.parts]
    while not all(p.done() for p in rest):
        for p in rest:
            if not p.done():
                p.advance()
    while vec.k < len(vec_stages):
        vec_end()
    c_last = links.copy(g.rbank.at[h], g.rbank.at[h], ctx.twin)
    wait_late()
    late = g.LSUM[0]
    for k in range(1, count):
        late = late + g.LSUM[k]
    g.late[...] = late
    g.stat[...] = g.STAT[...]
    c_last.wait_recv()
    links.drain()
    assert (links.sent, links.received, loads.used) == sem_counts, (links.sent, links.received, loads.used)


def vec_groups(count):
    bits = [2**i for i in range(count.bit_length() - 1)]
    return [tuple(bits[i : i + 2]) for i in range(0, len(bits), 2)]


def finish_kernel(total_rows, names, *refs):
    g = Ctx()
    for name, ref in zip(names, refs, strict=True):
        setattr(g, name, ref)
    h = lax.axis_index("heads")
    features = g.feats.shape[0]
    copies = []

    def copy(src, dst):
        c = pltpu.make_async_copy(src, dst, g.sems.at[len(copies)])
        c.start()
        copies.append(c)
        return c

    outs = [copy(g.output, g.o_output)]
    c_feats = copy(g.feats, g.FEATS)
    up_at = g.rffn.shape[0] // 5 * 2

    def block(ref, first, rows):
        return ref[first : first + rows, :].astype(F32)

    for b in range(4):
        cols = slice(128 * b, 128 * b + 128)
        g.DOWN[:, cols] = block(g.rffn, 512 * b, 512)
    outs.append(copy(g.DOWN, g.o_down))
    for b in range(4):
        cols = slice(128 * b, 128 * b + 128)
        g.UP[:, cols] = block(g.rffn, up_at + 512 * b, 512)
    outs.append(copy(g.UP, g.o_up))
    for b in range(4):
        cols = slice(128 * b, 128 * b + 128)
        for j in range(2):
            g.OUT[128 * j : 128 * j + 128, cols] = block(g.rffn, 2 * up_at + 512 * j + 128 * b, 128)
    outs.append(copy(g.OUT, g.o_out))
    for c in range(3):
        for p in range(2):
            g.QKV[c, :, 128 * p : 128 * p + 128] = g.rqkv[p, 512 * c : 512 * c + 512, :].astype(F32)
    outs.append(copy(g.QKV, g.o_qkv))
    for b in range(4):
        cols = slice(128 * b, 128 * b + 128)
        for s in range(2):
            g.BANKV[256 * s : 256 * s + 256, cols] = g.rbank[s, 256 * b : 256 * b + 256, :].astype(F32)
        g.o_encw[0:64, cols] = g.rbank[0, 1024 + 64 * b : 1024 + 64 * b + 64, :].astype(F32)
        g.o_encw[64:features, cols] = g.rbank[1, 1024 + 64 * b : 1024 + 64 * b + features - 64, :].astype(F32)
        g.o_encb[:, cols] = g.late[2 + b : 3 + b, :]
    outs.append(copy(g.BANKV, g.o_bank))
    g.o_outb[...] = g.vec[1:2, :]
    g.o_ag[...] = g.vec[2:3, :]
    g.o_ash[...] = g.vec[3:4, :]
    g.o_downb[...] = g.vec[4:5, :]
    g.o_fg[...] = g.vec[5:6, :]
    g.o_fsh[...] = g.vec[6:7, :]
    g.o_upb[...] = g.vec[pl.ds(7 + h, 1), :]
    mean, inverse = g.stat[0:1, :], g.stat[1:2, :]
    b1, b2 = g.late[0:1, :], g.late[1:2, :]
    var_grad = -0.5 * inverse * inverse * inverse * b2
    g.SQUARE[...] = jnp.zeros_like(g.SQUARE)
    g.SQUARE[0:1, :] = inverse
    g.SQUARE[1:2, :] = (-inverse * b1 - 2.0 * mean * var_grad) / total_rows
    g.SQUARE[2:3, :] = 2.0 * var_grad / total_rows
    columns = g.SQUARE[...].T
    inverse, first, slope = [columns[0:features, i : i + 1] for i in range(3)]
    c_feats.wait()
    g.o_feats[...] = g.uf[...] * inverse + first + g.FEATS[...] * slope
    for c in outs:
        c.wait()


def per_device(
    feats,
    feature_mask,
    splits,
    prompt_index,
    prompt_bank,
    enc_weight,
    enc_bias,
    qkv_weight,
    out_weight,
    out_bias,
    attn_gain,
    attn_shift,
    up_weight,
    up_bias,
    down_weight,
    down_bias,
    ffn_gain,
    ffn_shift,
    cotangent,
):
    n, features = feats.shape
    count = lax.axis_size("rows")
    total_rows = n * count * lax.axis_size("heads")
    d = prompt_bank.shape[1]
    columns = feats.T
    args = [
        columns, feature_mask, splits, prompt_index, prompt_bank, enc_weight, enc_bias[None], qkv_weight, out_weight,
        out_bias[None], attn_gain[None], attn_shift[None], up_weight, up_bias[None], down_weight, down_bias[None],
        ffn_gain[None], ffn_shift[None], cotangent,
    ]
    vmem = pl.BlockSpec(memory_space=pltpu.VMEM)
    hbm = pl.BlockSpec(memory_space=pl.ANY)
    in_specs = [pl.BlockSpec(memory_space=pltpu.SMEM) if k == "splits" else hbm for k in IN_NAMES]
    bits = [2**i for i in range(count.bit_length() - 1)]
    grain = 16 * count
    block_rows = {"d": 2048, "u": 2048, "o": 1024, "q": 1536, "r": 1536, "l": 1280}
    if count == 16:
        cuts, plan = CUTS, PLAN
    else:
        cuts, plan = {k: [(-(-r // grain) * grain, vec_groups(count))] for k, r in block_rows.items()}, []
    block_rows = {k: sum(r for r, _ in v) for k, v in cuts.items()}
    S = jax.ShapeDtypeStruct
    outs = {
        "output": S((n, d), F32),
        "uf": S((features, n), F32),
        "rffn": S((block_rows["d"] + block_rows["u"] + block_rows["o"], 128), BF),
        "rqkv": S((2, block_rows["q"], 128), BF),
        "rbank": S((2, block_rows["l"], 128), BF),
        "vec": S((16, d), F32),
        "late": S((8, 128), F32),
        "stat": S((8, 128), F32),
    }
    V = pltpu.VMEM
    scratch = {k + "_": V(args[IN_NAMES.index(k)].shape, args[IN_NAMES.index(k)].dtype) for k in SMALL}
    scratch |= {
        "F": V((2, features, n), F32),
        "WQKV": V((2, 3, d, 256), BF),
        "WO": V((2, 256, d), BF),
        "UB": V((2, 1, 512), F32),
        "WU": V((2, d, 512), BF),
        "WD": V((2, 512, d), BF),
        "BANKV": V(prompt_bank.shape, BF),
        "COT": V((n, d), F32),
        "SQUARE": V((128, 128), F32),
        "COLS": V((features, 128), F32),
        "TILE": V((2, 8, 128), F32),
        "LATE": V((2, 8, 128), F32),
        "MOM": V((count, 8, 128), F32),
        "LSUM": V((count, 8, 128), F32),
        "STAT": V((8, 128), F32),
        "VEC": V((16, d), F32),
        "VECR": V((16, d), F32),
        "VECS": V((len(vec_groups(count)), 4, 16, d), F32),
        "SEL": V((prompt_bank.shape[0], P_SIZE), BF),
        "SRC": V((KEYS, d), BF),
        "BIAS": V((CONTEXT_MAX - CONTEXT_MIN, 1), F32),
        "S": V((2, KEYS, n), F32),
        "WKV": V((4, d, 256), BF),
        "NL": V((2, features, n), BF),
        "HA": V((2, n, d), F32),
        "HB": V((2, n, d), BF),
        "Q": V((4, n, 128), BF),
        "K": V((4, KEYS, 128), BF),
        "V": V((4, KEYS, 128), BF),
        "E": V((4, KEYS, n), BF),
        "INV": V((4, 8, n), F32),
        "INNER": V((4, 8, n), F32),
        "AT": V((4, 128, n), BF),
        "A": V((n, d), BF),
        "XH": V((n, d), F32),
        "RS": V((n, 1), F32),
        "AB": V((n, d), BF),
        "DG": V((2, n, 512), F32),
        "ACT": V((2, n, 512), BF),
        "DU": V((2, n, 512), BF),
        "DJ": V((n, d), F32),
        "GM": V((n, d), BF),
        "GB": V((n, d), BF),
        "DOT": V((4, 128, n), BF),
        "DOT2": V((4, 128, n), BF),
        "DKV": V((4, KEYS, 256), BF),
        "DKVR": V((4, n, 256), BF),
        "DKVO": V((4, n, 256), BF),
        "DQT": V((4, 128, n), BF),
        "DQ": V((n, d), BF),
        "HQT": V((d, n), BF),
        "SRCT": V((d, n), BF),
        "DP": V((2, P_SIZE, d), BF),
        "GH": V((n, d), BF),
        "ENC": V((128, d), F32),
    }
    for k, r in block_rows.items():
        small = 256 if k == "l" else r
        scratch["CG" + k] = V((small, 128), BF)
        scratch["CR" + k] = V((small, 128), BF)
        scratch["CA" + k] = V((r, 128), BF)
        scratch["CV" + k] = V((r, 128), BF)
    parts = [stages for v in cuts.values() for _, stages in v]
    once = 23 + len(vec_groups(count))
    sem_counts = (once + len(parts), once + sum(2 * len(s) for s in parts), 8 + len(SMALL))
    for k, v in zip(("ssem", "rsem", "lsem"), sem_counts, strict=True):
        scratch[k] = pltpu.SemaphoreType.DMA((v,))
    names = IN_NAMES + OUT_NAMES + list(scratch)
    results = pl.pallas_call(
        functools.partial(layer_kernel, count, total_rows, cuts, plan, sem_counts, names),
        out_shape=[pltpu.VMEM(outs[k].shape, outs[k].dtype) for k in OUT_NAMES],
        in_specs=in_specs,
        out_specs=[vmem] * len(OUT_NAMES),
        scratch_shapes=list(scratch.values()),
        compiler_params=pltpu.CompilerParams(
            collective_id=0, has_side_effects=True, vmem_limit_bytes=VMEM_LIMIT
        ),
        name="layer",
    )(*args)
    finals = {
        "o_output": S((n, d), F32),
        "o_feats": S((features, n), F32),
        "o_bank": S(prompt_bank.shape, F32),
        "o_encw": S(enc_weight.shape, F32),
        "o_encb": S((1, d), F32),
        "o_qkv": S(qkv_weight.shape, F32),
        "o_out": S(out_weight.shape, F32),
        "o_outb": S((1, d), F32),
        "o_ag": S((1, d), F32),
        "o_ash": S((1, d), F32),
        "o_up": S(up_weight.shape, F32),
        "o_upb": S((1, up_bias.shape[0]), F32),
        "o_down": S(down_weight.shape, F32),
        "o_downb": S((1, d), F32),
        "o_fg": S((1, d), F32),
        "o_fsh": S((1, d), F32),
    }
    moved = {"o_output", "o_bank", "o_qkv", "o_out", "o_up", "o_down"}
    work = {
        "FEATS": V((features, n), F32),
        "DOWN": V(down_weight.shape, F32),
        "UP": V(up_weight.shape, F32),
        "OUT": V(out_weight.shape, F32),
        "QKV": V(qkv_weight.shape, F32),
        "BANKV": V(prompt_bank.shape, F32),
        "SQUARE": V((128, 128), F32),
        "sems": pltpu.SemaphoreType.DMA((7,)),
    }
    final = pl.pallas_call(
        functools.partial(finish_kernel, total_rows, ["feats"] + OUT_NAMES + list(finals) + list(work)),
        out_shape=list(finals.values()),
        in_specs=[hbm] + [vmem] * len(OUT_NAMES),
        out_specs=[hbm if k in moved else vmem for k in finals],
        scratch_shapes=list(work.values()),
        compiler_params=pltpu.CompilerParams(vmem_limit_bytes=VMEM_LIMIT),
        name="finish",
    )(columns, *[pltpu.with_memory_space_constraint(v, pltpu.VMEM) for v in results])
    vectors = ("o_encb", "o_outb", "o_ag", "o_ash", "o_upb", "o_downb", "o_fg", "o_fsh")
    return tuple(
        v[0] if k in vectors else v.T if k == "o_feats" else v for k, v in zip(finals, final, strict=True)
    )


def solution(mesh):
    whole = P(("rows", "heads"), None)
    placed = (
        whole, P("rows", None), P("rows"), P("rows", None), P(), P(), P(), P(None, None, "heads"), P("heads", None),
        P(), P(), P(), P(None, "heads"), P("heads"), P("heads", None), P(), P(), P(), whole,
    )
    return jax.shard_map(
        per_device,
        mesh=mesh,
        in_specs=placed,
        out_specs=(
            whole, whole, P(), P(), P(), P(None, None, "heads"), P("heads", None), P(), P(), P(), P(None, "heads"),
            P("heads"), P("heads", None), P(), P(), P(),
        ),
        check_vma=False,
    )
```

```python
import functools
import math

import jax
import jax.numpy as jnp
from jax import lax
from jax.experimental import pallas as pl
from jax.experimental.pallas import tpu as pltpu
from jax.sharding import PartitionSpec as P

BF = jnp.bfloat16
F32 = jnp.float32
MESH = pl.DeviceIdType.MESH
DH = 128
P_SIZE = 128
CONTEXT_MAX = 896
CONTEXT_MIN = 640
KEYS = CONTEXT_MAX + P_SIZE
EPS = 1e-05
HALF_ROOT = math.sqrt(0.5)
PDF_SCALE = 1.0 / math.sqrt(2.0 * math.pi)
LOG2E = math.log2(math.e)
Q_SCALE = DH**-0.5 * LOG2E
VMEM_LIMIT = 52 * 2**20


def _dot(a, b, ca, cb):
    return lax.dot_general(a, b, (((ca,), (cb,)), ((), ())), preferred_element_type=F32)


def nn(a, b):
    return _dot(a, b, 1, 0)


def nt(a, b):
    return _dot(a, b, 1, 1)


def tn(a, b):
    return _dot(a, b, 0, 0)


def row_sum(v):
    return jnp.sum(v, axis=0, keepdims=True)


def lane_mean(v):
    return jnp.mean(v, axis=-1, keepdims=True)


class Links:
    def __init__(self, send, recv):
        self.send, self.recv, self.sent, self.received, self.open = send, recv, 0, 0, []

    def send_sem(self):
        self.sent += 1
        return self.send.at[self.sent - 1]

    def recv_sem(self):
        self.received += 1
        return self.recv.at[self.received - 1]

    def start(self, src, dst, device, send, recv):
        c = pltpu.make_async_remote_copy(
            src_ref=src, dst_ref=dst, send_sem=send, recv_sem=recv, device_id=device, device_id_type=MESH
        )
        c.start()
        return c

    def copy(self, src, dst, device):
        c = self.start(src, dst, device, self.send_sem(), self.recv_sem())
        self.open.append(c.wait_send)
        return c

    def drain(self):
        for wait in self.open:
            wait()
        self.open = []


def wait_bytes(ref, sem):
    pltpu.make_async_copy(ref, ref, sem).wait()


class Loads:
    def __init__(self, sems):
        self.sems, self.used = sems, 0

    def copy(self, src, dst):
        c = pltpu.make_async_copy(src, dst, self.sems.at[self.used])
        self.used += 1
        c.start()
        return c


class Part:
    def __init__(self, ctx, block, first, rows, stages):
        self.ctx, self.first, self.rows = ctx, first, rows
        self.stages = [tuple(b for b in s if b) for s in stages]
        self.whole = len(stages[-1]) == 1 or 0 in stages[-1]
        self.acc, self.recv, self.full = block.acc, block.recv, block.full
        self.at = -1

    def begin(self):
        self.base, self.len, self.off, self.k = self.first, self.rows, 2 * self.first, 0
        self.send_sem = self.ctx.links.send_sem()
        self._start_scatter()

    def _digits(self, bits, mask):
        digit, row = 0, self.ctx.row
        for i, b in enumerate(bits):
            bit = (self.ctx.row // b) % 2
            if mask >> i & 1:
                row = row + b * (1 - 2 * bit)
                bit = 1 - bit
            digit = digit * 2 + bit
        return digit, row

    def _wait(self, rows):
        view = self.full.at[pl.ds(0, rows)]
        wait_bytes(view, self.recv_sem)
        wait_bytes(view, self.send_sem)

    def _exchanges(self):
        return self.whole and self.k == len(self.stages) - 1

    def _slot(self, digit):
        return pl.ds(pl.multiple_of(self.off + digit * self.len, 16), self.len)

    def _start_scatter(self):
        bits = self.stages[self.k]
        ways = 2 ** len(bits)
        self.recv_sem = self.ctx.links.recv_sem()
        mine, _ = self._digits(bits, 0)
        q = self.len // ways
        for mask in range(1, ways):
            digit, row = self._digits(bits, mask)
            if self._exchanges():
                src = self.acc.at[pl.ds(pl.multiple_of(self.base, 16), self.len)]
                dst = self.recv.at[self._slot(mine)]
            else:
                src = self.acc.at[pl.ds(pl.multiple_of(self.base + digit * q, 16), q)]
                dst = self.recv.at[pl.ds(self.off + (mask - 1) * q, q)]
            self.ctx.links.start(src, dst, (row, self.ctx.head), self.send_sem, self.recv_sem)

    def _end_scatter(self):
        bits = self.stages[self.k]
        ways = 2 ** len(bits)
        digit, _ = self._digits(bits, 0)
        if self._exchanges():
            mine = pl.ds(pl.multiple_of(self.base, 16), self.len)
            self.recv[self._slot(digit), :] = self.acc[mine, :]
            self._wait((ways - 1) * self.len)
            total = self.recv[self._slot(0), :].astype(F32)
            for i in range(1, ways):
                total = total + self.recv[self._slot(i), :].astype(F32)
            self.full[mine, :] = total.astype(BF)
            self._start_gather()
            return
        q = self.len // ways
        self.base = self.base + digit * q
        mine = pl.ds(pl.multiple_of(self.base, 16), q)
        self._wait((ways - 1) * q)
        total = self.acc[mine, :].astype(F32)
        for i in range(ways - 1):
            total = total + self.recv[pl.ds(self.off + i * q, q), :].astype(F32)
        self.off += (ways - 1) * q
        self.len = q
        self.k += 1
        if self.k < len(self.stages):
            self.acc[mine, :] = total.astype(BF)
            self._start_scatter()
        else:
            self.full[mine, :] = total.astype(BF)
            self._start_gather()

    def _start_gather(self):
        if self.k == 0:
            return
        bits = self.stages[self.k - 1]
        mine = self.full.at[pl.ds(pl.multiple_of(self.base, 16), self.len)]
        self.recv_sem = self.ctx.links.recv_sem()
        for mask in range(1, 2 ** len(bits)):
            _, row = self._digits(bits, mask)
            self.ctx.links.start(mine, mine, (row, self.ctx.head), self.send_sem, self.recv_sem)

    def _end_gather(self):
        bits = self.stages[self.k - 1]
        ways = 2 ** len(bits)
        self._wait((ways - 1) * self.len)
        digit, _ = self._digits(bits, 0)
        self.base = self.base - digit * self.len
        self.len = self.len * ways
        self.k -= 1
        self._start_gather()

    def steps(self):
        return 2 * len(self.stages) - self.whole

    def done(self):
        return self.at == self.steps()

    def advance(self):
        if self.at < 0:
            self.begin()
        elif self.at < len(self.stages):
            self._end_scatter()
        elif not self.done():
            self._end_gather()
        self.at += 1


class Block:
    def __init__(self, ctx, refs, cuts):
        self.ctx = ctx
        self.give, self.got, self.acc, self.recv, self.full = refs
        self.n = self.acc.shape[0]
        self.parts, first = [], 0
        for rows, stages in cuts:
            self.parts.append(Part(ctx, self, first, rows, stages))
            first += rows

    def send_core(self):
        self.core_copy = self.ctx.links.copy(self.give, self.got, self.ctx.twin)

    def merge_core(self):
        self.core_copy.wait_recv()
        for part in self.parts:
            rows = slice(part.first, part.first + part.rows)
            self.acc[rows, :] = (self.acc[rows, :].astype(F32) + self.got[rows, :].astype(F32)).astype(BF)


class Ctx:
    pass


def others_of(ctx, count):
    steps = sorted(range(1, count), key=lambda k: min(k, count - k))
    rows = [lax.rem(ctx.row + k, count) for k in steps]
    return [(row, head) for row in rows for head in (ctx.head, 1 - ctx.head)] + [ctx.twin]


def share_slots(ctx, slots, place, devices):
    mine = slots.at[place]
    send, recv = ctx.links.send_sem(), ctx.links.recv_sem()
    for device in devices:
        ctx.links.start(mine, mine, device, send, recv)
    others = slots.at[pl.ds(0, len(devices))]
    ctx.links.open.append(functools.partial(wait_bytes, others, send))
    return functools.partial(wait_bytes, others, recv)


SMALL = [
    "mask", "splits", "pidx", "encw", "encb", "outb", "ag", "ash", "downb", "fg", "fsh",
]
IN_NAMES = [
    "feats", "mask", "splits", "pidx", "bank", "encw", "encb", "qkvw", "outw", "outb", "ag", "ash", "upw",
    "upb", "downw", "downb", "fg", "fsh", "cot",
]
OUT_NAMES = [
    "output", "uf", "rffn", "rqkv", "rbank", "vec", "late", "stat",
]
CUTS = {
    "d": [(1024, [(2,), (1,), (4, 8)]), (1024, [(1, 2), (4, 8)])],
    "u": [(1024, [(1,), (4,), (2, 8)]), (1024, [(4,), (2,), (1,), (8,)])],
    "o": [(1024, [(1, 2), (8,), (4,)])],
    "q": [(256, [(2,), (1,), (4,), (8,)]), (512, [(1,), (2,), (4,), (8,)]), (768, [(4,), (1, 2), (8,)])],
    "r": [(768, [(1,), (2, 4), (8,)]), (768, [(2,), (1, 4), (8,)])],
    "l": [(768, [(4,), (1, 2), (8,)]), (512, [(1, 2), (4, 8)])],
}
PLAN = [
    [],
    [],
    ["d1", "d0"],
    [],
    [],
    ["u1", "u0", "o0"],
    [],
    ["d1"],
    [],
    ["d0", "u1", "u0"],
    ["d1"],
    ["o0", "q1", "q0", "q2"],
    ["d0", "u1", "u0"],
    ["d1", "q0", "q1"],
    ["o0"],
    ["u1", "q2", "d0"],
    ["u0", "r0", "l0", "r1", "l1", "o0"],
    [],
    ["d1", "q0", "q1", "u1", "q2", "d0", "r0", "u0", "l0", "r1", "q0", "o0", "q1", "u1", "l1", "q2", "d0", "r0", "l0", "u0", "r1", "q0", "q1", "l1", "r0", "l0", "o0", "u1", "q0", "q1", "r1", "q2", "l1", "u0", "d0", "q0", "r0", "u1", "l0", "r1", "q1", "l1", "q2", "q0", "r0", "l0", "q1", "r1"],
]


def layer_kernel(count, total_rows, cuts, plan, sem_counts, names, *refs):
    g = Ctx()
    for name, ref in zip(names, refs, strict=True):
        setattr(g, name, ref)
    features, n = g.feats.shape
    ctx = Ctx()
    ctx.row, ctx.head = lax.axis_index("rows"), lax.axis_index("heads")
    h = ctx.head
    o = 1 - h
    ctx.twin = (ctx.row, o)
    ctx.links = links = Links(g.ssem, g.rsem)
    loads = Loads(g.lsem)

    l_feats = loads.copy(g.feats, g.F.at[h])
    own = {
        "qkv": (g.qkvw, g.WQKV.at[h]),
        "out": (g.outw, g.WO.at[h]),
        "upb": (g.upb, g.UB.at[h]),
        "up": (g.upw, g.WU.at[h]),
        "down": (g.downw, g.WD.at[h]),
    }
    everyone = others_of(ctx, count)
    barrier = pltpu.get_barrier_semaphore()
    for device in everyone:
        pl.semaphore_signal(barrier, inc=1, device_id=device, device_id_type=MESH)
    l_small = [loads.copy(getattr(g, k), getattr(g, k + "_")) for k in SMALL]
    l_bank = loads.copy(g.bank, g.BANKV)
    l_own = {k: loads.copy(*v) for k, v in own.items()}
    l_cot = loads.copy(g.cot, g.COT)

    def to_rows(columns):
        for i, c in enumerate(columns):
            g.SQUARE[0:features, i : i + 1] = c
        return g.SQUARE[...].T[0:8, :]

    def lane_sum(v):
        return jnp.sum(v, axis=-1, keepdims=True)

    g.SQUARE[...] = jnp.zeros_like(g.SQUARE)
    l_feats.wait()
    f = g.F[h]
    rows = to_rows([lane_sum(f), lane_sum(f * f)])
    place = ctx.row * 2 + h
    g.MOM[place, :, 0:128] = rows[0:1]
    g.MOM[place, :, 128:256] = rows[1:2]
    pl.semaphore_wait(barrier, len(everyone))
    wait_moments = share_slots(ctx, g.MOM, place, everyone)
    c_feats = links.copy(g.feats, g.F.at[h], ctx.twin)
    c_own = {"qkv": links.copy(*own["qkv"], ctx.twin)}
    c_own |= {k: links.copy(*v, ctx.twin) for k, v in own.items() if k != "qkv"}

    for c in l_small:
        c.wait()
    selector = lax.broadcasted_iota(jnp.int32, (g.bank.shape[0], P_SIZE), 0) == g.pidx_[...]
    g.SEL[...] = jnp.where(selector, 1.0, 0.0).astype(BF)
    l_bank.wait()
    g.SRC[CONTEXT_MAX:KEYS, :] = tn(g.SEL[...], g.BANKV[...]).astype(BF)
    maybe = lax.broadcasted_iota(jnp.int32, (CONTEXT_MAX - CONTEXT_MIN, 1), 0) + CONTEXT_MIN
    g.BIAS[...] = jnp.where(maybe < g.splits_[0], 0.0, -1e30)
    g.VEC[...] = jnp.zeros_like(g.VEC)
    g.LATE[0] = jnp.zeros_like(g.LATE[0])
    live = g.mask_[...].astype(F32)
    scale = live * jnp.sqrt(features / jnp.sum(live, axis=-1, keepdims=True))
    g.STAT[...] = jnp.zeros_like(g.STAT)
    g.STAT[2:3, 0:features] = scale
    for c in l_own.values():
        c.wait()
    c_own["qkv"].wait_recv()
    for j in range(4):
        s, w = j // 2, pl.ds(128 * (j % 2), 128)
        g.WKV[j, :, 0:128] = g.WQKV[s, 1, :, w]
        g.WKV[j, :, 128:256] = g.WQKV[s, 2, :, w]

    c_feats.wait_recv()
    wait_moments()
    moments = g.MOM[0]
    for k in range(1, 2 * count):
        moments = moments + g.MOM[k]
    mean = moments[:, 0:128] / total_rows
    var = moments[:, 128:256] / total_rows - mean * mean
    g.STAT[0:1, :] = mean
    g.STAT[1:2, :] = lax.rsqrt(var + EPS)
    g.SQUARE[0:8, :] = g.STAT[...]
    columns = g.SQUARE[...].T
    mean, inverse, scale = [columns[0:features, i : i + 1] for i in range(3)]
    g.COLS[...] = columns[0:features, :]

    for s in range(2):
        g.NL[s] = (((g.F[s] - mean) * inverse) * scale).astype(BF)
        hidden = tn(g.NL[s], g.encw_[...]) + g.encb_[...]
        g.HA[s] = hidden
        g.HB[s] = hidden.astype(BF)
    g.SRC[0:n, :] = g.HB[0]
    g.SRC[n:CONTEXT_MAX, :] = g.HB[1, 0 : CONTEXT_MAX - n, :]

    for s in range(2):
        q = (nn(g.HB[h], g.WQKV[s, 0]) * Q_SCALE).astype(BF)
        for j in range(2):
            g.Q[2 * s + j] = q[:, 128 * j : 128 * j + 128]

    for j in range(4):
        kv = nn(g.SRC[...], g.WKV[j]).astype(BF)
        g.K[j] = kv[:, 0:128]
        g.V[j] = kv[:, 128:256]

    for j in range(5):
        if j < 4:
            scores = nt(g.K[j], g.Q[j])
            g.S[j % 2, 0:CONTEXT_MIN, :] = scores[0:CONTEXT_MIN]
            g.S[j % 2, CONTEXT_MIN:CONTEXT_MAX, :] = scores[CONTEXT_MIN:CONTEXT_MAX] + g.BIAS[...]
            g.S[j % 2, CONTEXT_MAX:KEYS, :] = scores[CONTEXT_MAX:KEYS]
        if j > 0:
            p = j - 1
            scores = g.S[p % 2]
            e = jnp.exp2(scores - jnp.max(scores, axis=0, keepdims=True))
            inv = 1.0 / row_sum(e)
            g.INV[p, 0:1, :] = inv
            e = e.astype(BF)
            g.E[p] = e
            g.AT[p] = (tn(g.V[p], e) * inv).astype(BF)

    c_own["out"].wait_recv()
    c_own["up"].wait_recv()
    c_own["upb"].wait_recv()
    c_own["down"].wait_recv()
    for j in range(4):
        g.A[:, 128 * j : 128 * j + 128] = g.AT[j].T
    l_cot.wait()

    branch = nn(g.A[:, 0:256], g.WO[0]) + nn(g.A[:, 256:512], g.WO[1]) + g.outb_[...]
    joined = g.HA[h] + branch
    center = joined - lane_mean(joined)
    rstd = lax.rsqrt(lane_mean(center * center) + EPS)
    xhat = center * rstd
    after = xhat * g.ag_[...] + g.ash_[...]
    g.XH[...] = xhat
    g.RS[...] = rstd
    low = after.astype(BF)
    g.AB[...] = low
    mixed = g.downb_[...]
    for s in range(2):
        u = nn(low, g.WU[s]) + g.UB[s]
        phi = 0.5 * (1.0 + lax.erf(u * HALF_ROOT))
        g.DG[s] = phi + u * (jnp.exp2(u * u * (-0.5 * LOG2E)) * PDF_SCALE)
        act = (u * phi).astype(BF)
        g.ACT[s] = act
        mixed = mixed + nn(act, g.WD[s])
    joined = after + mixed
    center = joined - lane_mean(joined)
    rstd = lax.rsqrt(lane_mean(center * center) + EPS)
    xhat = center * rstd
    g.output[...] = xhat * g.fg_[...] + g.fsh_[...]
    ct = g.COT[...]
    d = ct * g.fg_[...]
    d = rstd * (d - lane_mean(d) - xhat * lane_mean(d * xhat))
    g.DJ[...] = d
    gm = d.astype(BF)
    g.GM[...] = gm
    g.VEC[4:5, :] = row_sum(gm.astype(F32))
    g.VEC[5:6, :] = row_sum(ct * xhat)
    g.VEC[6:7, :] = row_sum(ct)

    def put(ref, first, value):
        r = value.shape[0]
        for b in range(value.shape[1] // 128):
            ref[first + r * b : first + r * b + r, :] = value[:, 128 * b : 128 * b + 128]

    rows_of = {k: sum(r for r, _ in v) for k, v in cuts.items()}
    fulls, at = {"l": g.rbank.at[h]}, 0
    for k in ("d", "u", "o"):
        fulls[k] = g.rffn.at[pl.ds(at, rows_of[k])]
        at += rows_of[k]
    for i, k in enumerate(("q", "r")):
        fulls[k] = g.rqkv.at[i]
    blocks = {
        k: Block(ctx, [getattr(g, p + k) for p in ("CG", "CR", "CA", "CV")] + [fulls[k]], v)
        for k, v in cuts.items()
    }
    down, up, out, qkv0, qkv1, last = blocks.values()

    def tick(i):
        for k in plan[i] if i < len(plan) else []:
            blocks[k[0]].parts[int(k[1])].advance()

    put(down.give, 0, tn(g.ACT[o], g.GM[...]).astype(BF))
    down.send_core()

    gm = g.GM[...]
    d = g.DJ[...]
    for s in range(2):
        du = (g.DG[s] * nt(gm, g.WD[s])).astype(BF)
        g.DU[s] = du
        g.VEC[7 + s : 8 + s, :] = row_sum(du.astype(F32))
        d = d + nt(du, g.WU[s])
    xhat = g.XH[...]
    g.VEC[2:3, :] = row_sum(d * xhat)
    g.VEC[3:4, :] = row_sum(d)
    d = d * g.ag_[...]
    d = g.RS[...] * (d - lane_mean(d) - xhat * lane_mean(d * xhat))
    g.DJ[...] = d
    gb = d.astype(BF)
    g.GB[...] = gb
    g.VEC[1:2, :] = row_sum(gb.astype(F32))
    put(down.acc, 0, tn(g.ACT[h], g.GM[...]).astype(BF))
    down.merge_core()
    tick(2)
    put(up.give, 0, tn(g.AB[...], g.DU[o]).astype(BF))
    up.send_core()
    for j in range(2):
        put(out.give, 128 * j * 4, nn(g.AT[2 * o + j], g.GB[...]).astype(BF))
    out.send_core()
    c_vec = links.copy(g.VEC, g.VECR, ctx.twin)
    put(up.acc, 0, tn(g.AB[...], g.DU[h]).astype(BF))
    for j in range(2):
        put(out.acc, 128 * j * 4, nn(g.AT[2 * h + j], g.GB[...]).astype(BF))
    tick(3)

    g.HQT[...] = g.HB[h].T
    g.SRCT[...] = g.SRC[pl.ds(pl.multiple_of(h * n, n), n), :].T
    for j in range(4):
        d = nt(g.WO[j // 2, 128 * (j % 2) : 128 * (j % 2) + 128, :], g.GB[...]).astype(BF)
        g.DOT[j] = d
        df = d.astype(F32)
        g.INNER[j, 0:1, :] = row_sum(df * g.AT[j].astype(F32))
        g.DOT2[j] = (df * g.INV[j, 0:1, :]).astype(BF)
    tick(4)
    up.merge_core()
    out.merge_core()
    tick(5)

    vec_stages = vec_groups(count)
    vec = Ctx()
    vec.k = 0

    def vec_start(value):
        bits = vec_stages[vec.k]
        digit, _ = down.parts[0]._digits(bits, 0)
        slots = g.VECS.at[vec.k]
        slots[digit] = value
        send, vec.sem = links.send_sem(), links.recv_sem()
        others = slots.at[pl.ds(0, 2 ** len(bits) - 1)]
        for mask in range(1, 2 ** len(bits)):
            _, row = down.parts[0]._digits(bits, mask)
            links.start(slots.at[digit], slots.at[digit], (row, h), send, vec.sem)
        links.open.append(functools.partial(wait_bytes, others, send))

    def vec_end():
        ways = 2 ** len(vec_stages[vec.k])
        wait_bytes(g.VECS.at[vec.k, pl.ds(0, ways - 1)], vec.sem)
        value = g.VECS[vec.k, 0]
        for i in range(1, ways):
            value = value + g.VECS[vec.k, i]
        vec.k += 1
        if vec.k < len(vec_stages):
            vec_start(value)
        else:
            g.vec[...] = value

    kv_copies = {}

    def attend_back(j):
        q, dot, dot2 = g.Q[j], g.DOT[j], g.DOT2[j]
        inner, factor = g.INNER[j, 0:1, :], g.INV[j, 0:1, :]
        dq = None
        for t in range(KEYS // 512):
            rows = slice(512 * t, 512 * t + 512)
            e = g.E[j, rows, :]
            upstream = nn(g.V[j, rows, :], dot)
            ds = (e.astype(F32) * ((upstream - inner) * factor)).astype(BF)
            g.DKV[j, rows, 0:128] = (nn(ds, q) * (DH**-0.5 / Q_SCALE)).astype(BF)
            g.DKV[j, rows, 128:256] = nt(e, dot2).astype(BF)
            part = tn(g.K[j, rows, :], ds)
            dq = part if dq is None else dq + part
        g.DQT[j] = (dq * DH**-0.5).astype(BF)
        other = pl.ds(pl.multiple_of(o * n, n), n)
        kv_copies[j] = links.copy(g.DKV.at[j, other], g.DKVR.at[j], ctx.twin)

    def merge_kv(j):
        kv_copies[j].wait_recv()
        mine = pl.ds(pl.multiple_of(h * n, n), n)
        g.DKVO[j] = (g.DKV[j, mine, :].astype(F32) + g.DKVR[j].astype(F32)).astype(BF)

    def q_grads(p, block):
        for j, ref in ((2 * o + p, block.give), (2 * h + p, block.acc)):
            put(ref, 0, nt(g.HQT[...], g.DQT[j]).astype(BF))

    def kv_grads(p, block):
        put(block.give, n, nn(g.SRCT[...], g.DKVO[2 * o + p]).astype(BF))
        block.send_core()
        put(block.acc, n, nn(g.SRCT[...], g.DKVO[2 * h + p]).astype(BF))

    attend_back(0)
    tick(6)
    attend_back(2)
    tick(7)
    q_grads(0, qkv0)
    attend_back(1)
    tick(8)
    merge_kv(0)
    merge_kv(2)
    kv_grads(0, qkv0)
    tick(9)
    attend_back(3)
    tick(10)
    qkv0.merge_core()
    c_vec.wait_recv()
    vec_start(g.VEC[...] + g.VECR[...])
    tick(11)
    q_grads(1, qkv1)
    for j in range(4):
        g.DQ[:, 128 * j : 128 * j + 128] = g.DQT[j].T
    dh = g.DJ[...] + nt(g.DQ[:, 0:256], g.WQKV[0, 0]) + nt(g.DQ[:, 256:512], g.WQKV[1, 0])
    tick(12)

    merge_kv(1)
    merge_kv(3)
    kvh = nt(g.DKVO[0], g.WKV[0])
    for j in range(1, 4):
        kvh = kvh + nt(g.DKVO[j], g.WKV[j])
    edge = CONTEXT_MAX - n
    g.DP[0] = kvh[edge:n, :].astype(BF)
    c_prompt = links.copy(g.DP.at[0], g.DP.at[1], ctx.twin)
    g.GH[0:edge, :] = (dh[0:edge] + kvh[0:edge]).astype(BF)
    first = jnp.where(h == 0, 1.0, 0.0)
    g.GH[edge:n, :] = (dh[edge:n] + kvh[edge:n] * first).astype(BF)
    tick(13)
    kv_grads(1, qkv1)
    tick(14)
    gh = g.GH[...]
    g.ENC[0:features, :] = nn(g.NL[h], gh)
    g.ENC[features:, :] = jnp.zeros_like(g.ENC[features:, :])
    bank_rows = g.bank.shape[0] // 2
    enc_at = bank_rows * 4
    for b in range(4):
        cols = slice(128 * b, 128 * b + 128)
        last.give[64 * b : 64 * b + 64, :] = g.ENC[pl.ds(pl.multiple_of(o * 64, 64), 64), cols].astype(BF)
        last.acc[enc_at + 64 * b : enc_at + 64 * b + 64, :] = g.ENC[
            pl.ds(pl.multiple_of(h * 64, 64), 64), cols
        ].astype(BF)
    last.send_core()
    c_prompt.wait_recv()
    put(
        last.acc,
        0,
        nn(g.SEL[pl.ds(pl.multiple_of(h * bank_rows, bank_rows), bank_rows), :], g.DP[o]).astype(BF),
    )
    tick(15)
    qkv1.merge_core()
    last.core_copy.wait_recv()
    rows = slice(enc_at, enc_at + 256)
    last.acc[rows, :] = (last.acc[rows, :].astype(F32) + last.got[...].astype(F32)).astype(BF)
    if last.n > enc_at + 256:
        last.acc[enc_at + 256 :, :] = jnp.zeros_like(last.acc[enc_at + 256 :, :])
    tick(16)
    vec_end()

    scale = g.COLS[:, 2:3]
    uf = nt(g.encw_[...], gh) * scale
    g.uf[...] = uf
    g.SQUARE[...] = jnp.zeros_like(g.SQUARE)
    g.LATE[0] = to_rows([lane_sum(uf), lane_sum(uf * (g.F[h] - g.COLS[:, 0:1]))])
    eb = row_sum(gh.astype(F32))
    for b in range(4):
        g.LATE[0, 2 + b : 3 + b, :] = eb[:, 128 * b : 128 * b + 128]
    c_late = links.copy(g.LATE.at[0], g.LATE.at[1], ctx.twin)
    tick(17)
    c_late.wait_recv()
    g.LSUM[ctx.row] = g.LATE[0] + g.LATE[1]
    wait_late = share_slots(ctx, g.LSUM, ctx.row, everyone[0:-1:2])
    tick(18)
    rest = [p for b in blocks.values() for p in b.parts]
    while not all(p.done() for p in rest):
        for p in rest:
            if not p.done():
                p.advance()
    while vec.k < len(vec_stages):
        vec_end()
    c_last = links.copy(g.rbank.at[h], g.rbank.at[h], ctx.twin)
    wait_late()
    late = g.LSUM[0]
    for k in range(1, count):
        late = late + g.LSUM[k]
    g.late[...] = late
    g.stat[...] = g.STAT[...]
    c_last.wait_recv()
    links.drain()
    assert (links.sent, links.received, loads.used) == sem_counts, (links.sent, links.received, loads.used)


def vec_groups(count):
    bits = [2**i for i in range(count.bit_length() - 1)]
    return [tuple(bits[i : i + 2]) for i in range(0, len(bits), 2)]


def finish_kernel(total_rows, names, *refs):
    g = Ctx()
    for name, ref in zip(names, refs, strict=True):
        setattr(g, name, ref)
    h = lax.axis_index("heads")
    features = g.feats.shape[0]
    copies = []

    def copy(src, dst):
        c = pltpu.make_async_copy(src, dst, g.sems.at[len(copies)])
        c.start()
        copies.append(c)
        return c

    outs = [copy(g.output, g.o_output)]
    c_feats = copy(g.feats, g.FEATS)
    up_at = g.rffn.shape[0] // 5 * 2

    def block(ref, first, rows):
        return ref[first : first + rows, :].astype(F32)

    for b in range(4):
        cols = slice(128 * b, 128 * b + 128)
        g.DOWN[:, cols] = block(g.rffn, 512 * b, 512)
    outs.append(copy(g.DOWN, g.o_down))
    for b in range(4):
        cols = slice(128 * b, 128 * b + 128)
        g.UP[:, cols] = block(g.rffn, up_at + 512 * b, 512)
    outs.append(copy(g.UP, g.o_up))
    for b in range(4):
        cols = slice(128 * b, 128 * b + 128)
        for j in range(2):
            g.OUT[128 * j : 128 * j + 128, cols] = block(g.rffn, 2 * up_at + 512 * j + 128 * b, 128)
    outs.append(copy(g.OUT, g.o_out))
    for c in range(3):
        for p in range(2):
            g.QKV[c, :, 128 * p : 128 * p + 128] = g.rqkv[p, 512 * c : 512 * c + 512, :].astype(F32)
    outs.append(copy(g.QKV, g.o_qkv))
    for b in range(4):
        cols = slice(128 * b, 128 * b + 128)
        for s in range(2):
            g.BANKV[256 * s : 256 * s + 256, cols] = g.rbank[s, 256 * b : 256 * b + 256, :].astype(F32)
        g.o_encw[0:64, cols] = g.rbank[0, 1024 + 64 * b : 1024 + 64 * b + 64, :].astype(F32)
        g.o_encw[64:features, cols] = g.rbank[1, 1024 + 64 * b : 1024 + 64 * b + features - 64, :].astype(F32)
        g.o_encb[:, cols] = g.late[2 + b : 3 + b, :]
    outs.append(copy(g.BANKV, g.o_bank))
    g.o_outb[...] = g.vec[1:2, :]
    g.o_ag[...] = g.vec[2:3, :]
    g.o_ash[...] = g.vec[3:4, :]
    g.o_downb[...] = g.vec[4:5, :]
    g.o_fg[...] = g.vec[5:6, :]
    g.o_fsh[...] = g.vec[6:7, :]
    g.o_upb[...] = g.vec[pl.ds(7 + h, 1), :]
    mean, inverse = g.stat[0:1, :], g.stat[1:2, :]
    b1, b2 = g.late[0:1, :], g.late[1:2, :]
    var_grad = -0.5 * inverse * inverse * inverse * b2
    g.SQUARE[...] = jnp.zeros_like(g.SQUARE)
    g.SQUARE[0:1, :] = inverse
    g.SQUARE[1:2, :] = (-inverse * b1 - 2.0 * mean * var_grad) / total_rows
    g.SQUARE[2:3, :] = 2.0 * var_grad / total_rows
    columns = g.SQUARE[...].T
    inverse, first, slope = [columns[0:features, i : i + 1] for i in range(3)]
    c_feats.wait()
    g.o_feats[...] = g.uf[...] * inverse + first + g.FEATS[...] * slope
    for c in outs:
        c.wait()


def per_device(
    feats,
    feature_mask,
    splits,
    prompt_index,
    prompt_bank,
    enc_weight,
    enc_bias,
    qkv_weight,
    out_weight,
    out_bias,
    attn_gain,
    attn_shift,
    up_weight,
    up_bias,
    down_weight,
    down_bias,
    ffn_gain,
    ffn_shift,
    cotangent,
):
    n, features = feats.shape
    count = lax.axis_size("rows")
    total_rows = n * count * lax.axis_size("heads")
    d = prompt_bank.shape[1]
    columns = feats.T
    args = [
        columns, feature_mask, splits, prompt_index, prompt_bank, enc_weight, enc_bias[None], qkv_weight, out_weight,
        out_bias[None], attn_gain[None], attn_shift[None], up_weight, up_bias[None], down_weight, down_bias[None],
        ffn_gain[None], ffn_shift[None], cotangent,
    ]
    vmem = pl.BlockSpec(memory_space=pltpu.VMEM)
    hbm = pl.BlockSpec(memory_space=pl.ANY)
    bits = [2**i for i in range(count.bit_length() - 1)]
    grain = 16 * count
    block_rows = {"d": 2048, "u": 2048, "o": 1024, "q": 1536, "r": 1536, "l": 1280}
    if count == 16:
        cuts, plan = CUTS, PLAN
    else:
        cuts, plan = {k: [(-(-r // grain) * grain, vec_groups(count))] for k, r in block_rows.items()}, []
    block_rows = {k: sum(r for r, _ in v) for k, v in cuts.items()}
    S = jax.ShapeDtypeStruct
    outs = {
        "output": S((n, d), F32),
        "uf": S((features, n), F32),
        "rffn": S((block_rows["d"] + block_rows["u"] + block_rows["o"], 128), BF),
        "rqkv": S((2, block_rows["q"], 128), BF),
        "rbank": S((2, block_rows["l"], 128), BF),
        "vec": S((16, d), F32),
        "late": S((8, 128), F32),
        "stat": S((8, 128), F32),
    }
    V = pltpu.VMEM
    scratch = {k + "_": V(args[IN_NAMES.index(k)].shape, args[IN_NAMES.index(k)].dtype) for k in SMALL}
    scratch["splits_"] = pltpu.SMEM(splits.shape, splits.dtype)
    scratch |= {
        "F": V((2, features, n), F32),
        "WQKV": V((2, 3, d, 256), BF),
        "WO": V((2, 256, d), BF),
        "UB": V((2, 1, 512), F32),
        "WU": V((2, d, 512), BF),
        "WD": V((2, 512, d), BF),
        "BANKV": V(prompt_bank.shape, BF),
        "COT": V((n, d), F32),
        "SQUARE": V((128, 128), F32),
        "COLS": V((features, 128), F32),
        "LATE": V((2, 8, 128), F32),
        "MOM": V((2 * count, 1, 256), F32),
        "LSUM": V((count, 8, 128), F32),
        "STAT": V((8, 128), F32),
        "VEC": V((16, d), F32),
        "VECR": V((16, d), F32),
        "VECS": V((len(vec_groups(count)), 4, 16, d), F32),
        "SEL": V((prompt_bank.shape[0], P_SIZE), BF),
        "SRC": V((KEYS, d), BF),
        "BIAS": V((CONTEXT_MAX - CONTEXT_MIN, 1), F32),
        "S": V((2, KEYS, n), F32),
        "WKV": V((4, d, 256), BF),
        "NL": V((2, features, n), BF),
        "HA": V((2, n, d), F32),
        "HB": V((2, n, d), BF),
        "Q": V((4, n, 128), BF),
        "K": V((4, KEYS, 128), BF),
        "V": V((4, KEYS, 128), BF),
        "E": V((4, KEYS, n), BF),
        "INV": V((4, 8, n), F32),
        "INNER": V((4, 8, n), F32),
        "AT": V((4, 128, n), BF),
        "A": V((n, d), BF),
        "XH": V((n, d), F32),
        "RS": V((n, 1), F32),
        "AB": V((n, d), BF),
        "DG": V((2, n, 512), F32),
        "ACT": V((2, n, 512), BF),
        "DU": V((2, n, 512), BF),
        "DJ": V((n, d), F32),
        "GM": V((n, d), BF),
        "GB": V((n, d), BF),
        "DOT": V((4, 128, n), BF),
        "DOT2": V((4, 128, n), BF),
        "DKV": V((4, KEYS, 256), BF),
        "DKVR": V((4, n, 256), BF),
        "DKVO": V((4, n, 256), BF),
        "DQT": V((4, 128, n), BF),
        "DQ": V((n, d), BF),
        "HQT": V((d, n), BF),
        "SRCT": V((d, n), BF),
        "DP": V((2, P_SIZE, d), BF),
        "GH": V((n, d), BF),
        "ENC": V((128, d), F32),
    }
    for k, r in block_rows.items():
        small = 256 if k == "l" else r
        scratch["CG" + k] = V((small, 128), BF)
        scratch["CR" + k] = V((small, 128), BF)
        scratch["CA" + k] = V((r, 128), BF)
        scratch["CV" + k] = V((2 * r, 128), BF)
    parts = [stages for v in cuts.values() for _, stages in v]
    once = 22 + len(vec_groups(count))
    sem_counts = (once + len(parts), once + sum(2 * len(s) - (len(s[-1]) == 1 or 0 in s[-1]) for s in parts), 8 + len(SMALL))
    for k, v in zip(("ssem", "rsem", "lsem"), sem_counts, strict=True):
        scratch[k] = pltpu.SemaphoreType.DMA((v,))
    names = IN_NAMES + OUT_NAMES + list(scratch)
    results = pl.pallas_call(
        functools.partial(layer_kernel, count, total_rows, cuts, plan, sem_counts, names),
        out_shape=[pltpu.VMEM(outs[k].shape, outs[k].dtype) for k in OUT_NAMES],
        in_specs=[hbm] * len(IN_NAMES),
        out_specs=[vmem] * len(OUT_NAMES),
        scratch_shapes=list(scratch.values()),
        compiler_params=pltpu.CompilerParams(
            collective_id=0, has_side_effects=True, vmem_limit_bytes=VMEM_LIMIT
        ),
        name="layer",
    )(*args)
    finals = {
        "o_output": S((n, d), F32),
        "o_feats": S((features, n), F32),
        "o_bank": S(prompt_bank.shape, F32),
        "o_encw": S(enc_weight.shape, F32),
        "o_encb": S((1, d), F32),
        "o_qkv": S(qkv_weight.shape, F32),
        "o_out": S(out_weight.shape, F32),
        "o_outb": S((1, d), F32),
        "o_ag": S((1, d), F32),
        "o_ash": S((1, d), F32),
        "o_up": S(up_weight.shape, F32),
        "o_upb": S((1, up_bias.shape[0]), F32),
        "o_down": S(down_weight.shape, F32),
        "o_downb": S((1, d), F32),
        "o_fg": S((1, d), F32),
        "o_fsh": S((1, d), F32),
    }
    moved = {"o_output", "o_bank", "o_qkv", "o_out", "o_up", "o_down"}
    work = {
        "FEATS": V((features, n), F32),
        "DOWN": V(down_weight.shape, F32),
        "UP": V(up_weight.shape, F32),
        "OUT": V(out_weight.shape, F32),
        "QKV": V(qkv_weight.shape, F32),
        "BANKV": V(prompt_bank.shape, F32),
        "SQUARE": V((128, 128), F32),
        "sems": pltpu.SemaphoreType.DMA((7,)),
    }
    final = pl.pallas_call(
        functools.partial(finish_kernel, total_rows, ["feats"] + OUT_NAMES + list(finals) + list(work)),
        out_shape=list(finals.values()),
        in_specs=[hbm] + [vmem] * len(OUT_NAMES),
        out_specs=[hbm if k in moved else vmem for k in finals],
        scratch_shapes=list(work.values()),
        compiler_params=pltpu.CompilerParams(vmem_limit_bytes=VMEM_LIMIT),
        name="finish",
    )(columns, *[pltpu.with_memory_space_constraint(v, pltpu.VMEM) for v in results])
    vectors = ("o_encb", "o_outb", "o_ag", "o_ash", "o_upb", "o_downb", "o_fg", "o_fsh")
    return tuple(
        v[0] if k in vectors else v.T if k == "o_feats" else v for k, v in zip(finals, final, strict=True)
    )


def solution(mesh):
    whole = P(("rows", "heads"), None)
    placed = (
        whole, P("rows", None), P("rows"), P("rows", None), P(), P(), P(), P(None, None, "heads"), P("heads", None),
        P(), P(), P(), P(None, "heads"), P("heads"), P("heads", None), P(), P(), P(), whole,
    )
    return jax.shard_map(
        per_device,
        mesh=mesh,
        in_specs=placed,
        out_specs=(
            whole, whole, P(), P(), P(), P(None, None, "heads"), P("heads", None), P(), P(), P(), P(None, "heads"),
            P("heads"), P("heads", None), P(), P(), P(),
        ),
        check_vma=False,
    )
```

```python
import functools
import math

import jax
import jax.numpy as jnp
from jax import lax
from jax.experimental import pallas as pl
from jax.experimental.pallas import tpu as pltpu
from jax.sharding import PartitionSpec as P

BF = jnp.bfloat16
F32 = jnp.float32
MESH = pl.DeviceIdType.MESH
DH = 128
P_SIZE = 128
CONTEXT_MAX = 896
CONTEXT_MIN = 640
KEYS = CONTEXT_MAX + P_SIZE
EPS = 1e-05
HALF_ROOT = math.sqrt(0.5)
PDF_SCALE = 1.0 / math.sqrt(2.0 * math.pi)
LOG2E = math.log2(math.e)
Q_SCALE = DH**-0.5 * LOG2E
VMEM_LIMIT = 52 * 2**20


def _dot(a, b, ca, cb):
    return lax.dot_general(a, b, (((ca,), (cb,)), ((), ())), preferred_element_type=F32)


def nn(a, b):
    return _dot(a, b, 1, 0)


def nt(a, b):
    return _dot(a, b, 1, 1)


def tn(a, b):
    return _dot(a, b, 0, 0)


def row_sum(v):
    return jnp.sum(v, axis=0, keepdims=True)


def lane_mean(v):
    return jnp.mean(v, axis=-1, keepdims=True)


class Links:
    def __init__(self, send, recv):
        self.send, self.recv, self.sent, self.received, self.open = send, recv, 0, 0, []

    def send_sem(self):
        self.sent += 1
        return self.send.at[self.sent - 1]

    def recv_sem(self):
        self.received += 1
        return self.recv.at[self.received - 1]

    def start(self, src, dst, device, send, recv):
        c = pltpu.make_async_remote_copy(
            src_ref=src, dst_ref=dst, send_sem=send, recv_sem=recv, device_id=device, device_id_type=MESH
        )
        c.start()
        return c

    def copy(self, src, dst, device):
        c = self.start(src, dst, device, self.send_sem(), self.recv_sem())
        self.open.append(c.wait_send)
        return c

    def drain(self):
        for wait in self.open:
            wait()
        self.open = []


def wait_bytes(ref, sem):
    pltpu.make_async_copy(ref, ref, sem).wait()


class Loads:
    def __init__(self, sems):
        self.sems, self.used = sems, 0

    def copy(self, src, dst):
        c = pltpu.make_async_copy(src, dst, self.sems.at[self.used])
        self.used += 1
        c.start()
        return c


class Part:
    def __init__(self, ctx, block, first, rows, stages):
        self.ctx, self.first, self.rows = ctx, first, rows
        self.stages = [tuple(b for b in s if b) for s in stages]
        self.whole = len(stages[-1]) == 1 or 0 in stages[-1]
        self.acc, self.recv, self.full = block.acc, block.recv, block.full
        self.at = -1

    def begin(self):
        self.base, self.len, self.off, self.k = self.first, self.rows, 2 * self.first, 0
        self.send_sem = self.ctx.links.send_sem()
        self._start_scatter()

    def _digits(self, bits, mask):
        digit, row = 0, self.ctx.row
        for i, b in enumerate(bits):
            bit = (self.ctx.row // b) % 2
            if mask >> i & 1:
                row = row + b * (1 - 2 * bit)
                bit = 1 - bit
            digit = digit * 2 + bit
        return digit, row

    def _wait(self, rows):
        view = self.full.at[pl.ds(0, rows)]
        wait_bytes(view, self.recv_sem)
        wait_bytes(view, self.send_sem)

    def _exchanges(self):
        return self.whole and self.k == len(self.stages) - 1

    def _slot(self, digit):
        return pl.ds(pl.multiple_of(self.off + digit * self.len, 16), self.len)

    def _start_scatter(self):
        bits = self.stages[self.k]
        ways = 2 ** len(bits)
        self.recv_sem = self.ctx.links.recv_sem()
        mine, _ = self._digits(bits, 0)
        q = self.len // ways
        for mask in range(1, ways):
            digit, row = self._digits(bits, mask)
            if self._exchanges():
                src = self.acc.at[pl.ds(pl.multiple_of(self.base, 16), self.len)]
                dst = self.recv.at[self._slot(mine)]
            else:
                src = self.acc.at[pl.ds(pl.multiple_of(self.base + digit * q, 16), q)]
                dst = self.recv.at[pl.ds(self.off + (mask - 1) * q, q)]
            self.ctx.links.start(src, dst, (row, self.ctx.head), self.send_sem, self.recv_sem)

    def _end_scatter(self):
        bits = self.stages[self.k]
        ways = 2 ** len(bits)
        digit, _ = self._digits(bits, 0)
        if self._exchanges():
            mine = pl.ds(pl.multiple_of(self.base, 16), self.len)
            self.recv[self._slot(digit), :] = self.acc[mine, :]
            self._wait((ways - 1) * self.len)
            total = self.recv[self._slot(0), :].astype(F32)
            for i in range(1, ways):
                total = total + self.recv[self._slot(i), :].astype(F32)
            self.full[mine, :] = total.astype(BF)
            self._start_gather()
            return
        q = self.len // ways
        self.base = self.base + digit * q
        mine = pl.ds(pl.multiple_of(self.base, 16), q)
        self._wait((ways - 1) * q)
        total = self.acc[mine, :].astype(F32)
        for i in range(ways - 1):
            total = total + self.recv[pl.ds(self.off + i * q, q), :].astype(F32)
        self.off += (ways - 1) * q
        self.len = q
        self.k += 1
        if self.k < len(self.stages):
            self.acc[mine, :] = total.astype(BF)
            self._start_scatter()
        else:
            self.full[mine, :] = total.astype(BF)
            self._start_gather()

    def _start_gather(self):
        if self.k == 0:
            return
        bits = self.stages[self.k - 1]
        mine = self.full.at[pl.ds(pl.multiple_of(self.base, 16), self.len)]
        self.recv_sem = self.ctx.links.recv_sem()
        for mask in range(1, 2 ** len(bits)):
            _, row = self._digits(bits, mask)
            self.ctx.links.start(mine, mine, (row, self.ctx.head), self.send_sem, self.recv_sem)

    def _end_gather(self):
        bits = self.stages[self.k - 1]
        ways = 2 ** len(bits)
        self._wait((ways - 1) * self.len)
        digit, _ = self._digits(bits, 0)
        self.base = self.base - digit * self.len
        self.len = self.len * ways
        self.k -= 1
        self._start_gather()

    def steps(self):
        return 2 * len(self.stages) - self.whole

    def done(self):
        return self.at == self.steps()

    def advance(self):
        if self.at < 0:
            self.begin()
        elif self.at < len(self.stages):
            self._end_scatter()
        elif not self.done():
            self._end_gather()
        self.at += 1


class Block:
    def __init__(self, ctx, refs, cuts):
        self.ctx = ctx
        self.give, self.got, self.acc, self.recv, self.full = refs
        self.n = self.acc.shape[0]
        self.parts, first = [], 0
        for rows, stages in cuts:
            self.parts.append(Part(ctx, self, first, rows, stages))
            first += rows

    def send_core(self):
        self.core_copy = self.ctx.links.copy(self.give, self.got, self.ctx.twin)

    def merge_core(self):
        self.core_copy.wait_recv()
        for part in self.parts:
            rows = slice(part.first, part.first + part.rows)
            self.acc[rows, :] = (self.acc[rows, :].astype(F32) + self.got[rows, :].astype(F32)).astype(BF)


class Ctx:
    pass


def others_of(ctx, count):
    steps = sorted(range(1, count), key=lambda k: min(k, count - k))
    rows = [lax.rem(ctx.row + k, count) for k in steps]
    return [(row, head) for row in rows for head in (ctx.head, 1 - ctx.head)] + [ctx.twin]


def share_slots(ctx, slots, place, devices):
    mine = slots.at[place]
    send, recv = ctx.links.send_sem(), ctx.links.recv_sem()
    for device in devices:
        ctx.links.start(mine, mine, device, send, recv)
    others = slots.at[pl.ds(0, len(devices))]
    ctx.links.open.append(functools.partial(wait_bytes, others, send))
    return functools.partial(wait_bytes, others, recv)


SMALL = [
    "mask", "splits", "pidx", "encw", "encb", "outb", "ag", "ash", "downb", "fg", "fsh",
]
IN_NAMES = [
    "feats", "mask", "splits", "pidx", "bank", "encw", "encb", "qkvw", "outw", "outb", "ag", "ash", "upw",
    "upb", "downw", "downb", "fg", "fsh", "cot",
]
OUT_NAMES = [
    "output", "uf", "rffn", "rqkv", "rbank", "vec", "late", "stat",
]
CUTS = {
    "d": [(1024, [(2,), (1,), (4, 8)]), (1024, [(1, 2), (4, 8)])],
    "u": [(1024, [(1,), (4,), (2, 8)]), (1024, [(4,), (2,), (1,), (8,)])],
    "o": [(1024, [(1, 2), (8,), (4,)])],
    "q": [(256, [(2,), (1,), (4,), (8,)]), (512, [(1,), (2,), (4,), (8,)]), (768, [(4,), (1, 2), (8,)])],
    "r": [(768, [(1,), (2, 4), (8,)]), (768, [(2,), (1, 4), (8,)])],
    "l": [(768, [(4,), (1, 2), (8,)]), (512, [(1, 2), (4, 8)])],
}
PLAN = [
    [],
    [],
    ["d1", "d0"],
    [],
    [],
    ["u1", "u0", "o0"],
    [],
    ["d1"],
    [],
    ["d0", "u1", "u0"],
    ["d1"],
    ["o0", "q1", "q0", "q2"],
    ["d0", "u1", "u0"],
    ["d1", "q0", "q1"],
    ["o0"],
    ["u1", "q2", "d0"],
    ["u0", "r0", "l0", "r1", "l1", "o0"],
    [],
    ["d1", "q0", "q1", "u1", "q2", "d0", "r0", "u0", "l0", "r1", "q0", "o0", "q1", "u1", "l1", "q2", "d0", "r0", "l0", "u0", "r1", "q0", "q1", "l1"],
    ["r0", "l0", "o0", "u1", "q0", "q1", "r1", "q2", "l1", "u0", "d0", "q0", "r0", "u1", "l0", "r1", "q1", "l1", "q2", "q0", "r0", "l0", "q1", "r1"],
]


def layer_kernel(count, total_rows, cuts, plan, sem_counts, names, *refs):
    g = Ctx()
    for name, ref in zip(names, refs, strict=True):
        setattr(g, name, ref)
    features, n = g.feats.shape
    ctx = Ctx()
    ctx.row, ctx.head = lax.axis_index("rows"), lax.axis_index("heads")
    h = ctx.head
    o = 1 - h
    ctx.twin = (ctx.row, o)
    ctx.links = links = Links(g.ssem, g.rsem)
    loads = Loads(g.lsem)

    l_feats = loads.copy(g.feats, g.F.at[h])
    own = {
        "qkv": (g.qkvw, g.WQKV.at[h]),
        "out": (g.outw, g.WO.at[h]),
        "upb": (g.upb, g.UB.at[h]),
        "up": (g.upw, g.WU.at[h]),
        "down": (g.downw, g.WD.at[h]),
    }
    everyone = others_of(ctx, count)
    barrier = pltpu.get_barrier_semaphore()
    for device in everyone:
        pl.semaphore_signal(barrier, inc=1, device_id=device, device_id_type=MESH)
    l_small = [loads.copy(getattr(g, k), getattr(g, k + "_")) for k in SMALL]
    l_bank = loads.copy(g.bank, g.BANKV)
    l_own = {k: loads.copy(*v) for k, v in own.items()}
    l_cot = loads.copy(g.cot, g.COT)

    def to_rows(columns):
        for i, c in enumerate(columns):
            g.SQUARE[0:features, i : i + 1] = c
        return g.SQUARE[...].T[0:8, :]

    def lane_sum(v):
        return jnp.sum(v, axis=-1, keepdims=True)

    def put_vector(half, i, value):
        for b in range(4):
            g.VEC[half, 4 * i + b : 4 * i + b + 1, :] = value[:, 128 * b : 128 * b + 128]

    g.SQUARE[...] = jnp.zeros_like(g.SQUARE)
    l_feats.wait()
    f = g.F[h]
    rows = to_rows([lane_sum(f), lane_sum(f * f)])
    place = ctx.row * 2 + h
    g.MOM[place, :, 0:128] = rows[0:1]
    g.MOM[place, :, 128:256] = rows[1:2]
    pl.semaphore_wait(barrier, len(everyone))
    wait_moments = share_slots(ctx, g.MOM, place, everyone)
    c_feats = links.copy(g.feats, g.F.at[h], ctx.twin)
    c_own = {"qkv": links.copy(*own["qkv"], ctx.twin)}
    c_own |= {k: links.copy(*v, ctx.twin) for k, v in own.items() if k != "qkv"}

    for c in l_small:
        c.wait()
    selector = lax.broadcasted_iota(jnp.int32, (g.bank.shape[0], P_SIZE), 0) == g.pidx_[...]
    g.SEL[...] = jnp.where(selector, 1.0, 0.0).astype(BF)
    l_bank.wait()
    g.SRC[CONTEXT_MAX:KEYS, :] = tn(g.SEL[...], g.BANKV[...]).astype(BF)
    maybe = lax.broadcasted_iota(jnp.int32, (CONTEXT_MAX - CONTEXT_MIN, 1), 0) + CONTEXT_MIN
    g.BIAS[...] = jnp.where(maybe < g.splits_[0], 0.0, -1e30)
    live = g.mask_[...].astype(F32)
    scale = live * jnp.sqrt(features / jnp.sum(live, axis=-1, keepdims=True))
    g.STAT[...] = jnp.zeros_like(g.STAT)
    g.STAT[2:3, 0:features] = scale
    for c in l_own.values():
        c.wait()
    c_own["qkv"].wait_recv()
    for j in range(4):
        s, w = j // 2, pl.ds(128 * (j % 2), 128)
        g.WKV[j, :, 0:128] = g.WQKV[s, 1, :, w]
        g.WKV[j, :, 128:256] = g.WQKV[s, 2, :, w]

    c_feats.wait_recv()
    wait_moments()
    moments = g.MOM[0]
    for k in range(1, 2 * count):
        moments = moments + g.MOM[k]
    mean = moments[:, 0:128] / total_rows
    var = moments[:, 128:256] / total_rows - mean * mean
    g.STAT[0:1, :] = mean
    g.STAT[1:2, :] = lax.rsqrt(var + EPS)
    g.SQUARE[0:8, :] = g.STAT[...]
    columns = g.SQUARE[...].T
    mean, inverse, scale = [columns[0:features, i : i + 1] for i in range(3)]
    g.COLS[...] = columns[0:features, :]

    for s in range(2):
        g.NL[s] = (((g.F[s] - mean) * inverse) * scale).astype(BF)
        hidden = tn(g.NL[s], g.encw_[...]) + g.encb_[...]
        g.HA[s] = hidden
        g.HB[s] = hidden.astype(BF)
    g.SRC[0:n, :] = g.HB[0]
    g.SRC[n:CONTEXT_MAX, :] = g.HB[1, 0 : CONTEXT_MAX - n, :]

    for s in range(2):
        q = (nn(g.HB[h], g.WQKV[s, 0]) * Q_SCALE).astype(BF)
        for j in range(2):
            g.Q[2 * s + j] = q[:, 128 * j : 128 * j + 128]

    for j in range(4):
        kv = nn(g.SRC[...], g.WKV[j]).astype(BF)
        g.K[j] = kv[:, 0:128]
        g.V[j] = kv[:, 128:256]

    for j in range(5):
        if j < 4:
            scores = nt(g.K[j], g.Q[j])
            g.S[j % 2, 0:CONTEXT_MIN, :] = scores[0:CONTEXT_MIN]
            g.S[j % 2, CONTEXT_MIN:CONTEXT_MAX, :] = scores[CONTEXT_MIN:CONTEXT_MAX] + g.BIAS[...]
            g.S[j % 2, CONTEXT_MAX:KEYS, :] = scores[CONTEXT_MAX:KEYS]
        if j > 0:
            p = j - 1
            scores = g.S[p % 2]
            e = jnp.exp2(scores - jnp.max(scores, axis=0, keepdims=True))
            inv = 1.0 / row_sum(e)
            g.INV[p, 0:1, :] = inv
            e = e.astype(BF)
            g.E[p] = e
            g.AT[p] = (tn(g.V[p], e) * inv).astype(BF)

    c_own["out"].wait_recv()
    c_own["up"].wait_recv()
    c_own["upb"].wait_recv()
    c_own["down"].wait_recv()
    for j in range(4):
        g.A[:, 128 * j : 128 * j + 128] = g.AT[j].T
    l_cot.wait()

    branch = nn(g.A[:, 0:256], g.WO[0]) + nn(g.A[:, 256:512], g.WO[1]) + g.outb_[...]
    joined = g.HA[h] + branch
    center = joined - lane_mean(joined)
    rstd = lax.rsqrt(lane_mean(center * center) + EPS)
    xhat = center * rstd
    after = xhat * g.ag_[...] + g.ash_[...]
    g.XH[...] = xhat
    g.RS[...] = rstd
    low = after.astype(BF)
    g.AB[...] = low
    mixed = g.downb_[...]
    for s in range(2):
        u = nn(low, g.WU[s]) + g.UB[s]
        phi = 0.5 * (1.0 + lax.erf(u * HALF_ROOT))
        g.DG[s] = phi + u * (jnp.exp2(u * u * (-0.5 * LOG2E)) * PDF_SCALE)
        act = (u * phi).astype(BF)
        g.ACT[s] = act
        mixed = mixed + nn(act, g.WD[s])
    joined = after + mixed
    center = joined - lane_mean(joined)
    rstd = lax.rsqrt(lane_mean(center * center) + EPS)
    xhat = center * rstd
    g.output[...] = xhat * g.fg_[...] + g.fsh_[...]
    ct = g.COT[...]
    d = ct * g.fg_[...]
    d = rstd * (d - lane_mean(d) - xhat * lane_mean(d * xhat))
    g.DJ[...] = d
    gm = d.astype(BF)
    g.GM[...] = gm
    put_vector(1, 0, row_sum(gm.astype(F32)))
    put_vector(1, 1, row_sum(ct * xhat))
    put_vector(1, 2, row_sum(ct))

    def put(ref, first, value):
        r = value.shape[0]
        for b in range(value.shape[1] // 128):
            ref[first + r * b : first + r * b + r, :] = value[:, 128 * b : 128 * b + 128]

    rows_of = {k: sum(r for r, _ in v) for k, v in cuts.items()}
    fulls, at = {"l": g.rbank.at[h]}, 0
    for k in ("d", "u", "o"):
        fulls[k] = g.rffn.at[pl.ds(at, rows_of[k])]
        at += rows_of[k]
    for i, k in enumerate(("q", "r")):
        fulls[k] = g.rqkv.at[i]
    blocks = {
        k: Block(ctx, [getattr(g, p + k) for p in ("CG", "CR", "CA", "CV")] + [fulls[k]], v)
        for k, v in cuts.items()
    }
    down, up, out, qkv0, qkv1, last = blocks.values()

    def tick(i):
        for k in plan[i] if i < len(plan) else []:
            blocks[k[0]].parts[int(k[1])].advance()
            share_last()

    def share_last():
        if not hasattr(ctx, "c_last") and all(p.done() for p in last.parts):
            ctx.c_last = links.copy(g.rbank.at[h], g.rbank.at[h], ctx.twin)

    put(down.give, 0, tn(g.ACT[o], g.GM[...]).astype(BF))
    down.send_core()

    gm = g.GM[...]
    d = g.DJ[...]
    for s in range(2):
        du = (g.DG[s] * nt(gm, g.WD[s])).astype(BF)
        g.DU[s] = du
        put_vector(s, 3, row_sum(du.astype(F32)))
        d = d + nt(du, g.WU[s])
    xhat = g.XH[...]
    put_vector(0, 1, row_sum(d * xhat))
    put_vector(0, 2, row_sum(d))
    d = d * g.ag_[...]
    d = g.RS[...] * (d - lane_mean(d) - xhat * lane_mean(d * xhat))
    g.DJ[...] = d
    gb = d.astype(BF)
    g.GB[...] = gb
    put_vector(0, 0, row_sum(gb.astype(F32)))
    put(down.acc, 0, tn(g.ACT[h], g.GM[...]).astype(BF))
    down.merge_core()
    tick(2)
    put(up.give, 0, tn(g.AB[...], g.DU[o]).astype(BF))
    up.send_core()
    for j in range(2):
        put(out.give, 128 * j * 4, nn(g.AT[2 * o + j], g.GB[...]).astype(BF))
    out.send_core()
    c_vec = links.copy(g.VEC.at[o], g.VECR, ctx.twin)
    put(up.acc, 0, tn(g.AB[...], g.DU[h]).astype(BF))
    for j in range(2):
        put(out.acc, 128 * j * 4, nn(g.AT[2 * h + j], g.GB[...]).astype(BF))
    tick(3)

    g.HQT[...] = g.HB[h].T
    g.SRCT[...] = g.SRC[pl.ds(pl.multiple_of(h * n, n), n), :].T
    for j in range(4):
        d = nt(g.WO[j // 2, 128 * (j % 2) : 128 * (j % 2) + 128, :], g.GB[...]).astype(BF)
        g.DOT[j] = d
        df = d.astype(F32)
        g.INNER[j, 0:1, :] = row_sum(df * g.AT[j].astype(F32))
        g.DOT2[j] = (df * g.INV[j, 0:1, :]).astype(BF)
    tick(4)
    up.merge_core()
    out.merge_core()
    tick(5)

    vec_stages = vec_groups(count)
    vec = Ctx()
    vec.k = 0

    def vec_start(value):
        bits = vec_stages[vec.k]
        digit, _ = down.parts[0]._digits(bits, 0)
        slots = g.VECS.at[vec.k]
        slots[digit] = value
        send, vec.sem = links.send_sem(), links.recv_sem()
        others = slots.at[pl.ds(0, 2 ** len(bits) - 1)]
        for mask in range(1, 2 ** len(bits)):
            _, row = down.parts[0]._digits(bits, mask)
            links.start(slots.at[digit], slots.at[digit], (row, h), send, vec.sem)
        links.open.append(functools.partial(wait_bytes, others, send))

    def vec_end():
        ways = 2 ** len(vec_stages[vec.k])
        wait_bytes(g.VECS.at[vec.k, pl.ds(0, ways - 1)], vec.sem)
        value = g.VECS[vec.k, 0]
        for i in range(1, ways):
            value = value + g.VECS[vec.k, i]
        vec.k += 1
        if vec.k < len(vec_stages):
            vec_start(value)
        else:
            g.vec[h] = value
            vec.copy = links.copy(g.vec.at[h], g.vec.at[h], ctx.twin)

    kv_copies = {}

    def attend_back(j):
        q, dot, dot2 = g.Q[j], g.DOT[j], g.DOT2[j]
        inner, factor = g.INNER[j, 0:1, :], g.INV[j, 0:1, :]
        dq = None
        for t in range(KEYS // 512):
            rows = slice(512 * t, 512 * t + 512)
            e = g.E[j, rows, :]
            upstream = nn(g.V[j, rows, :], dot)
            ds = (e.astype(F32) * ((upstream - inner) * factor)).astype(BF)
            g.DKV[j, rows, 0:128] = (nn(ds, q) * (DH**-0.5 / Q_SCALE)).astype(BF)
            g.DKV[j, rows, 128:256] = nt(e, dot2).astype(BF)
            part = tn(g.K[j, rows, :], ds)
            dq = part if dq is None else dq + part
        g.DQT[j] = (dq * DH**-0.5).astype(BF)
        other = pl.ds(pl.multiple_of(o * n, n), n)
        kv_copies[j] = links.copy(g.DKV.at[j, other], g.DKVR.at[j], ctx.twin)

    def merge_kv(j):
        kv_copies[j].wait_recv()
        mine = pl.ds(pl.multiple_of(h * n, n), n)
        g.DKVO[j] = (g.DKV[j, mine, :].astype(F32) + g.DKVR[j].astype(F32)).astype(BF)

    def q_grads(p, block):
        for j, ref in ((2 * o + p, block.give), (2 * h + p, block.acc)):
            put(ref, 0, nt(g.HQT[...], g.DQT[j]).astype(BF))

    def kv_grads(p, block):
        put(block.give, n, nn(g.SRCT[...], g.DKVO[2 * o + p]).astype(BF))
        block.send_core()
        put(block.acc, n, nn(g.SRCT[...], g.DKVO[2 * h + p]).astype(BF))

    attend_back(0)
    tick(6)
    attend_back(2)
    tick(7)
    q_grads(0, qkv0)
    attend_back(1)
    tick(8)
    merge_kv(0)
    merge_kv(2)
    kv_grads(0, qkv0)
    tick(9)
    attend_back(3)
    tick(10)
    qkv0.merge_core()
    c_vec.wait_recv()
    vec_start(g.VEC[h] + g.VECR[...])
    tick(11)
    q_grads(1, qkv1)
    for j in range(4):
        g.DQ[:, 128 * j : 128 * j + 128] = g.DQT[j].T
    dh = g.DJ[...] + nt(g.DQ[:, 0:256], g.WQKV[0, 0]) + nt(g.DQ[:, 256:512], g.WQKV[1, 0])
    tick(12)

    merge_kv(1)
    merge_kv(3)
    kvh = nt(g.DKVO[0], g.WKV[0])
    for j in range(1, 4):
        kvh = kvh + nt(g.DKVO[j], g.WKV[j])
    edge = CONTEXT_MAX - n
    g.DP[0] = kvh[edge:n, :].astype(BF)
    c_prompt = links.copy(g.DP.at[0], g.DP.at[1], ctx.twin)
    g.GH[0:edge, :] = (dh[0:edge] + kvh[0:edge]).astype(BF)
    first = jnp.where(h == 0, 1.0, 0.0)
    g.GH[edge:n, :] = (dh[edge:n] + kvh[edge:n] * first).astype(BF)
    tick(13)
    kv_grads(1, qkv1)
    tick(14)
    gh = g.GH[...]
    g.ENC[0:features, :] = nn(g.NL[h], gh)
    g.ENC[features:, :] = jnp.zeros_like(g.ENC[features:, :])
    bank_rows = g.bank.shape[0] // 2
    enc_at = bank_rows * 4
    for b in range(4):
        cols = slice(128 * b, 128 * b + 128)
        last.give[64 * b : 64 * b + 64, :] = g.ENC[pl.ds(pl.multiple_of(o * 64, 64), 64), cols].astype(BF)
        last.acc[enc_at + 64 * b : enc_at + 64 * b + 64, :] = g.ENC[
            pl.ds(pl.multiple_of(h * 64, 64), 64), cols
        ].astype(BF)
    last.send_core()
    c_prompt.wait_recv()
    put(
        last.acc,
        0,
        nn(g.SEL[pl.ds(pl.multiple_of(h * bank_rows, bank_rows), bank_rows), :], g.DP[o]).astype(BF),
    )
    tick(15)
    qkv1.merge_core()
    last.core_copy.wait_recv()
    rows = slice(enc_at, enc_at + 256)
    last.acc[rows, :] = (last.acc[rows, :].astype(F32) + last.got[...].astype(F32)).astype(BF)
    if last.n > enc_at + 256:
        last.acc[enc_at + 256 :, :] = jnp.zeros_like(last.acc[enc_at + 256 :, :])
    tick(16)
    vec_end()

    scale = g.COLS[:, 2:3]
    uf = nt(g.encw_[...], gh) * scale
    g.uf[...] = uf
    g.SQUARE[...] = jnp.zeros_like(g.SQUARE)
    rows = to_rows([lane_sum(uf), lane_sum(uf * (g.F[h] - g.COLS[:, 0:1]))])
    eb = row_sum(gh.astype(F32))
    g.LATE[0, :, 0:128] = rows[0:1]
    g.LATE[0, :, 128:256] = rows[1:2]
    g.LATE[0, :, 256:384] = eb[:, 0:128]
    g.LATE[1] = eb[:, 128:512]
    c_late = links.copy(g.LATE.at[o], g.LATER, ctx.twin)
    tick(17)
    c_late.wait_recv()
    g.LSUM[ctx.row] = g.LATE[h] + g.LATER[...]
    wait_late = share_slots(ctx, g.LSUM, ctx.row, everyone[0:-1:2])
    tick(18)
    while vec.k < len(vec_stages):
        vec_end()
    wait_late()
    late = g.LSUM[0]
    for k in range(1, count):
        late = late + g.LSUM[k]
    g.late[h] = late
    c_late_half = links.copy(g.late.at[h], g.late.at[h], ctx.twin)
    tick(19)
    rest = [p for b in blocks.values() for p in b.parts]
    while not all(p.done() for p in rest):
        for p in rest:
            if not p.done():
                p.advance()
                share_last()
    g.stat[...] = g.STAT[...]
    vec.copy.wait_recv()
    c_late_half.wait_recv()
    ctx.c_last.wait_recv()
    links.drain()
    assert (links.sent, links.received, loads.used) == sem_counts, (links.sent, links.received, loads.used)


def vec_groups(count):
    bits = [2**i for i in range(count.bit_length() - 1)]
    return [tuple(bits[i : i + 2]) for i in range(0, len(bits), 2)]


def finish_kernel(total_rows, names, *refs):
    g = Ctx()
    for name, ref in zip(names, refs, strict=True):
        setattr(g, name, ref)
    h = lax.axis_index("heads")
    features = g.feats.shape[0]
    copies = []

    def copy(src, dst):
        c = pltpu.make_async_copy(src, dst, g.sems.at[len(copies)])
        c.start()
        copies.append(c)
        return c

    outs = [copy(g.output, g.o_output)]
    c_feats = copy(g.feats, g.FEATS)
    up_at = g.rffn.shape[0] // 5 * 2

    late = jnp.concatenate([g.late[0], g.late[1]], axis=-1)
    vectors = [
        (0, 0, g.o_outb), (0, 1, g.o_ag), (0, 2, g.o_ash), (1, 0, g.o_downb), (1, 1, g.o_fg), (1, 2, g.o_fsh),
    ]

    def block(ref, first, rows):
        return ref[first : first + rows, :].astype(F32)

    for b in range(4):
        cols = slice(128 * b, 128 * b + 128)
        g.DOWN[:, cols] = block(g.rffn, 512 * b, 512)
    outs.append(copy(g.DOWN, g.o_down))
    for b in range(4):
        cols = slice(128 * b, 128 * b + 128)
        g.UP[:, cols] = block(g.rffn, up_at + 512 * b, 512)
    outs.append(copy(g.UP, g.o_up))
    for b in range(4):
        cols = slice(128 * b, 128 * b + 128)
        for j in range(2):
            g.OUT[128 * j : 128 * j + 128, cols] = block(g.rffn, 2 * up_at + 512 * j + 128 * b, 128)
    outs.append(copy(g.OUT, g.o_out))
    for c in range(3):
        for p in range(2):
            g.QKV[c, :, 128 * p : 128 * p + 128] = g.rqkv[p, 512 * c : 512 * c + 512, :].astype(F32)
    outs.append(copy(g.QKV, g.o_qkv))
    for b in range(4):
        cols = slice(128 * b, 128 * b + 128)
        for s in range(2):
            g.BANKV[256 * s : 256 * s + 256, cols] = g.rbank[s, 256 * b : 256 * b + 256, :].astype(F32)
        g.o_encw[0:64, cols] = g.rbank[0, 1024 + 64 * b : 1024 + 64 * b + 64, :].astype(F32)
        g.o_encw[64:features, cols] = g.rbank[1, 1024 + 64 * b : 1024 + 64 * b + features - 64, :].astype(F32)
        g.o_encb[:, cols] = late[:, 256 + 128 * b : 384 + 128 * b]
        for s, i, ref in vectors:
            ref[:, cols] = g.vec[s, 4 * i + b : 4 * i + b + 1, :]
        g.o_upb[:, cols] = g.vec[h, 12 + b : 13 + b, :]
    outs.append(copy(g.BANKV, g.o_bank))
    mean, inverse = g.stat[0:1, :], g.stat[1:2, :]
    b1, b2 = late[:, 0:128], late[:, 128:256]
    var_grad = -0.5 * inverse * inverse * inverse * b2
    g.SQUARE[...] = jnp.zeros_like(g.SQUARE)
    g.SQUARE[0:1, :] = inverse
    g.SQUARE[1:2, :] = (-inverse * b1 - 2.0 * mean * var_grad) / total_rows
    g.SQUARE[2:3, :] = 2.0 * var_grad / total_rows
    columns = g.SQUARE[...].T
    inverse, first, slope = [columns[0:features, i : i + 1] for i in range(3)]
    c_feats.wait()
    g.o_feats[...] = g.uf[...] * inverse + first + g.FEATS[...] * slope
    for c in outs:
        c.wait()


def per_device(
    feats,
    feature_mask,
    splits,
    prompt_index,
    prompt_bank,
    enc_weight,
    enc_bias,
    qkv_weight,
    out_weight,
    out_bias,
    attn_gain,
    attn_shift,
    up_weight,
    up_bias,
    down_weight,
    down_bias,
    ffn_gain,
    ffn_shift,
    cotangent,
):
    n, features = feats.shape
    count = lax.axis_size("rows")
    total_rows = n * count * lax.axis_size("heads")
    d = prompt_bank.shape[1]
    columns = feats.T
    args = [
        columns, feature_mask, splits, prompt_index, prompt_bank, enc_weight, enc_bias[None], qkv_weight, out_weight,
        out_bias[None], attn_gain[None], attn_shift[None], up_weight, up_bias[None], down_weight, down_bias[None],
        ffn_gain[None], ffn_shift[None], cotangent,
    ]
    vmem = pl.BlockSpec(memory_space=pltpu.VMEM)
    hbm = pl.BlockSpec(memory_space=pl.ANY)
    bits = [2**i for i in range(count.bit_length() - 1)]
    grain = 16 * count
    block_rows = {"d": 2048, "u": 2048, "o": 1024, "q": 1536, "r": 1536, "l": 1280}
    if count == 16:
        cuts, plan = CUTS, PLAN
    else:
        cuts, plan = {k: [(-(-r // grain) * grain, vec_groups(count))] for k, r in block_rows.items()}, []
    block_rows = {k: sum(r for r, _ in v) for k, v in cuts.items()}
    S = jax.ShapeDtypeStruct
    outs = {
        "output": S((n, d), F32),
        "uf": S((features, n), F32),
        "rffn": S((block_rows["d"] + block_rows["u"] + block_rows["o"], 128), BF),
        "rqkv": S((2, block_rows["q"], 128), BF),
        "rbank": S((2, block_rows["l"], 128), BF),
        "vec": S((2, 16, 128), F32),
        "late": S((2, 1, 384), F32),
        "stat": S((8, 128), F32),
    }
    V = pltpu.VMEM
    scratch = {k + "_": V(args[IN_NAMES.index(k)].shape, args[IN_NAMES.index(k)].dtype) for k in SMALL}
    scratch["splits_"] = pltpu.SMEM(splits.shape, splits.dtype)
    scratch |= {
        "F": V((2, features, n), F32),
        "WQKV": V((2, 3, d, 256), BF),
        "WO": V((2, 256, d), BF),
        "UB": V((2, 1, 512), F32),
        "WU": V((2, d, 512), BF),
        "WD": V((2, 512, d), BF),
        "BANKV": V(prompt_bank.shape, BF),
        "COT": V((n, d), F32),
        "SQUARE": V((128, 128), F32),
        "COLS": V((features, 128), F32),
        "LATE": V((2, 1, 384), F32),
        "LATER": V((1, 384), F32),
        "MOM": V((2 * count, 1, 256), F32),
        "LSUM": V((count, 1, 384), F32),
        "STAT": V((8, 128), F32),
        "VEC": V((2, 16, 128), F32),
        "VECR": V((16, 128), F32),
        "VECS": V((len(vec_groups(count)), 4, 16, 128), F32),
        "SEL": V((prompt_bank.shape[0], P_SIZE), BF),
        "SRC": V((KEYS, d), BF),
        "BIAS": V((CONTEXT_MAX - CONTEXT_MIN, 1), F32),
        "S": V((2, KEYS, n), F32),
        "WKV": V((4, d, 256), BF),
        "NL": V((2, features, n), BF),
        "HA": V((2, n, d), F32),
        "HB": V((2, n, d), BF),
        "Q": V((4, n, 128), BF),
        "K": V((4, KEYS, 128), BF),
        "V": V((4, KEYS, 128), BF),
        "E": V((4, KEYS, n), BF),
        "INV": V((4, 8, n), F32),
        "INNER": V((4, 8, n), F32),
        "AT": V((4, 128, n), BF),
        "A": V((n, d), BF),
        "XH": V((n, d), F32),
        "RS": V((n, 1), F32),
        "AB": V((n, d), BF),
        "DG": V((2, n, 512), F32),
        "ACT": V((2, n, 512), BF),
        "DU": V((2, n, 512), BF),
        "DJ": V((n, d), F32),
        "GM": V((n, d), BF),
        "GB": V((n, d), BF),
        "DOT": V((4, 128, n), BF),
        "DOT2": V((4, 128, n), BF),
        "DKV": V((4, KEYS, 256), BF),
        "DKVR": V((4, n, 256), BF),
        "DKVO": V((4, n, 256), BF),
        "DQT": V((4, 128, n), BF),
        "DQ": V((n, d), BF),
        "HQT": V((d, n), BF),
        "SRCT": V((d, n), BF),
        "DP": V((2, P_SIZE, d), BF),
        "GH": V((n, d), BF),
        "ENC": V((128, d), F32),
    }
    for k, r in block_rows.items():
        small = 256 if k == "l" else r
        scratch["CG" + k] = V((small, 128), BF)
        scratch["CR" + k] = V((small, 128), BF)
        scratch["CA" + k] = V((r, 128), BF)
        scratch["CV" + k] = V((2 * r, 128), BF)
    parts = [stages for v in cuts.values() for _, stages in v]
    once = 24 + len(vec_groups(count))
    sem_counts = (once + len(parts), once + sum(2 * len(s) - (len(s[-1]) == 1 or 0 in s[-1]) for s in parts), 8 + len(SMALL))
    for k, v in zip(("ssem", "rsem", "lsem"), sem_counts, strict=True):
        scratch[k] = pltpu.SemaphoreType.DMA((v,))
    names = IN_NAMES + OUT_NAMES + list(scratch)
    results = pl.pallas_call(
        functools.partial(layer_kernel, count, total_rows, cuts, plan, sem_counts, names),
        out_shape=[pltpu.VMEM(outs[k].shape, outs[k].dtype) for k in OUT_NAMES],
        in_specs=[hbm] * len(IN_NAMES),
        out_specs=[vmem] * len(OUT_NAMES),
        scratch_shapes=list(scratch.values()),
        compiler_params=pltpu.CompilerParams(
            collective_id=0, has_side_effects=True, vmem_limit_bytes=VMEM_LIMIT
        ),
        name="layer",
    )(*args)
    finals = {
        "o_output": S((n, d), F32),
        "o_feats": S((features, n), F32),
        "o_bank": S(prompt_bank.shape, F32),
        "o_encw": S(enc_weight.shape, F32),
        "o_encb": S((1, d), F32),
        "o_qkv": S(qkv_weight.shape, F32),
        "o_out": S(out_weight.shape, F32),
        "o_outb": S((1, d), F32),
        "o_ag": S((1, d), F32),
        "o_ash": S((1, d), F32),
        "o_up": S(up_weight.shape, F32),
        "o_upb": S((1, up_bias.shape[0]), F32),
        "o_down": S(down_weight.shape, F32),
        "o_downb": S((1, d), F32),
        "o_fg": S((1, d), F32),
        "o_fsh": S((1, d), F32),
    }
    moved = {"o_output", "o_bank", "o_qkv", "o_out", "o_up", "o_down"}
    work = {
        "FEATS": V((features, n), F32),
        "DOWN": V(down_weight.shape, F32),
        "UP": V(up_weight.shape, F32),
        "OUT": V(out_weight.shape, F32),
        "QKV": V(qkv_weight.shape, F32),
        "BANKV": V(prompt_bank.shape, F32),
        "SQUARE": V((128, 128), F32),
        "sems": pltpu.SemaphoreType.DMA((7,)),
    }
    final = pl.pallas_call(
        functools.partial(finish_kernel, total_rows, ["feats"] + OUT_NAMES + list(finals) + list(work)),
        out_shape=list(finals.values()),
        in_specs=[hbm] + [vmem] * len(OUT_NAMES),
        out_specs=[hbm if k in moved else vmem for k in finals],
        scratch_shapes=list(work.values()),
        compiler_params=pltpu.CompilerParams(vmem_limit_bytes=VMEM_LIMIT),
        name="finish",
    )(columns, *[pltpu.with_memory_space_constraint(v, pltpu.VMEM) for v in results])
    vectors = ("o_encb", "o_outb", "o_ag", "o_ash", "o_upb", "o_downb", "o_fg", "o_fsh")
    return tuple(
        v[0] if k in vectors else v.T if k == "o_feats" else v for k, v in zip(finals, final, strict=True)
    )


def solution(mesh):
    whole = P(("rows", "heads"), None)
    placed = (
        whole, P("rows", None), P("rows"), P("rows", None), P(), P(), P(), P(None, None, "heads"), P("heads", None),
        P(), P(), P(), P(None, "heads"), P("heads"), P("heads", None), P(), P(), P(), whole,
    )
    return jax.shard_map(
        per_device,
        mesh=mesh,
        in_specs=placed,
        out_specs=(
            whole, whole, P(), P(), P(), P(None, None, "heads"), P("heads", None), P(), P(), P(), P(None, "heads"),
            P("heads"), P("heads", None), P(), P(), P(),
        ),
        check_vma=False,
    )
```

```python
import functools
import math

import jax
import jax.numpy as jnp
from jax import lax
from jax.experimental import pallas as pl
from jax.experimental.pallas import tpu as pltpu
from jax.sharding import PartitionSpec as P

BF = jnp.bfloat16
F32 = jnp.float32
MESH = pl.DeviceIdType.MESH
DH = 128
P_SIZE = 128
CONTEXT_MAX = 896
CONTEXT_MIN = 640
KEYS = CONTEXT_MAX + P_SIZE
EPS = 1e-05
HALF_ROOT = math.sqrt(0.5)
PDF_SCALE = 1.0 / math.sqrt(2.0 * math.pi)
LOG2E = math.log2(math.e)
Q_SCALE = DH**-0.5 * LOG2E
VMEM_LIMIT = 52 * 2**20


def _dot(a, b, ca, cb):
    return lax.dot_general(a, b, (((ca,), (cb,)), ((), ())), preferred_element_type=F32)


def nn(a, b):
    return _dot(a, b, 1, 0)


def nt(a, b):
    return _dot(a, b, 1, 1)


def tn(a, b):
    return _dot(a, b, 0, 0)


def row_sum(v):
    return jnp.sum(v, axis=0, keepdims=True)


def lane_mean(v):
    return jnp.mean(v, axis=-1, keepdims=True)


class Links:
    def __init__(self, send, recv):
        self.send, self.recv, self.sent, self.received, self.open = send, recv, 0, 0, []

    def send_sem(self):
        self.sent += 1
        return self.send.at[self.sent - 1]

    def recv_sem(self):
        self.received += 1
        return self.recv.at[self.received - 1]

    def start(self, src, dst, device, send, recv):
        c = pltpu.make_async_remote_copy(
            src_ref=src, dst_ref=dst, send_sem=send, recv_sem=recv, device_id=device, device_id_type=MESH
        )
        c.start()
        return c

    def copy(self, src, dst, device):
        c = self.start(src, dst, device, self.send_sem(), self.recv_sem())
        self.open.append(c.wait_send)
        return c

    def drain(self):
        for wait in self.open:
            wait()
        self.open = []


def wait_bytes(ref, sem):
    pltpu.make_async_copy(ref, ref, sem).wait()


class Loads:
    def __init__(self, sems):
        self.sems, self.used = sems, 0

    def copy(self, src, dst):
        c = pltpu.make_async_copy(src, dst, self.sems.at[self.used])
        self.used += 1
        c.start()
        return c


class Part:
    def __init__(self, ctx, block, first, rows, stages):
        self.ctx, self.first, self.rows = ctx, first, rows
        self.stages = [tuple(b for b in s if b) for s in stages]
        self.whole = len(stages[-1]) == 1 or 0 in stages[-1]
        self.acc, self.recv, self.full = block.acc, block.recv, block.full
        self.at = -1

    def begin(self):
        self.base, self.len, self.off, self.k = self.first, self.rows, 2 * self.first, 0
        self.send_sem = self.ctx.links.send_sem()
        self._start_scatter()

    def _digits(self, bits, mask):
        digit, row = 0, self.ctx.row
        for i, b in enumerate(bits):
            bit = (self.ctx.row // b) % 2
            if mask >> i & 1:
                row = row + b * (1 - 2 * bit)
                bit = 1 - bit
            digit = digit * 2 + bit
        return digit, row

    def _wait(self, rows):
        view = self.full.at[pl.ds(0, rows)]
        wait_bytes(view, self.recv_sem)
        wait_bytes(view, self.send_sem)

    def _exchanges(self):
        return self.whole and self.k == len(self.stages) - 1

    def _slot(self, digit):
        return pl.ds(pl.multiple_of(self.off + digit * self.len, 16), self.len)

    def _start_scatter(self):
        bits = self.stages[self.k]
        ways = 2 ** len(bits)
        self.recv_sem = self.ctx.links.recv_sem()
        mine, _ = self._digits(bits, 0)
        q = self.len // ways
        for mask in range(1, ways):
            digit, row = self._digits(bits, mask)
            if self._exchanges():
                src = self.acc.at[pl.ds(pl.multiple_of(self.base, 16), self.len)]
                dst = self.recv.at[self._slot(mine)]
            else:
                src = self.acc.at[pl.ds(pl.multiple_of(self.base + digit * q, 16), q)]
                dst = self.recv.at[pl.ds(self.off + (mask - 1) * q, q)]
            self.ctx.links.start(src, dst, (row, self.ctx.head), self.send_sem, self.recv_sem)

    def _end_scatter(self):
        bits = self.stages[self.k]
        ways = 2 ** len(bits)
        digit, _ = self._digits(bits, 0)
        if self._exchanges():
            mine = pl.ds(pl.multiple_of(self.base, 16), self.len)
            self.recv[self._slot(digit), :] = self.acc[mine, :]
            self._wait((ways - 1) * self.len)
            total = self.recv[self._slot(0), :].astype(F32)
            for i in range(1, ways):
                total = total + self.recv[self._slot(i), :].astype(F32)
            self.full[mine, :] = total.astype(BF)
            self._start_gather()
            return
        q = self.len // ways
        self.base = self.base + digit * q
        mine = pl.ds(pl.multiple_of(self.base, 16), q)
        self._wait((ways - 1) * q)
        total = self.acc[mine, :].astype(F32)
        for i in range(ways - 1):
            total = total + self.recv[pl.ds(self.off + i * q, q), :].astype(F32)
        self.off += (ways - 1) * q
        self.len = q
        self.k += 1
        if self.k < len(self.stages):
            self.acc[mine, :] = total.astype(BF)
            self._start_scatter()
        else:
            self.full[mine, :] = total.astype(BF)
            self._start_gather()

    def _start_gather(self):
        if self.k == 0:
            return
        bits = self.stages[self.k - 1]
        mine = self.full.at[pl.ds(pl.multiple_of(self.base, 16), self.len)]
        self.recv_sem = self.ctx.links.recv_sem()
        for mask in range(1, 2 ** len(bits)):
            _, row = self._digits(bits, mask)
            self.ctx.links.start(mine, mine, (row, self.ctx.head), self.send_sem, self.recv_sem)

    def _end_gather(self):
        bits = self.stages[self.k - 1]
        ways = 2 ** len(bits)
        self._wait((ways - 1) * self.len)
        digit, _ = self._digits(bits, 0)
        self.base = self.base - digit * self.len
        self.len = self.len * ways
        self.k -= 1
        self._start_gather()

    def steps(self):
        return 2 * len(self.stages) - self.whole

    def done(self):
        return self.at == self.steps()

    def advance(self):
        if self.at < 0:
            self.begin()
        elif self.at < len(self.stages):
            self._end_scatter()
        elif not self.done():
            self._end_gather()
        self.at += 1


class Block:
    def __init__(self, ctx, refs, cuts):
        self.ctx = ctx
        self.give, self.got, self.acc, self.recv, self.full = refs
        self.n = self.acc.shape[0]
        self.parts, first = [], 0
        for rows, stages in cuts:
            self.parts.append(Part(ctx, self, first, rows, stages))
            first += rows

    def send_core(self):
        self.core_copy = self.ctx.links.copy(self.give, self.got, self.ctx.twin)

    def merge_core(self):
        self.core_copy.wait_recv()
        for part in self.parts:
            rows = slice(part.first, part.first + part.rows)
            self.acc[rows, :] = (self.acc[rows, :].astype(F32) + self.got[rows, :].astype(F32)).astype(BF)


class Ctx:
    pass


def others_of(ctx, count):
    steps = sorted(range(1, count), key=lambda k: min(k, count - k))
    rows = [lax.rem(ctx.row + k, count) for k in steps]
    return [(row, head) for row in rows for head in (ctx.head, 1 - ctx.head)] + [ctx.twin]


def share_slots(ctx, slots, place, devices):
    mine = slots.at[place]
    send, recv = ctx.links.send_sem(), ctx.links.recv_sem()
    for device in devices:
        ctx.links.start(mine, mine, device, send, recv)
    others = slots.at[pl.ds(0, len(devices))]
    ctx.links.open.append(functools.partial(wait_bytes, others, send))
    return functools.partial(wait_bytes, others, recv)


SMALL = [
    "mask", "splits", "pidx", "encw", "encb", "outb", "ag", "ash", "downb", "fg", "fsh",
]
IN_NAMES = [
    "feats", "mask", "splits", "pidx", "bank", "encw", "encb", "qkvw", "outw", "outb", "ag", "ash", "upw",
    "upb", "downw", "downb", "fg", "fsh", "cot",
]
OUT_NAMES = [
    "output", "uf", "rffn", "rqkv", "rbank", "vec", "late", "stat",
]
CUTS = {
    "d": [(1024, [(2,), (1,), (4, 8)]), (1024, [(1, 2), (4, 8)])],
    "u": [(1024, [(1,), (4,), (2, 8)]), (1024, [(4,), (2,), (1,), (8,)])],
    "o": [(1024, [(1, 2), (8,), (4,)])],
    "q": [(256, [(2,), (1,), (4,), (8,)]), (512, [(1,), (2,), (4,), (8,)]), (768, [(4,), (1, 2), (8,)])],
    "r": [(768, [(1,), (2, 4), (8,)]), (768, [(2,), (1, 4), (8,)])],
    "l": [(768, [(4,), (1, 2), (8,)]), (512, [(1, 2), (4, 8)])],
}
PLAN = [
    [],
    [],
    ["d1", "d0"],
    [],
    [],
    ["u1", "u0", "o0"],
    [],
    ["d1"],
    [],
    ["d0", "u1", "u0"],
    ["d1"],
    ["o0", "q1", "q0", "q2"],
    ["d0", "u1", "u0"],
    ["d1", "q0", "q1"],
    ["o0"],
    ["u1", "q2", "d0"],
    ["u0", "r0", "l0", "r1", "l1", "o0"],
    [],
    ["d1", "q0", "q1", "u1", "q2", "d0", "r0", "u0", "l0", "r1", "q0", "o0", "q1", "u1", "l1", "q2", "d0", "r0", "l0", "u0", "r1", "q0", "q1", "l1"],
    ["r0", "l0", "o0", "u1", "q0", "q1", "r1", "q2", "l1", "u0", "d0", "q0", "r0", "u1", "l0", "r1", "q1", "l1", "q2", "q0", "r0", "l0", "q1", "r1"],
]


def layer_kernel(count, total_rows, cuts, plan, sem_counts, names, *refs):
    g = Ctx()
    for name, ref in zip(names, refs, strict=True):
        setattr(g, name, ref)
    features, n = g.feats.shape
    ctx = Ctx()
    ctx.row, ctx.head = lax.axis_index("rows"), lax.axis_index("heads")
    h = ctx.head
    o = 1 - h
    ctx.twin = (ctx.row, o)
    ctx.links = links = Links(g.ssem, g.rsem)
    loads = Loads(g.lsem)

    l_feats = loads.copy(g.feats, g.F.at[h])
    own = {
        "qkv": (g.qkvw, g.WQKV.at[h]),
        "out": (g.outw, g.WO.at[h]),
        "upb": (g.upb, g.UB.at[h]),
        "up": (g.upw, g.WU.at[h]),
        "down": (g.downw, g.WD.at[h]),
    }
    everyone = others_of(ctx, count)
    barrier = pltpu.get_barrier_semaphore()
    for device in everyone:
        pl.semaphore_signal(barrier, inc=1, device_id=device, device_id_type=MESH)
    l_small = [loads.copy(getattr(g, k), getattr(g, k + "_")) for k in SMALL]
    l_bank = loads.copy(g.bank, g.BANKV)
    l_own = {k: loads.copy(*v) for k, v in own.items()}
    l_cot = loads.copy(g.cot, g.COT)

    def to_rows(columns):
        for i, c in enumerate(columns):
            g.SQUARE[0:features, i : i + 1] = c
        return g.SQUARE[...].T[0:8, :]

    def lane_sum(v):
        return jnp.sum(v, axis=-1, keepdims=True)

    def put_vector(half, i, value):
        for b in range(4):
            g.VEC[half, 4 * i + b : 4 * i + b + 1, :] = value[:, 128 * b : 128 * b + 128]

    g.SQUARE[...] = jnp.zeros_like(g.SQUARE)
    l_feats.wait()
    f = g.F[h]
    rows = to_rows([lane_sum(f), lane_sum(f * f)])
    place = ctx.row * 2 + h
    g.MOM[place, :, 0:128] = rows[0:1]
    g.MOM[place, :, 128:256] = rows[1:2]
    pl.semaphore_wait(barrier, len(everyone))
    wait_moments = share_slots(ctx, g.MOM, place, everyone)
    c_feats = links.copy(g.feats, g.F.at[h], ctx.twin)
    c_own = {"qkv": links.copy(*own["qkv"], ctx.twin)}
    c_own |= {k: links.copy(*v, ctx.twin) for k, v in own.items() if k != "qkv"}

    for c in l_small:
        c.wait()
    selector = lax.broadcasted_iota(jnp.int32, (g.bank.shape[0], P_SIZE), 0) == g.pidx_[...]
    g.SEL[...] = jnp.where(selector, 1.0, 0.0).astype(BF)
    l_bank.wait()
    g.SRC[CONTEXT_MAX:KEYS, :] = tn(g.SEL[...], g.BANKV[...]).astype(BF)
    maybe = lax.broadcasted_iota(jnp.int32, (CONTEXT_MAX - CONTEXT_MIN, 1), 0) + CONTEXT_MIN
    g.BIAS[...] = jnp.where(maybe < g.splits_[0], 0.0, -1e30)
    live = g.mask_[...].astype(F32)
    scale = live * jnp.sqrt(features / jnp.sum(live, axis=-1, keepdims=True))
    g.STAT[...] = jnp.zeros_like(g.STAT)
    g.V[:, :, 128:] = jnp.ones_like(g.V[:, :, 128:])
    g.STAT[2:3, 0:features] = scale
    for c in l_own.values():
        c.wait()
    c_own["qkv"].wait_recv()
    for j in range(4):
        s, w = j // 2, pl.ds(128 * (j % 2), 128)
        g.WKV[j, :, 0:128] = g.WQKV[s, 1, :, w]
        g.WKV[j, :, 128:256] = g.WQKV[s, 2, :, w]

    c_feats.wait_recv()
    wait_moments()
    moments = g.MOM[0]
    for k in range(1, 2 * count):
        moments = moments + g.MOM[k]
    mean = moments[:, 0:128] / total_rows
    var = moments[:, 128:256] / total_rows - mean * mean
    g.STAT[0:1, :] = mean
    g.STAT[1:2, :] = lax.rsqrt(var + EPS)
    g.SQUARE[0:8, :] = g.STAT[...]
    columns = g.SQUARE[...].T
    mean, inverse, scale = [columns[0:features, i : i + 1] for i in range(3)]
    g.COLS[...] = columns[0:features, :]

    for s in range(2):
        g.NL[s] = (((g.F[s] - mean) * inverse) * scale).astype(BF)
        hidden = tn(g.NL[s], g.encw_[...]) + g.encb_[...]
        g.HA[s] = hidden
        g.HB[s] = hidden.astype(BF)
    g.SRC[0:n, :] = g.HB[0]
    g.SRC[n:CONTEXT_MAX, :] = g.HB[1, 0 : CONTEXT_MAX - n, :]

    for s in range(2):
        q = (nn(g.HB[h], g.WQKV[s, 0]) * Q_SCALE).astype(BF)
        for j in range(2):
            g.Q[2 * s + j] = q[:, 128 * j : 128 * j + 128]

    for j in range(4):
        kv = nn(g.SRC[...], g.WKV[j]).astype(BF)
        g.K[j] = kv[:, 0:128]
        g.V[j, :, 0:128] = kv[:, 128:256]

    for j in range(5):
        if j < 4:
            scores = nt(g.K[j], g.Q[j])
            g.S[j % 2, 0:CONTEXT_MIN, :] = scores[0:CONTEXT_MIN]
            g.S[j % 2, CONTEXT_MIN:CONTEXT_MAX, :] = scores[CONTEXT_MIN:CONTEXT_MAX] + g.BIAS[...]
            g.S[j % 2, CONTEXT_MAX:KEYS, :] = scores[CONTEXT_MAX:KEYS]
        if j > 0:
            p = j - 1
            scores = g.S[p % 2]
            e = jnp.exp2(scores - jnp.max(scores, axis=0, keepdims=True))
            e = e.astype(BF)
            g.E[p] = e
            mixed = tn(g.V[p], e)
            inv = 1.0 / mixed[128:129]
            g.INV[p, 0:1, :] = inv
            g.AT[p] = (mixed[0:128] * inv).astype(BF)

    c_own["out"].wait_recv()
    c_own["up"].wait_recv()
    c_own["upb"].wait_recv()
    c_own["down"].wait_recv()
    for j in range(4):
        g.A[:, 128 * j : 128 * j + 128] = g.AT[j].T
    l_cot.wait()

    branch = nn(g.A[:, 0:256], g.WO[0]) + nn(g.A[:, 256:512], g.WO[1]) + g.outb_[...]
    joined = g.HA[h] + branch
    center = joined - lane_mean(joined)
    rstd = lax.rsqrt(lane_mean(center * center) + EPS)
    xhat = center * rstd
    after = xhat * g.ag_[...] + g.ash_[...]
    g.XH[...] = xhat
    g.RS[...] = rstd
    low = after.astype(BF)
    g.AB[...] = low
    mixed = g.downb_[...]
    for s in range(2):
        u = nn(low, g.WU[s]) + g.UB[s]
        phi = 0.5 * (1.0 + lax.erf(u * HALF_ROOT))
        g.DG[s] = phi + u * (jnp.exp2(u * u * (-0.5 * LOG2E)) * PDF_SCALE)
        act = (u * phi).astype(BF)
        g.ACT[s] = act
        mixed = mixed + nn(act, g.WD[s])
    joined = after + mixed
    center = joined - lane_mean(joined)
    rstd = lax.rsqrt(lane_mean(center * center) + EPS)
    xhat = center * rstd
    g.output[...] = xhat * g.fg_[...] + g.fsh_[...]
    ct = g.COT[...]
    d = ct * g.fg_[...]
    d = rstd * (d - lane_mean(d) - xhat * lane_mean(d * xhat))
    g.DJ[...] = d
    gm = d.astype(BF)
    g.GM[...] = gm
    put_vector(1, 0, row_sum(gm.astype(F32)))
    put_vector(1, 1, row_sum(ct * xhat))
    put_vector(1, 2, row_sum(ct))

    def put(ref, first, value):
        r = value.shape[0]
        for b in range(value.shape[1] // 128):
            ref[first + r * b : first + r * b + r, :] = value[:, 128 * b : 128 * b + 128]

    rows_of = {k: sum(r for r, _ in v) for k, v in cuts.items()}
    fulls, at = {"l": g.rbank.at[h]}, 0
    for k in ("d", "u", "o"):
        fulls[k] = g.rffn.at[pl.ds(at, rows_of[k])]
        at += rows_of[k]
    for i, k in enumerate(("q", "r")):
        fulls[k] = g.rqkv.at[i]
    blocks = {
        k: Block(ctx, [getattr(g, p + k) for p in ("CG", "CR", "CA", "CV")] + [fulls[k]], v)
        for k, v in cuts.items()
    }
    down, up, out, qkv0, qkv1, last = blocks.values()

    def tick(i):
        for k in plan[i] if i < len(plan) else []:
            blocks[k[0]].parts[int(k[1])].advance()
            share_last()

    def share_last():
        if not hasattr(ctx, "c_last") and all(p.done() for p in last.parts):
            ctx.c_last = links.copy(g.rbank.at[h], g.rbank.at[h], ctx.twin)

    put(down.give, 0, tn(g.ACT[o], g.GM[...]).astype(BF))
    down.send_core()

    gm = g.GM[...]
    d = g.DJ[...]
    for s in range(2):
        du = (g.DG[s] * nt(gm, g.WD[s])).astype(BF)
        g.DU[s] = du
        put_vector(s, 3, row_sum(du.astype(F32)))
        d = d + nt(du, g.WU[s])
    xhat = g.XH[...]
    put_vector(0, 1, row_sum(d * xhat))
    put_vector(0, 2, row_sum(d))
    d = d * g.ag_[...]
    d = g.RS[...] * (d - lane_mean(d) - xhat * lane_mean(d * xhat))
    g.DJ[...] = d
    gb = d.astype(BF)
    g.GB[...] = gb
    put_vector(0, 0, row_sum(gb.astype(F32)))
    put(down.acc, 0, tn(g.ACT[h], g.GM[...]).astype(BF))
    down.merge_core()
    tick(2)
    put(up.give, 0, tn(g.AB[...], g.DU[o]).astype(BF))
    up.send_core()
    for j in range(2):
        put(out.give, 128 * j * 4, nn(g.AT[2 * o + j], g.GB[...]).astype(BF))
    out.send_core()
    c_vec = links.copy(g.VEC.at[o], g.VECR, ctx.twin)
    put(up.acc, 0, tn(g.AB[...], g.DU[h]).astype(BF))
    for j in range(2):
        put(out.acc, 128 * j * 4, nn(g.AT[2 * h + j], g.GB[...]).astype(BF))
    tick(3)

    g.HQT[...] = g.HB[h].T
    g.SRCT[...] = g.SRC[pl.ds(pl.multiple_of(h * n, n), n), :].T
    for j in range(4):
        d = nt(g.WO[j // 2, 128 * (j % 2) : 128 * (j % 2) + 128, :], g.GB[...]).astype(BF)
        g.DOT[j] = d
        df = d.astype(F32)
        g.INNER[j, 0:1, :] = row_sum(df * g.AT[j].astype(F32))
        g.DOT2[j] = (df * g.INV[j, 0:1, :]).astype(BF)
    tick(4)
    up.merge_core()
    out.merge_core()
    tick(5)

    vec_stages = vec_groups(count)
    vec = Ctx()
    vec.k = 0

    def vec_start(value):
        bits = vec_stages[vec.k]
        digit, _ = down.parts[0]._digits(bits, 0)
        slots = g.VECS.at[vec.k]
        slots[digit] = value
        send, vec.sem = links.send_sem(), links.recv_sem()
        others = slots.at[pl.ds(0, 2 ** len(bits) - 1)]
        for mask in range(1, 2 ** len(bits)):
            _, row = down.parts[0]._digits(bits, mask)
            links.start(slots.at[digit], slots.at[digit], (row, h), send, vec.sem)
        links.open.append(functools.partial(wait_bytes, others, send))

    def vec_end():
        ways = 2 ** len(vec_stages[vec.k])
        wait_bytes(g.VECS.at[vec.k, pl.ds(0, ways - 1)], vec.sem)
        value = g.VECS[vec.k, 0]
        for i in range(1, ways):
            value = value + g.VECS[vec.k, i]
        vec.k += 1
        if vec.k < len(vec_stages):
            vec_start(value)
        else:
            g.vec[h] = value
            vec.copy = links.copy(g.vec.at[h], g.vec.at[h], ctx.twin)

    kv_copies = {}

    def attend_back(j):
        q, dot, dot2 = g.Q[j], g.DOT[j], g.DOT2[j]
        inner, factor = g.INNER[j, 0:1, :], g.INV[j, 0:1, :]
        dq = None
        for t in range(KEYS // 512):
            rows = slice(512 * t, 512 * t + 512)
            e = g.E[j, rows, :]
            upstream = nn(g.V[j, rows, 0:128], dot)
            ds = (e.astype(F32) * ((upstream - inner) * factor)).astype(BF)
            g.DKV[j, rows, 0:128] = (nn(ds, q) * (DH**-0.5 / Q_SCALE)).astype(BF)
            g.DKV[j, rows, 128:256] = nt(e, dot2).astype(BF)
            part = tn(g.K[j, rows, :], ds)
            dq = part if dq is None else dq + part
        g.DQT[j] = (dq * DH**-0.5).astype(BF)
        other = pl.ds(pl.multiple_of(o * n, n), n)
        kv_copies[j] = links.copy(g.DKV.at[j, other], g.DKVR.at[j], ctx.twin)

    def merge_kv(j):
        kv_copies[j].wait_recv()
        mine = pl.ds(pl.multiple_of(h * n, n), n)
        g.DKVO[j] = (g.DKV[j, mine, :].astype(F32) + g.DKVR[j].astype(F32)).astype(BF)

    def q_grads(p, block):
        for j, ref in ((2 * o + p, block.give), (2 * h + p, block.acc)):
            put(ref, 0, nt(g.HQT[...], g.DQT[j]).astype(BF))

    def kv_grads(p, block):
        put(block.give, n, nn(g.SRCT[...], g.DKVO[2 * o + p]).astype(BF))
        block.send_core()
        put(block.acc, n, nn(g.SRCT[...], g.DKVO[2 * h + p]).astype(BF))

    attend_back(0)
    tick(6)
    attend_back(2)
    tick(7)
    q_grads(0, qkv0)
    attend_back(1)
    tick(8)
    merge_kv(0)
    merge_kv(2)
    kv_grads(0, qkv0)
    tick(9)
    attend_back(3)
    tick(10)
    qkv0.merge_core()
    c_vec.wait_recv()
    vec_start(g.VEC[h] + g.VECR[...])
    tick(11)
    q_grads(1, qkv1)
    for j in range(4):
        g.DQ[:, 128 * j : 128 * j + 128] = g.DQT[j].T
    dh = g.DJ[...] + nt(g.DQ[:, 0:256], g.WQKV[0, 0]) + nt(g.DQ[:, 256:512], g.WQKV[1, 0])
    tick(12)

    merge_kv(1)
    merge_kv(3)
    kvh = nt(g.DKVO[0], g.WKV[0])
    for j in range(1, 4):
        kvh = kvh + nt(g.DKVO[j], g.WKV[j])
    edge = CONTEXT_MAX - n
    g.DP[0] = kvh[edge:n, :].astype(BF)
    c_prompt = links.copy(g.DP.at[0], g.DP.at[1], ctx.twin)
    g.GH[0:edge, :] = (dh[0:edge] + kvh[0:edge]).astype(BF)
    first = jnp.where(h == 0, 1.0, 0.0)
    g.GH[edge:n, :] = (dh[edge:n] + kvh[edge:n] * first).astype(BF)
    tick(13)
    kv_grads(1, qkv1)
    tick(14)
    gh = g.GH[...]
    g.ENC[0:features, :] = nn(g.NL[h], gh)
    g.ENC[features:, :] = jnp.zeros_like(g.ENC[features:, :])
    bank_rows = g.bank.shape[0] // 2
    enc_at = bank_rows * 4
    for b in range(4):
        cols = slice(128 * b, 128 * b + 128)
        last.give[64 * b : 64 * b + 64, :] = g.ENC[pl.ds(pl.multiple_of(o * 64, 64), 64), cols].astype(BF)
        last.acc[enc_at + 64 * b : enc_at + 64 * b + 64, :] = g.ENC[
            pl.ds(pl.multiple_of(h * 64, 64), 64), cols
        ].astype(BF)
    last.send_core()
    c_prompt.wait_recv()
    put(
        last.acc,
        0,
        nn(g.SEL[pl.ds(pl.multiple_of(h * bank_rows, bank_rows), bank_rows), :], g.DP[o]).astype(BF),
    )
    tick(15)
    qkv1.merge_core()
    last.core_copy.wait_recv()
    rows = slice(enc_at, enc_at + 256)
    last.acc[rows, :] = (last.acc[rows, :].astype(F32) + last.got[...].astype(F32)).astype(BF)
    if last.n > enc_at + 256:
        last.acc[enc_at + 256 :, :] = jnp.zeros_like(last.acc[enc_at + 256 :, :])
    tick(16)
    vec_end()

    scale = g.COLS[:, 2:3]
    uf = nt(g.encw_[...], gh) * scale
    g.uf[...] = uf
    g.SQUARE[...] = jnp.zeros_like(g.SQUARE)
    rows = to_rows([lane_sum(uf), lane_sum(uf * (g.F[h] - g.COLS[:, 0:1]))])
    eb = row_sum(gh.astype(F32))
    g.LATE[0, :, 0:128] = rows[0:1]
    g.LATE[0, :, 128:256] = rows[1:2]
    g.LATE[0, :, 256:384] = eb[:, 0:128]
    g.LATE[1] = eb[:, 128:512]
    c_late = links.copy(g.LATE.at[o], g.LATER, ctx.twin)
    tick(17)
    c_late.wait_recv()
    g.LSUM[ctx.row] = g.LATE[h] + g.LATER[...]
    wait_late = share_slots(ctx, g.LSUM, ctx.row, everyone[0:-1:2])
    tick(18)
    while vec.k < len(vec_stages):
        vec_end()
    wait_late()
    late = g.LSUM[0]
    for k in range(1, count):
        late = late + g.LSUM[k]
    g.late[h] = late
    c_late_half = links.copy(g.late.at[h], g.late.at[h], ctx.twin)
    links.drain()
    tick(19)
    rest = [p for b in blocks.values() for p in b.parts]
    while not all(p.done() for p in rest):
        for p in rest:
            if not p.done():
                p.advance()
                share_last()
    g.stat[...] = g.STAT[...]
    vec.copy.wait_recv()
    c_late_half.wait_recv()
    ctx.c_last.wait_recv()
    links.drain()
    assert (links.sent, links.received, loads.used) == sem_counts, (links.sent, links.received, loads.used)


def vec_groups(count):
    bits = [2**i for i in range(count.bit_length() - 1)]
    return [tuple(bits[i : i + 2]) for i in range(0, len(bits), 2)]


def finish_kernel(total_rows, names, *refs):
    g = Ctx()
    for name, ref in zip(names, refs, strict=True):
        setattr(g, name, ref)
    h = lax.axis_index("heads")
    features = g.feats.shape[0]
    copies = []

    def copy(src, dst):
        c = pltpu.make_async_copy(src, dst, g.sems.at[len(copies)])
        c.start()
        copies.append(c)
        return c

    def done(*results):
        for k in results:
            copy(getattr(g, "s_" + k), getattr(g, "o_" + k))

    copy(g.output, g.o_output)
    c_feats = copy(g.feats, g.FEATS)
    up_at = g.rffn.shape[0] // 5 * 2

    def block(ref, first, rows):
        return ref[first : first + rows, :].astype(F32)

    columns = [slice(128 * b, 128 * b + 128) for b in range(4)]
    for b, cols in enumerate(columns):
        g.s_down[:, cols] = block(g.rffn, 512 * b, 512)
    done("down")
    for b, cols in enumerate(columns):
        g.s_up[:, cols] = block(g.rffn, up_at + 512 * b, 512)
    done("up")
    for c in range(3):
        for p in range(2):
            g.s_qkv[c, :, 128 * p : 128 * p + 128] = g.rqkv[p, 512 * c : 512 * c + 512, :].astype(F32)
    done("qkv")
    for b, cols in enumerate(columns):
        for s in range(2):
            g.s_bank[256 * s : 256 * s + 256, cols] = g.rbank[s, 256 * b : 256 * b + 256, :].astype(F32)
    done("bank")
    for b, cols in enumerate(columns):
        for j in range(2):
            g.s_out[128 * j : 128 * j + 128, cols] = block(g.rffn, 2 * up_at + 512 * j + 128 * b, 128)
    done("out")
    late = jnp.concatenate([g.late[0], g.late[1]], axis=-1)
    vectors = [(0, 0, "outb"), (0, 1, "ag"), (0, 2, "ash"), (1, 0, "downb"), (1, 1, "fg"), (1, 2, "fsh"), (h, 3, "upb")]
    for b, cols in enumerate(columns):
        g.s_encw[0:64, cols] = g.rbank[0, 1024 + 64 * b : 1024 + 64 * b + 64, :].astype(F32)
        g.s_encw[64:features, cols] = g.rbank[1, 1024 + 64 * b : 1024 + 64 * b + features - 64, :].astype(F32)
        g.s_encb[:, cols] = late[:, 256 + 128 * b : 384 + 128 * b]
        for s, i, k in vectors:
            getattr(g, "s_" + k)[:, cols] = g.vec[s, 4 * i + b : 4 * i + b + 1, :]
    done("encw", "encb", *[k for _, _, k in vectors])
    mean, inverse = g.stat[0:1, :], g.stat[1:2, :]
    b1, b2 = late[:, 0:128], late[:, 128:256]
    var_grad = -0.5 * inverse * inverse * inverse * b2
    g.SQUARE[...] = jnp.zeros_like(g.SQUARE)
    g.SQUARE[0:1, :] = inverse
    g.SQUARE[1:2, :] = (-inverse * b1 - 2.0 * mean * var_grad) / total_rows
    g.SQUARE[2:3, :] = 2.0 * var_grad / total_rows
    turned = g.SQUARE[...].T
    inverse, first, slope = [turned[0:features, i : i + 1] for i in range(3)]
    c_feats.wait()
    g.s_feats[...] = g.uf[...] * inverse + first + g.FEATS[...] * slope
    done("feats")
    for c in copies:
        if c is not c_feats:
            c.wait()


def per_device(
    feats,
    feature_mask,
    splits,
    prompt_index,
    prompt_bank,
    enc_weight,
    enc_bias,
    qkv_weight,
    out_weight,
    out_bias,
    attn_gain,
    attn_shift,
    up_weight,
    up_bias,
    down_weight,
    down_bias,
    ffn_gain,
    ffn_shift,
    cotangent,
):
    n, features = feats.shape
    count = lax.axis_size("rows")
    total_rows = n * count * lax.axis_size("heads")
    d = prompt_bank.shape[1]
    columns = feats.T
    args = [
        columns, feature_mask, splits, prompt_index, prompt_bank, enc_weight, enc_bias[None], qkv_weight, out_weight,
        out_bias[None], attn_gain[None], attn_shift[None], up_weight, up_bias[None], down_weight, down_bias[None],
        ffn_gain[None], ffn_shift[None], cotangent,
    ]
    vmem = pl.BlockSpec(memory_space=pltpu.VMEM)
    hbm = pl.BlockSpec(memory_space=pl.ANY)
    bits = [2**i for i in range(count.bit_length() - 1)]
    grain = 16 * count
    block_rows = {"d": 2048, "u": 2048, "o": 1024, "q": 1536, "r": 1536, "l": 1280}
    if count == 16:
        cuts, plan = CUTS, PLAN
    else:
        cuts, plan = {k: [(-(-r // grain) * grain, vec_groups(count))] for k, r in block_rows.items()}, []
    block_rows = {k: sum(r for r, _ in v) for k, v in cuts.items()}
    S = jax.ShapeDtypeStruct
    outs = {
        "output": S((n, d), F32),
        "uf": S((features, n), F32),
        "rffn": S((block_rows["d"] + block_rows["u"] + block_rows["o"], 128), BF),
        "rqkv": S((2, block_rows["q"], 128), BF),
        "rbank": S((2, block_rows["l"], 128), BF),
        "vec": S((2, 16, 128), F32),
        "late": S((2, 1, 384), F32),
        "stat": S((8, 128), F32),
    }
    V = pltpu.VMEM
    scratch = {k + "_": V(args[IN_NAMES.index(k)].shape, args[IN_NAMES.index(k)].dtype) for k in SMALL}
    scratch["splits_"] = pltpu.SMEM(splits.shape, splits.dtype)
    scratch |= {
        "F": V((2, features, n), F32),
        "WQKV": V((2, 3, d, 256), BF),
        "WO": V((2, 256, d), BF),
        "UB": V((2, 1, 512), F32),
        "WU": V((2, d, 512), BF),
        "WD": V((2, 512, d), BF),
        "BANKV": V(prompt_bank.shape, BF),
        "COT": V((n, d), F32),
        "SQUARE": V((128, 128), F32),
        "COLS": V((features, 128), F32),
        "LATE": V((2, 1, 384), F32),
        "LATER": V((1, 384), F32),
        "MOM": V((2 * count, 1, 256), F32),
        "LSUM": V((count, 1, 384), F32),
        "STAT": V((8, 128), F32),
        "VEC": V((2, 16, 128), F32),
        "VECR": V((16, 128), F32),
        "VECS": V((len(vec_groups(count)), 4, 16, 128), F32),
        "SEL": V((prompt_bank.shape[0], P_SIZE), BF),
        "SRC": V((KEYS, d), BF),
        "BIAS": V((CONTEXT_MAX - CONTEXT_MIN, 1), F32),
        "S": V((2, KEYS, n), F32),
        "WKV": V((4, d, 256), BF),
        "NL": V((2, features, n), BF),
        "HA": V((2, n, d), F32),
        "HB": V((2, n, d), BF),
        "Q": V((4, n, 128), BF),
        "K": V((4, KEYS, 128), BF),
        "V": V((4, KEYS, 144), BF),
        "E": V((4, KEYS, n), BF),
        "INV": V((4, 8, n), F32),
        "INNER": V((4, 8, n), F32),
        "AT": V((4, 128, n), BF),
        "A": V((n, d), BF),
        "XH": V((n, d), F32),
        "RS": V((n, 1), F32),
        "AB": V((n, d), BF),
        "DG": V((2, n, 512), F32),
        "ACT": V((2, n, 512), BF),
        "DU": V((2, n, 512), BF),
        "DJ": V((n, d), F32),
        "GM": V((n, d), BF),
        "GB": V((n, d), BF),
        "DOT": V((4, 128, n), BF),
        "DOT2": V((4, 128, n), BF),
        "DKV": V((4, KEYS, 256), BF),
        "DKVR": V((4, n, 256), BF),
        "DKVO": V((4, n, 256), BF),
        "DQT": V((4, 128, n), BF),
        "DQ": V((n, d), BF),
        "HQT": V((d, n), BF),
        "SRCT": V((d, n), BF),
        "DP": V((2, P_SIZE, d), BF),
        "GH": V((n, d), BF),
        "ENC": V((128, d), F32),
    }
    for k, r in block_rows.items():
        small = 256 if k == "l" else r
        scratch["CG" + k] = V((small, 128), BF)
        scratch["CR" + k] = V((small, 128), BF)
        scratch["CA" + k] = V((r, 128), BF)
        scratch["CV" + k] = V((2 * r, 128), BF)
    parts = [stages for v in cuts.values() for _, stages in v]
    once = 24 + len(vec_groups(count))
    sem_counts = (once + len(parts), once + sum(2 * len(s) - (len(s[-1]) == 1 or 0 in s[-1]) for s in parts), 8 + len(SMALL))
    for k, v in zip(("ssem", "rsem", "lsem"), sem_counts, strict=True):
        scratch[k] = pltpu.SemaphoreType.DMA((v,))
    names = IN_NAMES + OUT_NAMES + list(scratch)
    results = pl.pallas_call(
        functools.partial(layer_kernel, count, total_rows, cuts, plan, sem_counts, names),
        out_shape=[pltpu.VMEM(outs[k].shape, outs[k].dtype) for k in OUT_NAMES],
        in_specs=[hbm] * len(IN_NAMES),
        out_specs=[vmem] * len(OUT_NAMES),
        scratch_shapes=list(scratch.values()),
        compiler_params=pltpu.CompilerParams(
            collective_id=0, has_side_effects=True, vmem_limit_bytes=VMEM_LIMIT
        ),
        name="layer",
    )(*args)
    finals = {
        "o_output": S((n, d), F32),
        "o_feats": S((features, n), F32),
        "o_bank": S(prompt_bank.shape, F32),
        "o_encw": S(enc_weight.shape, F32),
        "o_encb": S((1, d), F32),
        "o_qkv": S(qkv_weight.shape, F32),
        "o_out": S(out_weight.shape, F32),
        "o_outb": S((1, d), F32),
        "o_ag": S((1, d), F32),
        "o_ash": S((1, d), F32),
        "o_up": S(up_weight.shape, F32),
        "o_upb": S((1, up_bias.shape[0]), F32),
        "o_down": S(down_weight.shape, F32),
        "o_downb": S((1, d), F32),
        "o_fg": S((1, d), F32),
        "o_fsh": S((1, d), F32),
    }
    work = {"FEATS": V((features, n), F32), "SQUARE": V((128, 128), F32)}
    work |= {"s" + k[1:]: V(v.shape, F32) for k, v in finals.items() if k != "o_output"}
    work["sems"] = pltpu.SemaphoreType.DMA((1 + len(finals),))
    final = pl.pallas_call(
        functools.partial(finish_kernel, total_rows, ["feats"] + OUT_NAMES + list(finals) + list(work)),
        out_shape=list(finals.values()),
        in_specs=[hbm] + [vmem] * len(OUT_NAMES),
        out_specs=[hbm] * len(finals),
        scratch_shapes=list(work.values()),
        compiler_params=pltpu.CompilerParams(vmem_limit_bytes=VMEM_LIMIT),
        name="finish",
    )(columns, *[pltpu.with_memory_space_constraint(v, pltpu.VMEM) for v in results])
    vectors = ("o_encb", "o_outb", "o_ag", "o_ash", "o_upb", "o_downb", "o_fg", "o_fsh")
    return tuple(
        v[0] if k in vectors else v.T if k == "o_feats" else v for k, v in zip(finals, final, strict=True)
    )


def solution(mesh):
    whole = P(("rows", "heads"), None)
    placed = (
        whole, P("rows", None), P("rows"), P("rows", None), P(), P(), P(), P(None, None, "heads"), P("heads", None),
        P(), P(), P(), P(None, "heads"), P("heads"), P("heads", None), P(), P(), P(), whole,
    )
    return jax.shard_map(
        per_device,
        mesh=mesh,
        in_specs=placed,
        out_specs=(
            whole, whole, P(), P(), P(), P(None, None, "heads"), P("heads", None), P(), P(), P(), P(None, "heads"),
            P("heads"), P("heads", None), P(), P(), P(),
        ),
        check_vma=False,
    )
```

```python
import functools
import math

import jax
import jax.numpy as jnp
from jax import lax
from jax.experimental import pallas as pl
from jax.experimental.pallas import tpu as pltpu
from jax.sharding import PartitionSpec as P

BF = jnp.bfloat16
F32 = jnp.float32
MESH = pl.DeviceIdType.MESH
DH = 128
P_SIZE = 128
CONTEXT_MAX = 896
CONTEXT_MIN = 640
KEYS = CONTEXT_MAX + P_SIZE
EPS = 1e-05
HALF_ROOT = math.sqrt(0.5)
PDF_SCALE = 1.0 / math.sqrt(2.0 * math.pi)
LOG2E = math.log2(math.e)
Q_SCALE = DH**-0.5 * LOG2E
VMEM_LIMIT = 52 * 2**20


def _dot(a, b, ca, cb):
    return lax.dot_general(a, b, (((ca,), (cb,)), ((), ())), preferred_element_type=F32)


def nn(a, b):
    return _dot(a, b, 1, 0)


def nt(a, b):
    return _dot(a, b, 1, 1)


def tn(a, b):
    return _dot(a, b, 0, 0)


def row_sum(v):
    return jnp.sum(v, axis=0, keepdims=True)


def lane_mean(v):
    return jnp.mean(v, axis=-1, keepdims=True)


class Links:
    def __init__(self, send, recv):
        self.send, self.recv, self.sent, self.received, self.open = send, recv, 0, 0, []

    def send_sem(self):
        self.sent += 1
        return self.send.at[self.sent - 1]

    def recv_sem(self):
        self.received += 1
        return self.recv.at[self.received - 1]

    def start(self, src, dst, device, send, recv):
        c = pltpu.make_async_remote_copy(
            src_ref=src, dst_ref=dst, send_sem=send, recv_sem=recv, device_id=device, device_id_type=MESH
        )
        c.start()
        return c

    def copy(self, src, dst, device):
        c = self.start(src, dst, device, self.send_sem(), self.recv_sem())
        self.open.append(c.wait_send)
        return c

    def drain(self):
        for wait in self.open:
            wait()
        self.open = []


def wait_bytes(ref, sem):
    pltpu.make_async_copy(ref, ref, sem).wait()


class Loads:
    def __init__(self, sems):
        self.sems, self.used = sems, 0

    def copy(self, src, dst):
        c = pltpu.make_async_copy(src, dst, self.sems.at[self.used])
        self.used += 1
        c.start()
        return c


class Part:
    def __init__(self, ctx, block, first, rows, stages):
        self.ctx, self.first, self.rows = ctx, first, rows
        self.stages = [tuple(b for b in s if b) for s in stages]
        self.whole = len(stages[-1]) == 1 or 0 in stages[-1]
        self.acc, self.recv, self.full = block.acc, block.recv, block.full
        self.at = -1

    def begin(self):
        self.base, self.len, self.off, self.k = self.first, self.rows, 2 * self.first, 0
        self.send_sem = self.ctx.links.send_sem()
        self._start_scatter()

    def _digits(self, bits, mask):
        digit, row = 0, self.ctx.row
        for i, b in enumerate(bits):
            bit = (self.ctx.row // b) % 2
            if mask >> i & 1:
                row = row + b * (1 - 2 * bit)
                bit = 1 - bit
            digit = digit * 2 + bit
        return digit, row

    def _wait(self, rows):
        view = self.full.at[pl.ds(0, rows)]
        wait_bytes(view, self.recv_sem)
        wait_bytes(view, self.send_sem)

    def _exchanges(self):
        return self.whole and self.k == len(self.stages) - 1

    def _slot(self, digit):
        return pl.ds(pl.multiple_of(self.off + digit * self.len, 16), self.len)

    def _start_scatter(self):
        bits = self.stages[self.k]
        ways = 2 ** len(bits)
        self.recv_sem = self.ctx.links.recv_sem()
        mine, _ = self._digits(bits, 0)
        q = self.len // ways
        for mask in range(1, ways):
            digit, row = self._digits(bits, mask)
            if self._exchanges():
                src = self.acc.at[pl.ds(pl.multiple_of(self.base, 16), self.len)]
                dst = self.recv.at[self._slot(mine)]
            else:
                src = self.acc.at[pl.ds(pl.multiple_of(self.base + digit * q, 16), q)]
                dst = self.recv.at[pl.ds(self.off + (mask - 1) * q, q)]
            self.ctx.links.start(src, dst, (row, self.ctx.head), self.send_sem, self.recv_sem)

    def _end_scatter(self):
        bits = self.stages[self.k]
        ways = 2 ** len(bits)
        digit, _ = self._digits(bits, 0)
        if self._exchanges():
            mine = pl.ds(pl.multiple_of(self.base, 16), self.len)
            self.recv[self._slot(digit), :] = self.acc[mine, :]
            self._wait((ways - 1) * self.len)
            total = self.recv[self._slot(0), :].astype(F32)
            for i in range(1, ways):
                total = total + self.recv[self._slot(i), :].astype(F32)
            self.full[mine, :] = total.astype(BF)
            self._start_gather()
            return
        q = self.len // ways
        self.base = self.base + digit * q
        mine = pl.ds(pl.multiple_of(self.base, 16), q)
        self._wait((ways - 1) * q)
        total = self.acc[mine, :].astype(F32)
        for i in range(ways - 1):
            total = total + self.recv[pl.ds(self.off + i * q, q), :].astype(F32)
        self.off += (ways - 1) * q
        self.len = q
        self.k += 1
        if self.k < len(self.stages):
            self.acc[mine, :] = total.astype(BF)
            self._start_scatter()
        else:
            self.full[mine, :] = total.astype(BF)
            self._start_gather()

    def _start_gather(self):
        if self.k == 0:
            return
        bits = self.stages[self.k - 1]
        mine = self.full.at[pl.ds(pl.multiple_of(self.base, 16), self.len)]
        self.recv_sem = self.ctx.links.recv_sem()
        for mask in range(1, 2 ** len(bits)):
            _, row = self._digits(bits, mask)
            self.ctx.links.start(mine, mine, (row, self.ctx.head), self.send_sem, self.recv_sem)

    def _end_gather(self):
        bits = self.stages[self.k - 1]
        ways = 2 ** len(bits)
        self._wait((ways - 1) * self.len)
        digit, _ = self._digits(bits, 0)
        self.base = self.base - digit * self.len
        self.len = self.len * ways
        self.k -= 1
        self._start_gather()

    def steps(self):
        return 2 * len(self.stages) - self.whole

    def done(self):
        return self.at == self.steps()

    def advance(self):
        if self.at < 0:
            self.begin()
        elif self.at < len(self.stages):
            self._end_scatter()
        elif not self.done():
            self._end_gather()
        self.at += 1


class Block:
    def __init__(self, ctx, refs, cuts):
        self.ctx = ctx
        self.give, self.got, self.acc, self.recv, self.full = refs
        self.n = self.acc.shape[0]
        self.parts, first = [], 0
        for rows, stages in cuts:
            self.parts.append(Part(ctx, self, first, rows, stages))
            first += rows

    def send_core(self):
        self.core_copy = self.ctx.links.copy(self.give, self.got, self.ctx.twin)

    def merge_core(self):
        self.core_copy.wait_recv()
        for part in self.parts:
            rows = slice(part.first, part.first + part.rows)
            self.acc[rows, :] = (self.acc[rows, :].astype(F32) + self.got[rows, :].astype(F32)).astype(BF)


class Ctx:
    pass


def others_of(ctx, count):
    steps = sorted(range(1, count), key=lambda k: min(k, count - k))
    rows = [lax.rem(ctx.row + k, count) for k in steps]
    return [(row, head) for row in rows for head in (ctx.head, 1 - ctx.head)] + [ctx.twin]


def share_slots(ctx, slots, place, devices):
    mine = slots.at[place]
    send, recv = ctx.links.send_sem(), ctx.links.recv_sem()
    for device in devices:
        ctx.links.start(mine, mine, device, send, recv)
    others = slots.at[pl.ds(0, len(devices))]
    ctx.links.open.append(functools.partial(wait_bytes, others, send))
    return functools.partial(wait_bytes, others, recv)


SMALL = [
    "mask", "splits", "pidx", "encw", "encb", "outb", "ag", "ash", "downb", "fg", "fsh",
]
IN_NAMES = [
    "feats", "mask", "splits", "pidx", "bank", "encw", "encb", "qkvw", "outw", "outb", "ag", "ash", "upw",
    "upb", "downw", "downb", "fg", "fsh", "cot",
]
OUT_NAMES = [
    "output", "uf", "rffn", "rqkv", "rbank", "vec", "late", "stat",
]
CUTS = {
    "d": [(1024, [(2,), (1,), (4, 8)]), (1024, [(1, 2), (4, 8)])],
    "u": [(1024, [(1,), (4,), (2, 8)]), (1024, [(4,), (2,), (1,), (8,)])],
    "o": [(1024, [(1, 2), (8,), (4,)])],
    "q": [(256, [(2,), (1,), (4,), (8,)]), (512, [(1,), (2,), (4,), (8,)]), (768, [(4,), (1, 2), (8,)])],
    "r": [(768, [(1,), (2, 4), (8,)]), (768, [(2,), (1, 4), (8,)])],
    "l": [(768, [(4,), (1, 2), (8,)]), (512, [(1, 2), (4, 8)])],
}
PLAN = [
    [],
    [],
    ["d1", "d0"],
    [],
    [],
    ["u1", "u0", "o0"],
    [],
    ["d1"],
    [],
    ["d0", "u1", "u0"],
    ["d1"],
    ["o0", "q1", "q0", "q2"],
    ["d0", "u1", "u0"],
    ["d1", "q0", "q1"],
    ["o0"],
    ["u1", "q2", "d0"],
    ["u0", "r0", "l0", "r1", "l1", "o0"],
    [],
    ["d1", "q0", "q1", "u1", "q2", "d0", "r0", "u0", "l0", "r1", "q0", "o0", "q1", "u1", "l1", "q2", "d0", "r0", "l0", "u0", "r1", "q0", "q1", "l1"],
    ["r0", "l0", "o0", "u1", "q0", "q1", "r1", "q2", "l1", "u0", "d0", "q0", "r0", "u1", "l0", "r1", "q1", "l1", "q2", "q0", "r0", "l0", "q1", "r1"],
]


def layer_kernel(count, total_rows, cuts, plan, sem_counts, names, *refs):
    g = Ctx()
    for name, ref in zip(names, refs, strict=True):
        setattr(g, name, ref)
    features, n = g.feats.shape
    ctx = Ctx()
    ctx.row, ctx.head = lax.axis_index("rows"), lax.axis_index("heads")
    h = ctx.head
    o = 1 - h
    ctx.twin = (ctx.row, o)
    ctx.links = links = Links(g.ssem, g.rsem)
    loads = Loads(g.lsem)

    l_feats = loads.copy(g.feats, g.F.at[h])
    own = {
        "qkv": (g.qkvw, g.WQKV.at[h]),
        "out": (g.outw, g.WO.at[h]),
        "upb": (g.upb, g.UB.at[h]),
        "up": (g.upw, g.WU.at[h]),
        "down": (g.downw, g.WD.at[h]),
    }
    everyone = others_of(ctx, count)
    barrier = pltpu.get_barrier_semaphore()
    for device in everyone:
        pl.semaphore_signal(barrier, inc=1, device_id=device, device_id_type=MESH)
    l_small = [loads.copy(getattr(g, k), getattr(g, k + "_")) for k in SMALL]
    l_bank = loads.copy(g.bank, g.BANKV)
    l_own = {k: loads.copy(*v) for k, v in own.items()}
    l_cot = loads.copy(g.cot, g.COT)

    def to_rows(columns):
        for i, c in enumerate(columns):
            g.SQUARE[0:features, i : i + 1] = c
        return g.SQUARE[...].T[0:8, :]

    def lane_sum(v):
        return jnp.sum(v, axis=-1, keepdims=True)

    def put_vector(half, i, value):
        for b in range(4):
            g.VEC[half, 4 * i + b : 4 * i + b + 1, :] = value[:, 128 * b : 128 * b + 128]

    g.SQUARE[...] = jnp.zeros_like(g.SQUARE)
    l_feats.wait()
    f = g.F[h]
    rows = to_rows([lane_sum(f), lane_sum(f * f)])
    place = ctx.row * 2 + h
    g.MOM[place, :, 0:128] = rows[0:1]
    g.MOM[place, :, 128:256] = rows[1:2]
    pl.semaphore_wait(barrier, len(everyone))
    wait_moments = share_slots(ctx, g.MOM, place, everyone)
    c_feats = links.copy(g.feats, g.F.at[h], ctx.twin)
    c_own = {"qkv": links.copy(*own["qkv"], ctx.twin)}
    c_own |= {k: links.copy(*v, ctx.twin) for k, v in own.items() if k != "qkv"}

    for c in l_small:
        c.wait()
    selector = lax.broadcasted_iota(jnp.int32, (g.bank.shape[0], P_SIZE), 0) == g.pidx_[...]
    g.SEL[...] = jnp.where(selector, 1.0, 0.0).astype(BF)
    l_bank.wait()
    g.SRC[CONTEXT_MAX:KEYS, :] = tn(g.SEL[...], g.BANKV[...]).astype(BF)
    maybe = lax.broadcasted_iota(jnp.int32, (CONTEXT_MAX - CONTEXT_MIN, 1), 0) + CONTEXT_MIN
    g.BIAS[...] = jnp.where(maybe < g.splits_[0], 0.0, -1e30)
    live = g.mask_[...].astype(F32)
    scale = live * jnp.sqrt(features / jnp.sum(live, axis=-1, keepdims=True))
    g.STAT[...] = jnp.zeros_like(g.STAT)
    g.V[:, :, 128:] = jnp.ones_like(g.V[:, :, 128:])
    g.STAT[2:3, 0:features] = scale
    for c in l_own.values():
        c.wait()
    c_own["qkv"].wait_recv()
    for j in range(4):
        s, w = j // 2, pl.ds(128 * (j % 2), 128)
        g.WKV[j, :, 0:128] = g.WQKV[s, 1, :, w]
        g.WKV[j, :, 128:256] = g.WQKV[s, 2, :, w]

    c_feats.wait_recv()
    wait_moments()
    moments = g.MOM[0]
    for k in range(1, 2 * count):
        moments = moments + g.MOM[k]
    mean = moments[:, 0:128] / total_rows
    var = moments[:, 128:256] / total_rows - mean * mean
    g.STAT[0:1, :] = mean
    g.STAT[1:2, :] = lax.rsqrt(var + EPS)
    g.SQUARE[0:8, :] = g.STAT[...]
    columns = g.SQUARE[...].T
    mean, inverse, scale = [columns[0:features, i : i + 1] for i in range(3)]
    g.COLS[...] = columns[0:features, :]

    for s in range(2):
        g.NL[s] = (((g.F[s] - mean) * inverse) * scale).astype(BF)
        hidden = tn(g.NL[s], g.encw_[...]) + g.encb_[...]
        g.HA[s] = hidden
        g.HB[s] = hidden.astype(BF)
    g.SRC[0:n, :] = g.HB[0]
    g.SRC[n:CONTEXT_MAX, :] = g.HB[1, 0 : CONTEXT_MAX - n, :]

    for s in range(2):
        q = (nn(g.HB[h], g.WQKV[s, 0]) * Q_SCALE).astype(BF)
        for j in range(2):
            g.Q[2 * s + j] = q[:, 128 * j : 128 * j + 128]

    for j in range(4):
        kv = nn(g.SRC[...], g.WKV[j]).astype(BF)
        g.K[j] = kv[:, 0:128]
        g.V[j, :, 0:128] = kv[:, 128:256]

    for j in range(5):
        if j < 4:
            scores = nt(g.K[j], g.Q[j])
            g.S[j % 2, 0:CONTEXT_MIN, :] = scores[0:CONTEXT_MIN]
            g.S[j % 2, CONTEXT_MIN:CONTEXT_MAX, :] = scores[CONTEXT_MIN:CONTEXT_MAX] + g.BIAS[...]
            g.S[j % 2, CONTEXT_MAX:KEYS, :] = scores[CONTEXT_MAX:KEYS]
        if j > 0:
            p = j - 1
            scores = g.S[p % 2]
            e = jnp.exp2(scores - jnp.max(scores, axis=0, keepdims=True))
            e = e.astype(BF)
            g.E[p] = e
            mixed = tn(g.V[p], e)
            inv = 1.0 / mixed[128:129]
            g.INV[p, 0:1, :] = inv
            g.AT[p] = (mixed[0:128] * inv).astype(BF)

    c_own["out"].wait_recv()
    c_own["up"].wait_recv()
    c_own["upb"].wait_recv()
    c_own["down"].wait_recv()
    for j in range(4):
        g.A[:, 128 * j : 128 * j + 128] = g.AT[j].T
    l_cot.wait()

    branch = nn(g.A[:, 0:256], g.WO[0]) + nn(g.A[:, 256:512], g.WO[1]) + g.outb_[...]
    joined = g.HA[h] + branch
    center = joined - lane_mean(joined)
    rstd = lax.rsqrt(lane_mean(center * center) + EPS)
    xhat = center * rstd
    after = xhat * g.ag_[...] + g.ash_[...]
    g.XH[...] = xhat
    g.RS[...] = rstd
    low = after.astype(BF)
    g.AB[...] = low
    mixed = g.downb_[...]
    for s in range(2):
        u = nn(low, g.WU[s]) + g.UB[s]
        phi = 0.5 * (1.0 + lax.erf(u * HALF_ROOT))
        g.DG[s] = phi + u * (jnp.exp2(u * u * (-0.5 * LOG2E)) * PDF_SCALE)
        act = (u * phi).astype(BF)
        g.ACT[s] = act
        mixed = mixed + nn(act, g.WD[s])
    joined = after + mixed
    center = joined - lane_mean(joined)
    rstd = lax.rsqrt(lane_mean(center * center) + EPS)
    xhat = center * rstd
    g.output[...] = xhat * g.fg_[...] + g.fsh_[...]
    ct = g.COT[...]
    d = ct * g.fg_[...]
    d = rstd * (d - lane_mean(d) - xhat * lane_mean(d * xhat))
    g.DJ[...] = d
    gm = d.astype(BF)
    g.GM[...] = gm
    put_vector(1, 0, row_sum(gm.astype(F32)))
    put_vector(1, 1, row_sum(ct * xhat))
    put_vector(1, 2, row_sum(ct))

    def put(ref, first, value):
        r = value.shape[0]
        for b in range(value.shape[1] // 128):
            ref[first + r * b : first + r * b + r, :] = value[:, 128 * b : 128 * b + 128]

    rows_of = {k: sum(r for r, _ in v) for k, v in cuts.items()}
    fulls, at = {"l": g.rbank.at[h]}, 0
    for k in ("d", "u", "o"):
        fulls[k] = g.rffn.at[pl.ds(at, rows_of[k])]
        at += rows_of[k]
    for i, k in enumerate(("q", "r")):
        fulls[k] = g.rqkv.at[i]
    blocks = {
        k: Block(ctx, [getattr(g, p + k) for p in ("CG", "CR", "CA", "CV")] + [fulls[k]], v)
        for k, v in cuts.items()
    }
    down, up, out, qkv0, qkv1, last = blocks.values()

    def tick(i):
        for k in plan[i] if i < len(plan) else []:
            blocks[k[0]].parts[int(k[1])].advance()
            share_last()

    def share_last():
        if not hasattr(ctx, "c_last") and all(p.done() for p in last.parts):
            ctx.c_last = links.copy(g.rbank.at[h], g.rbank.at[h], ctx.twin)

    put(down.give, 0, tn(g.ACT[o], g.GM[...]).astype(BF))
    down.send_core()

    gm = g.GM[...]
    d = g.DJ[...]
    for s in range(2):
        du = (g.DG[s] * nt(gm, g.WD[s])).astype(BF)
        g.DU[s] = du
        put_vector(s, 3, row_sum(du.astype(F32)))
        d = d + nt(du, g.WU[s])
    xhat = g.XH[...]
    put_vector(0, 1, row_sum(d * xhat))
    put_vector(0, 2, row_sum(d))
    d = d * g.ag_[...]
    d = g.RS[...] * (d - lane_mean(d) - xhat * lane_mean(d * xhat))
    g.DJ[...] = d
    gb = d.astype(BF)
    g.GB[...] = gb
    put_vector(0, 0, row_sum(gb.astype(F32)))
    put(down.acc, 0, tn(g.ACT[h], g.GM[...]).astype(BF))
    down.merge_core()
    tick(2)
    put(up.give, 0, tn(g.AB[...], g.DU[o]).astype(BF))
    up.send_core()
    for j in range(2):
        put(out.give, 128 * j * 4, nn(g.AT[2 * o + j], g.GB[...]).astype(BF))
    out.send_core()
    c_vec = links.copy(g.VEC.at[o], g.VECR, ctx.twin)
    put(up.acc, 0, tn(g.AB[...], g.DU[h]).astype(BF))
    for j in range(2):
        put(out.acc, 128 * j * 4, nn(g.AT[2 * h + j], g.GB[...]).astype(BF))
    tick(3)

    g.HQT[...] = g.HB[h].T
    g.SRCT[...] = g.SRC[pl.ds(pl.multiple_of(h * n, n), n), :].T
    for j in range(4):
        d = nt(g.WO[j // 2, 128 * (j % 2) : 128 * (j % 2) + 128, :], g.GB[...]).astype(BF)
        d = (d.astype(F32) * g.INV[j, 0:1, :]).astype(BF)
        g.DOT2[j] = d
        g.INNER[j, 0:1, :] = row_sum(d.astype(F32) * g.AT[j].astype(F32))
    tick(4)
    up.merge_core()
    out.merge_core()
    tick(5)

    vec_stages = vec_groups(count)
    vec = Ctx()
    vec.k = 0

    def vec_start(value):
        bits = vec_stages[vec.k]
        digit, _ = down.parts[0]._digits(bits, 0)
        slots = g.VECS.at[vec.k]
        slots[digit] = value
        send, vec.sem = links.send_sem(), links.recv_sem()
        others = slots.at[pl.ds(0, 2 ** len(bits) - 1)]
        for mask in range(1, 2 ** len(bits)):
            _, row = down.parts[0]._digits(bits, mask)
            links.start(slots.at[digit], slots.at[digit], (row, h), send, vec.sem)
        links.open.append(functools.partial(wait_bytes, others, send))

    def vec_end():
        ways = 2 ** len(vec_stages[vec.k])
        wait_bytes(g.VECS.at[vec.k, pl.ds(0, ways - 1)], vec.sem)
        value = g.VECS[vec.k, 0]
        for i in range(1, ways):
            value = value + g.VECS[vec.k, i]
        vec.k += 1
        if vec.k < len(vec_stages):
            vec_start(value)
        else:
            g.vec[h] = value
            vec.copy = links.copy(g.vec.at[h], g.vec.at[h], ctx.twin)

    kv_copies = {}

    def attend_back(j):
        q, dot2, inner = g.Q[j], g.DOT2[j], g.INNER[j, 0:1, :]
        dq = None
        for t in range(KEYS // 512):
            rows = slice(512 * t, 512 * t + 512)
            e = g.E[j, rows, :]
            upstream = nn(g.V[j, rows, 0:128], dot2)
            ds = (e.astype(F32) * (upstream - inner)).astype(BF)
            g.DKV[j, rows, 0:128] = (nn(ds, q) * (DH**-0.5 / Q_SCALE)).astype(BF)
            g.DKV[j, rows, 128:256] = nt(e, dot2).astype(BF)
            part = tn(g.K[j, rows, :], ds)
            dq = part if dq is None else dq + part
        g.DQT[j] = (dq * DH**-0.5).astype(BF)
        other = pl.ds(pl.multiple_of(o * n, n), n)
        kv_copies[j] = links.copy(g.DKV.at[j, other], g.DKVR.at[j], ctx.twin)

    def merge_kv(j):
        kv_copies[j].wait_recv()
        mine = pl.ds(pl.multiple_of(h * n, n), n)
        g.DKVO[j] = (g.DKV[j, mine, :].astype(F32) + g.DKVR[j].astype(F32)).astype(BF)

    def q_grads(p, block):
        for j, ref in ((2 * o + p, block.give), (2 * h + p, block.acc)):
            put(ref, 0, nt(g.HQT[...], g.DQT[j]).astype(BF))

    def kv_grads(p, block):
        put(block.give, n, nn(g.SRCT[...], g.DKVO[2 * o + p]).astype(BF))
        block.send_core()
        put(block.acc, n, nn(g.SRCT[...], g.DKVO[2 * h + p]).astype(BF))

    attend_back(0)
    tick(6)
    attend_back(2)
    tick(7)
    q_grads(0, qkv0)
    attend_back(1)
    tick(8)
    merge_kv(0)
    merge_kv(2)
    kv_grads(0, qkv0)
    tick(9)
    attend_back(3)
    tick(10)
    qkv0.merge_core()
    c_vec.wait_recv()
    vec_start(g.VEC[h] + g.VECR[...])
    tick(11)
    q_grads(1, qkv1)
    for j in range(4):
        g.DQ[:, 128 * j : 128 * j + 128] = g.DQT[j].T
    dh = g.DJ[...] + nt(g.DQ[:, 0:256], g.WQKV[0, 0]) + nt(g.DQ[:, 256:512], g.WQKV[1, 0])
    tick(12)

    merge_kv(1)
    merge_kv(3)
    kvh = nt(g.DKVO[0], g.WKV[0])
    for j in range(1, 4):
        kvh = kvh + nt(g.DKVO[j], g.WKV[j])
    edge = CONTEXT_MAX - n
    g.DP[0] = kvh[edge:n, :].astype(BF)
    c_prompt = links.copy(g.DP.at[0], g.DP.at[1], ctx.twin)
    g.GH[0:edge, :] = (dh[0:edge] + kvh[0:edge]).astype(BF)
    first = jnp.where(h == 0, 1.0, 0.0)
    g.GH[edge:n, :] = (dh[edge:n] + kvh[edge:n] * first).astype(BF)
    tick(13)
    kv_grads(1, qkv1)
    tick(14)
    gh = g.GH[...]
    g.ENC[0:features, :] = nn(g.NL[h], gh)
    g.ENC[features:, :] = jnp.zeros_like(g.ENC[features:, :])
    bank_rows = g.bank.shape[0] // 2
    enc_at = bank_rows * 4
    for b in range(4):
        cols = slice(128 * b, 128 * b + 128)
        last.give[64 * b : 64 * b + 64, :] = g.ENC[pl.ds(pl.multiple_of(o * 64, 64), 64), cols].astype(BF)
        last.acc[enc_at + 64 * b : enc_at + 64 * b + 64, :] = g.ENC[
            pl.ds(pl.multiple_of(h * 64, 64), 64), cols
        ].astype(BF)
    last.send_core()
    c_prompt.wait_recv()
    put(
        last.acc,
        0,
        nn(g.SEL[pl.ds(pl.multiple_of(h * bank_rows, bank_rows), bank_rows), :], g.DP[o]).astype(BF),
    )
    tick(15)
    qkv1.merge_core()
    last.core_copy.wait_recv()
    rows = slice(enc_at, enc_at + 256)
    last.acc[rows, :] = (last.acc[rows, :].astype(F32) + last.got[...].astype(F32)).astype(BF)
    if last.n > enc_at + 256:
        last.acc[enc_at + 256 :, :] = jnp.zeros_like(last.acc[enc_at + 256 :, :])
    tick(16)
    vec_end()

    scale = g.COLS[:, 2:3]
    uf = nt(g.encw_[...], gh) * scale
    g.uf[...] = uf
    g.SQUARE[...] = jnp.zeros_like(g.SQUARE)
    rows = to_rows([lane_sum(uf), lane_sum(uf * (g.F[h] - g.COLS[:, 0:1]))])
    eb = row_sum(gh.astype(F32))
    g.LATE[0, :, 0:128] = rows[0:1]
    g.LATE[0, :, 128:256] = rows[1:2]
    g.LATE[0, :, 256:384] = eb[:, 0:128]
    g.LATE[1] = eb[:, 128:512]
    c_late = links.copy(g.LATE.at[o], g.LATER, ctx.twin)
    tick(17)
    c_late.wait_recv()
    g.LSUM[ctx.row] = g.LATE[h] + g.LATER[...]
    wait_late = share_slots(ctx, g.LSUM, ctx.row, everyone[0:-1:2])
    tick(18)
    while vec.k < len(vec_stages):
        vec_end()
    wait_late()
    late = g.LSUM[0]
    for k in range(1, count):
        late = late + g.LSUM[k]
    g.late[h] = late
    c_late_half = links.copy(g.late.at[h], g.late.at[h], ctx.twin)
    links.drain()
    tick(19)
    rest = [p for b in blocks.values() for p in b.parts]
    while not all(p.done() for p in rest):
        for p in rest:
            if not p.done():
                p.advance()
                share_last()
    g.stat[...] = g.STAT[...]
    vec.copy.wait_recv()
    c_late_half.wait_recv()
    ctx.c_last.wait_recv()
    links.drain()
    assert (links.sent, links.received, loads.used) == sem_counts, (links.sent, links.received, loads.used)


def vec_groups(count):
    bits = [2**i for i in range(count.bit_length() - 1)]
    return [tuple(bits[i : i + 2]) for i in range(0, len(bits), 2)]


def finish_kernel(total_rows, names, *refs):
    g = Ctx()
    for name, ref in zip(names, refs, strict=True):
        setattr(g, name, ref)
    h = lax.axis_index("heads")
    features = g.feats.shape[0]
    copies = []

    def copy(src, dst):
        c = pltpu.make_async_copy(src, dst, g.sems.at[len(copies)])
        c.start()
        copies.append(c)
        return c

    def done(*results):
        for k in results:
            copy(getattr(g, "s_" + k), getattr(g, "o_" + k))

    copy(g.output, g.o_output)
    c_feats = copy(g.feats, g.FEATS)
    up_at = g.rffn.shape[0] // 5 * 2

    def block(ref, first, rows):
        return ref[first : first + rows, :].astype(F32)

    columns = [slice(128 * b, 128 * b + 128) for b in range(4)]
    for b, cols in enumerate(columns):
        g.s_down[:, cols] = block(g.rffn, 512 * b, 512)
    done("down")
    for b, cols in enumerate(columns):
        g.s_up[:, cols] = block(g.rffn, up_at + 512 * b, 512)
    done("up")
    for c in range(3):
        for p in range(2):
            g.s_qkv[c, :, 128 * p : 128 * p + 128] = g.rqkv[p, 512 * c : 512 * c + 512, :].astype(F32)
    done("qkv")
    for b, cols in enumerate(columns):
        for s in range(2):
            g.s_bank[256 * s : 256 * s + 256, cols] = g.rbank[s, 256 * b : 256 * b + 256, :].astype(F32)
    done("bank")
    for b, cols in enumerate(columns):
        for j in range(2):
            g.s_out[128 * j : 128 * j + 128, cols] = block(g.rffn, 2 * up_at + 512 * j + 128 * b, 128)
    done("out")
    late = jnp.concatenate([g.late[0], g.late[1]], axis=-1)
    vectors = [(0, 0, "outb"), (0, 1, "ag"), (0, 2, "ash"), (1, 0, "downb"), (1, 1, "fg"), (1, 2, "fsh"), (h, 3, "upb")]
    for b, cols in enumerate(columns):
        g.s_encw[0:64, cols] = g.rbank[0, 1024 + 64 * b : 1024 + 64 * b + 64, :].astype(F32)
        g.s_encw[64:features, cols] = g.rbank[1, 1024 + 64 * b : 1024 + 64 * b + features - 64, :].astype(F32)
        g.s_encb[:, cols] = late[:, 256 + 128 * b : 384 + 128 * b]
        for s, i, k in vectors:
            getattr(g, "s_" + k)[:, cols] = g.vec[s, 4 * i + b : 4 * i + b + 1, :]
    done("encw", "encb", *[k for _, _, k in vectors])
    mean, inverse = g.stat[0:1, :], g.stat[1:2, :]
    b1, b2 = late[:, 0:128], late[:, 128:256]
    var_grad = -0.5 * inverse * inverse * inverse * b2
    g.SQUARE[...] = jnp.zeros_like(g.SQUARE)
    g.SQUARE[0:1, :] = inverse
    g.SQUARE[1:2, :] = (-inverse * b1 - 2.0 * mean * var_grad) / total_rows
    g.SQUARE[2:3, :] = 2.0 * var_grad / total_rows
    turned = g.SQUARE[...].T
    inverse, first, slope = [turned[0:features, i : i + 1] for i in range(3)]
    c_feats.wait()
    g.s_feats[...] = g.uf[...] * inverse + first + g.FEATS[...] * slope
    done("feats")
    for c in copies:
        if c is not c_feats:
            c.wait()


def per_device(
    feats,
    feature_mask,
    splits,
    prompt_index,
    prompt_bank,
    enc_weight,
    enc_bias,
    qkv_weight,
    out_weight,
    out_bias,
    attn_gain,
    attn_shift,
    up_weight,
    up_bias,
    down_weight,
    down_bias,
    ffn_gain,
    ffn_shift,
    cotangent,
):
    n, features = feats.shape
    count = lax.axis_size("rows")
    total_rows = n * count * lax.axis_size("heads")
    d = prompt_bank.shape[1]
    columns = feats.T
    args = [
        columns, feature_mask, splits, prompt_index, prompt_bank, enc_weight, enc_bias[None], qkv_weight, out_weight,
        out_bias[None], attn_gain[None], attn_shift[None], up_weight, up_bias[None], down_weight, down_bias[None],
        ffn_gain[None], ffn_shift[None], cotangent,
    ]
    vmem = pl.BlockSpec(memory_space=pltpu.VMEM)
    hbm = pl.BlockSpec(memory_space=pl.ANY)
    bits = [2**i for i in range(count.bit_length() - 1)]
    grain = 16 * count
    block_rows = {"d": 2048, "u": 2048, "o": 1024, "q": 1536, "r": 1536, "l": 1280}
    if count == 16:
        cuts, plan = CUTS, PLAN
    else:
        cuts, plan = {k: [(-(-r // grain) * grain, vec_groups(count))] for k, r in block_rows.items()}, []
    block_rows = {k: sum(r for r, _ in v) for k, v in cuts.items()}
    S = jax.ShapeDtypeStruct
    outs = {
        "output": S((n, d), F32),
        "uf": S((features, n), F32),
        "rffn": S((block_rows["d"] + block_rows["u"] + block_rows["o"], 128), BF),
        "rqkv": S((2, block_rows["q"], 128), BF),
        "rbank": S((2, block_rows["l"], 128), BF),
        "vec": S((2, 16, 128), F32),
        "late": S((2, 1, 384), F32),
        "stat": S((8, 128), F32),
    }
    V = pltpu.VMEM
    scratch = {k + "_": V(args[IN_NAMES.index(k)].shape, args[IN_NAMES.index(k)].dtype) for k in SMALL}
    scratch["splits_"] = pltpu.SMEM(splits.shape, splits.dtype)
    scratch |= {
        "F": V((2, features, n), F32),
        "WQKV": V((2, 3, d, 256), BF),
        "WO": V((2, 256, d), BF),
        "UB": V((2, 1, 512), F32),
        "WU": V((2, d, 512), BF),
        "WD": V((2, 512, d), BF),
        "BANKV": V(prompt_bank.shape, BF),
        "COT": V((n, d), F32),
        "SQUARE": V((128, 128), F32),
        "COLS": V((features, 128), F32),
        "LATE": V((2, 1, 384), F32),
        "LATER": V((1, 384), F32),
        "MOM": V((2 * count, 1, 256), F32),
        "LSUM": V((count, 1, 384), F32),
        "STAT": V((8, 128), F32),
        "VEC": V((2, 16, 128), F32),
        "VECR": V((16, 128), F32),
        "VECS": V((len(vec_groups(count)), 4, 16, 128), F32),
        "SEL": V((prompt_bank.shape[0], P_SIZE), BF),
        "SRC": V((KEYS, d), BF),
        "BIAS": V((CONTEXT_MAX - CONTEXT_MIN, 1), F32),
        "S": V((2, KEYS, n), F32),
        "WKV": V((4, d, 256), BF),
        "NL": V((2, features, n), BF),
        "HA": V((2, n, d), F32),
        "HB": V((2, n, d), BF),
        "Q": V((4, n, 128), BF),
        "K": V((4, KEYS, 128), BF),
        "V": V((4, KEYS, 144), BF),
        "E": V((4, KEYS, n), BF),
        "INV": V((4, 8, n), F32),
        "INNER": V((4, 8, n), F32),
        "AT": V((4, 128, n), BF),
        "A": V((n, d), BF),
        "XH": V((n, d), F32),
        "RS": V((n, 1), F32),
        "AB": V((n, d), BF),
        "DG": V((2, n, 512), F32),
        "ACT": V((2, n, 512), BF),
        "DU": V((2, n, 512), BF),
        "DJ": V((n, d), F32),
        "GM": V((n, d), BF),
        "GB": V((n, d), BF),
        "DOT2": V((4, 128, n), BF),
        "DKV": V((4, KEYS, 256), BF),
        "DKVR": V((4, n, 256), BF),
        "DKVO": V((4, n, 256), BF),
        "DQT": V((4, 128, n), BF),
        "DQ": V((n, d), BF),
        "HQT": V((d, n), BF),
        "SRCT": V((d, n), BF),
        "DP": V((2, P_SIZE, d), BF),
        "GH": V((n, d), BF),
        "ENC": V((128, d), F32),
    }
    for k, r in block_rows.items():
        small = 256 if k == "l" else r
        scratch["CG" + k] = V((small, 128), BF)
        scratch["CR" + k] = V((small, 128), BF)
        scratch["CA" + k] = V((r, 128), BF)
        scratch["CV" + k] = V((2 * r, 128), BF)
    parts = [stages for v in cuts.values() for _, stages in v]
    once = 24 + len(vec_groups(count))
    sem_counts = (once + len(parts), once + sum(2 * len(s) - (len(s[-1]) == 1 or 0 in s[-1]) for s in parts), 8 + len(SMALL))
    for k, v in zip(("ssem", "rsem", "lsem"), sem_counts, strict=True):
        scratch[k] = pltpu.SemaphoreType.DMA((v,))
    names = IN_NAMES + OUT_NAMES + list(scratch)
    results = pl.pallas_call(
        functools.partial(layer_kernel, count, total_rows, cuts, plan, sem_counts, names),
        out_shape=[pltpu.VMEM(outs[k].shape, outs[k].dtype) for k in OUT_NAMES],
        in_specs=[hbm] * len(IN_NAMES),
        out_specs=[vmem] * len(OUT_NAMES),
        scratch_shapes=list(scratch.values()),
        compiler_params=pltpu.CompilerParams(
            collective_id=0, has_side_effects=True, vmem_limit_bytes=VMEM_LIMIT
        ),
        name="layer",
    )(*args)
    finals = {
        "o_output": S((n, d), F32),
        "o_feats": S((features, n), F32),
        "o_bank": S(prompt_bank.shape, F32),
        "o_encw": S(enc_weight.shape, F32),
        "o_encb": S((1, d), F32),
        "o_qkv": S(qkv_weight.shape, F32),
        "o_out": S(out_weight.shape, F32),
        "o_outb": S((1, d), F32),
        "o_ag": S((1, d), F32),
        "o_ash": S((1, d), F32),
        "o_up": S(up_weight.shape, F32),
        "o_upb": S((1, up_bias.shape[0]), F32),
        "o_down": S(down_weight.shape, F32),
        "o_downb": S((1, d), F32),
        "o_fg": S((1, d), F32),
        "o_fsh": S((1, d), F32),
    }
    work = {"FEATS": V((features, n), F32), "SQUARE": V((128, 128), F32)}
    work |= {"s" + k[1:]: V(v.shape, F32) for k, v in finals.items() if k != "o_output"}
    work["sems"] = pltpu.SemaphoreType.DMA((1 + len(finals),))
    final = pl.pallas_call(
        functools.partial(finish_kernel, total_rows, ["feats"] + OUT_NAMES + list(finals) + list(work)),
        out_shape=list(finals.values()),
        in_specs=[hbm] + [vmem] * len(OUT_NAMES),
        out_specs=[hbm] * len(finals),
        scratch_shapes=list(work.values()),
        compiler_params=pltpu.CompilerParams(vmem_limit_bytes=VMEM_LIMIT),
        name="finish",
    )(columns, *[pltpu.with_memory_space_constraint(v, pltpu.VMEM) for v in results])
    vectors = ("o_encb", "o_outb", "o_ag", "o_ash", "o_upb", "o_downb", "o_fg", "o_fsh")
    return tuple(
        v[0] if k in vectors else v.T if k == "o_feats" else v for k, v in zip(finals, final, strict=True)
    )


def solution(mesh):
    whole = P(("rows", "heads"), None)
    placed = (
        whole, P("rows", None), P("rows"), P("rows", None), P(), P(), P(), P(None, None, "heads"), P("heads", None),
        P(), P(), P(), P(None, "heads"), P("heads"), P("heads", None), P(), P(), P(), whole,
    )
    return jax.shard_map(
        per_device,
        mesh=mesh,
        in_specs=placed,
        out_specs=(
            whole, whole, P(), P(), P(), P(None, None, "heads"), P("heads", None), P(), P(), P(), P(None, "heads"),
            P("heads"), P("heads", None), P(), P(), P(),
        ),
        check_vma=False,
    )
```
